32 devices in a mesh: section: 2 (over core), dp: 4 (over z), tensor: 4 (over y, x).
Axes of the slice: x: 2, y: 2, z: 4, core: 2. Of those that a mesh axis runs over, the one named last changes fastest.
Arguments:
- inputs: bfloat16 [8, 1088, 768], P('dp', 'tensor'), may hold values from -6 to 6
- cotangent: bfloat16 [8, 1088, 768], P('dp', 'tensor'), may hold values from -6 to 6
- w_qkv: bfloat16 [2, 3, 768, 768], P('section', None, None, 'tensor'), may hold values from -0.21875 to 0.21875
- w_out: bfloat16 [2, 768, 768], P('section', 'tensor'), may hold values from -1.75 to 1.75
- w_up: bfloat16 [2, 768, 3072], P('section', None, 'tensor'), may hold values from -0.21875 to 0.21875
- w_down: bfloat16 [2, 3072, 768], P('section', 'tensor'), may hold values from -0.109375 to 0.109375
- gains: float32 [2, 2, 768], P('section'), may hold values from 0.5 to 1.5
- image_sizes: int32 [8, 2], P('dp'), may hold values from 12 to 24, as said below
- lengths: int32 [8], P('dp'), may hold values from 5 to 512, as said below
- shifts: int32 [2], replicated, may hold values from 1 to 11
Outputs:
- ends: bfloat16 [2, 8, 1088, 768], P('section', 'dp', 'tensor')
- grad_qkv: float32 [2, 3, 768, 768], P('section', None, 'dp', 'tensor')
- grad_out: float32 [2, 768, 768], P('section', 'tensor', 'dp')
- grad_up: float32 [2, 768, 3072], P('section', 'dp', 'tensor')
- grad_down: float32 [2, 3072, 768], P('section', ('tensor', 'dp'))
- grad_gains: float32 [2, 2, 768], P('section', None, ('dp', 'tensor'))
The draws below stay inside these ranges and needn't reach their ends.
Inputs may be any that keep to these rules, and one draw needn't show every extreme that they name: `image_sizes`: one image of each draw covers the whole grid. `lengths`: one image of each draw fills all 512 answer slots.
All inputs are finite; a program needn't handle non-finite values.
Results may differ from the reference program's by a relative error of at most 0.025.
Values may be sent and summed in bfloat16 or wider, within the bound.
A program may use at most 192 MiB of HBM per device.

```python
import jax
import jax.numpy as jnp
from jax import lax

D = 768
H = 12
FF = 3072
HD = 64
WIN = 12
GRID = 24
QL = 512
S = 1088
IMAGES = 8


def draw_image_sizes(key, part):
    key = jax.random.fold_in(key, 11)
    pick_key, size_key = jax.random.split(key)
    drawn = jax.random.randint(size_key, (IMAGES, 2), WIN, GRID + 1, dtype=jnp.int32)
    chosen = jax.random.randint(pick_key, (), 0, IMAGES, dtype=jnp.int32)
    rows_all = jnp.arange(IMAGES, dtype=jnp.int32)[:, None]
    return jnp.where(rows_all == chosen, GRID, drawn).astype(jnp.int32)


def draw_lengths(key, part):
    key = jax.random.fold_in(key, 23)
    pick_key, length_key = jax.random.split(key)
    drawn = jax.random.randint(length_key, (IMAGES,), 5, QL + 1, dtype=jnp.int32)
    chosen = jax.random.randint(pick_key, (), 0, IMAGES, dtype=jnp.int32)
    return jnp.where(jnp.arange(IMAGES, dtype=jnp.int32) == chosen, QL, drawn).astype(jnp.int32)


def steps_of(rng, dims, cuts, least, largest):
    factor_of, own = 1.0, jax.random.fold_in(rng, 6)
    for dim, shards_of in cuts:
        draws = jnp.exp(jax.random.uniform(jax.random.fold_in(own, dim), (shards_of,), jnp.float32, least / len(cuts), largest / len(cuts)))
        factor_of = factor_of * jnp.repeat(draws, dims[dim] // shards_of).reshape([-1 if axis == dim else 1 for axis in range(len(dims))])
    return factor_of


def normal_values(key, dims, spread, reach, cuts=(), kind=jnp.bfloat16):
    array = spread * jax.random.normal(key, dims, jnp.float32)
    if cuts:
        array = array * steps_of(key, dims, cuts, -0.22, 0.18)
    return jnp.clip(array, -reach, reach).astype(kind)


def setup_inputs(seed: int = 0) -> dict:
    streams_of = jax.random.split(jax.random.key(seed), 11)
    return {
        "inputs": normal_values(streams_of[0], (IMAGES, S, D), 1.0, 6.0, ((0, 4), (1, 4))),
        "cotangent": normal_values(streams_of[1], (IMAGES, S, D), 1.0, 6.0, ((0, 4), (1, 4))),
        "w_qkv": normal_values(streams_of[2], (2, 3, D, D), D ** -0.5, 0.21875, ((0, 2), (3, 4))),
        "w_out": normal_values(streams_of[3], (2, D, D), (D // 64) ** -0.5, 1.75, ((0, 2), (1, 4))),
        "w_up": normal_values(streams_of[4], (2, D, FF), D ** -0.5, 0.21875, ((0, 2), (2, 4))),
        "w_down": normal_values(streams_of[5], (2, FF, D), FF ** -0.5, 0.109375, ((0, 2), (1, 4))),
        "gains": jnp.clip(1.0 + 0.1 * jax.random.normal(streams_of[6], (2, 2, D), jnp.float32), 0.5, 1.5),
        "image_sizes": draw_image_sizes(jax.random.fold_in(streams_of[10], 71), 0),
        "lengths": draw_lengths(jax.random.fold_in(streams_of[10], 71), 0),
        "shifts": jax.random.randint(streams_of[9], (2,), 1, WIN).astype(jnp.int32),
    }


@jax.custom_vjp
def low(v):
    return lax.optimization_barrier(v.astype(jnp.bfloat16)).astype(jnp.float32)

@jax.custom_vjp
def low_back(v):
    return v

def low_keep(v):
    return (low(v), None)

def low_pass(kept, grad):
    return (grad,)

def back_keep(v):
    return (v, None)

def back_low(kept, grad):
    return (low(grad),)
low.defvjp(low_keep, low_pass)
low_back.defvjp(back_keep, back_low)
epsilon = 1e-05
masked_score = -1000000000.0
highest = lax.Precision.HIGHEST

def allowed_pairs(image_size, answer_length, offsets):
    patches = GRID * GRID
    tokens = jnp.arange(patches + QL, dtype=jnp.int32)
    is_patch = tokens < patches
    grid_row = tokens // GRID
    grid_col = tokens % GRID
    live_patch = is_patch & (grid_row < image_size[0]) & (grid_col < image_size[1])
    live_answer = jnp.logical_not(is_patch) & (tokens - patches < answer_length)
    window_row = (grid_row + offsets[0]) // WIN
    window_col = (grid_col + offsets[1]) // WIN
    same_window = (window_row[:, None] == window_row[None, :]) & (window_col[:, None] == window_col[None, :])
    from_patch = is_patch[:, None] & live_patch[None, :] & same_window
    earlier = live_answer[None, :] & (tokens[None, :] < tokens[:, None])
    from_answer = jnp.logical_not(is_patch)[:, None] & (live_patch[None, :] | earlier)
    return from_patch | from_answer | (tokens[:, None] == tokens[None, :])

def normalize(values, gain):
    centered = values - lax.optimization_barrier(jnp.mean(values, axis=-1, keepdims=True))
    return centered * lax.rsqrt(lax.optimization_barrier(jnp.mean(centered * centered, axis=-1, keepdims=True)) + epsilon) * gain

def layer_forward(values, qkv_weight, out_weight, up_weight, down_weight, gain_pair, allowed):
    token_count = values.shape[0]
    normed = low(normalize(values, gain_pair[0]))
    projected = low_back(low(jnp.einsum('sd,jde->jse', normed, qkv_weight, precision=highest)))
    head_parts = projected.reshape(3, token_count, H, HD)
    scores = low_back(jnp.einsum('qhe,khe->hqk', head_parts[0], head_parts[1], precision=highest) * HD ** (-0.5))
    scores = jnp.where(allowed[None], scores, masked_score)
    probs = jax.nn.softmax(scores, axis=-1)
    mixed = low_back(low(jnp.einsum('hqk,khe->qhe', low(probs), head_parts[2], precision=highest)))
    mixed = mixed.reshape(token_count, D)
    after_attn = values + low_back(jnp.dot(mixed, out_weight, precision=highest))
    second = low(normalize(after_attn, gain_pair[1]))
    hidden = low_back(jnp.dot(second, up_weight, precision=highest))
    acted = low(jax.nn.gelu(hidden, approximate=False))
    return after_attn + low_back(jnp.dot(acted, down_weight, precision=highest))

def two_layers(values, qkv_weight, out_weight, up_weight, down_weight, gain_all, image_size, answer_length, shifts):
    first = layer_forward(values, qkv_weight[0], out_weight[0], up_weight[0], down_weight[0], gain_all[0], allowed_pairs(image_size, answer_length, shifts * 0))
    passed = low_back(low(first))
    return layer_forward(passed, qkv_weight[1], out_weight[1], up_weight[1], down_weight[1], gain_all[1], allowed_pairs(image_size, answer_length, shifts))

def reference(inputs, cotangent, w_qkv, w_out, w_up, w_down, gains, image_sizes, lengths, shifts):
    checked = jax.checkpoint(two_layers)

    def forward(values, qkv_weight, out_weight, up_weight, down_weight, gain_all):

        def one_image(item):
            return checked(item[0], qkv_weight, out_weight, up_weight, down_weight, gain_all, item[1], item[2], shifts)
        return lax.map(one_image, (values, image_sizes, lengths))
    output, pullback = jax.vjp(forward, inputs.astype(jnp.float32), w_qkv.astype(jnp.float32), w_out.astype(jnp.float32), w_up.astype(jnp.float32), w_down.astype(jnp.float32), gains.astype(jnp.float32))
    grads = pullback(cotangent.astype(jnp.float32))
    ends = jnp.stack([grads[0].astype(jnp.bfloat16), output.astype(jnp.bfloat16)])
    return (ends, grads[1], grads[2], grads[3], grads[4], grads[5])
```

```python
import functools

import jax
import jax.numpy as jnp
from jax import lax
from jax.experimental import pallas as pl
from jax.experimental.pallas import tpu as pltpu
from jax.sharding import PartitionSpec as P

MESH = pl.DeviceIdType.MESH
VMEM = pltpu.VMEM
ANY = pl.ANY
BF = jnp.bfloat16
F32 = jnp.float32

HD = 64
WIN = 12
GRID = 24
QL = 512
EPS = 1e-05
OFF = -1e30
LIMIT = 60 * 2**20

NT = (((1,), (1,)), ((), ()))
TN = (((0,), (0,)), ((), ()))


def mm(a, b):
    return jnp.dot(a, b, preferred_element_type=F32)


def mm_nt(a, b):
    return lax.dot_general(a, b, NT, preferred_element_type=F32)


def mm_tn(a, b):
    return lax.dot_general(a, b, TN, preferred_element_type=F32)


def normalize(values):
    centered = values - jnp.mean(values, axis=-1, keepdims=True)
    inverse = lax.rsqrt(jnp.mean(centered * centered, axis=-1, keepdims=True) + EPS)
    return centered * inverse, inverse


def normalize_back(grad, normed, inverse, gain):
    t = grad * gain
    return inverse * (
        t
        - jnp.mean(t, axis=-1, keepdims=True)
        - normed * jnp.mean(t * normed, axis=-1, keepdims=True)
    )


def place():
    return lax.axis_index("section"), lax.axis_index("dp"), lax.axis_index("tensor")


def partner_of(t):
    return t + 1 - 2 * lax.rem(t, 2)


def across_of(t):
    return lax.rem(t + 2, 4)


def greet(*devices):
    barrier = pltpu.get_barrier_semaphore()
    for device in devices:
        pl.semaphore_signal(barrier, inc=1, device_id=device, device_id_type=MESH)
    pl.semaphore_wait(barrier, len(devices))


def send(src, dst, sems, index, device):
    return pltpu.make_async_remote_copy(
        src_ref=src,
        dst_ref=dst,
        send_sem=sems[0].at[index],
        recv_sem=sems[1].at[index],
        device_id=device,
        device_id_type=MESH,
    )


def pick_start(layer, refs, dsts, sem):
    core = lax.axis_index("section")

    @pl.when(core == layer)
    def _():
        for n, (mine, other) in enumerate(refs):
            pltpu.make_async_copy(mine, dsts[n], sem.at[n]).start()

    @pl.when(core != layer)
    def _():
        for n, (mine, other) in enumerate(refs):
            pltpu.make_async_copy(other, dsts[n], sem.at[n]).start()


def pick_wait(refs, dsts, sem, n):
    pltpu.make_async_copy(refs[n][0], dsts[n], sem.at[n]).wait()


def head_lanes(rows, h):
    lanes = lax.broadcasted_iota(jnp.int32, (rows, 3 * HD), 1)
    return (lanes >= h * HD) & (lanes < h * HD + HD)


def fill_bias(bias_ref, colinfo, rowinfo, rows):
    info = rowinfo[rows, :]
    cw, ca, cj = colinfo[0:1, :], colinfo[1:2, :], colinfo[2:3, :]
    rw, ra, ri = info[:, 0:1], info[:, 1:2], info[:, 2:3]
    allowed = (cw == rw) | (ca < ra) | (cj == ri)
    bias_ref[...] = jnp.where(allowed, 0.0, OFF)


def chunk_rows(i, chunk):
    return pl.ds(pl.multiple_of(i * chunk, 16), chunk)


def attn_fwd_kernel(
    layer, x_ref, gain_ref, colinfo, rowinfo, wout_ref, wa, wb, wc, wd,
    x1_ref, q_ref, k_ref, v_ref, mixed_ref, lse_ref,
    w_scr, a_scr, bias_scr, other_scr, wsem, kv_s, kv_r, mix_s, mix_r,
):
    s, d, t = place()
    partner = (s, d, partner_of(t))
    sibling = (1 - s, d, t)
    refs = [(wa, wc), (wb, wd)]
    dsts = [w_scr.at[0], w_scr.at[1]]
    pick_start(layer, refs, dsts, wsem)
    greet(partner, sibling)
    count = x_ref.shape[0]
    chunk = count // 2
    own = pl.ds(pl.multiple_of(s * count, 16), count)

    @pl.loop(0, 2)
    def _(i):
        rows = chunk_rows(i, chunk)
        normed, _ = normalize(x_ref[rows, :].astype(F32))
        a_scr[rows, :] = (normed * gain_ref[...]).astype(BF)

    for j in range(2):
        pick_wait(refs, dsts, wsem, j)
    outs = []
    for j in range(2):
        k_ref[j, own, :] = mm(a_scr[...], w_scr[j, 1]).astype(BF)
        v_ref[j, own, :] = mm(a_scr[...], w_scr[j, 2]).astype(BF)
        for n, ref in enumerate((k_ref, v_ref)):
            copy = send(ref.at[j, own], ref.at[j, own], (kv_s, kv_r), j * 2 + n, sibling)
            copy.start()
            outs.append(copy)
    for j in range(2):
        q_ref[j] = (mm(a_scr[...], w_scr[j, 0]) * HD**-0.5).astype(BF)
    for copy in outs:
        copy.wait()

    def mix_copy(i, j):
        rows = chunk_rows(i, chunk)
        return send(mixed_ref.at[j, rows], other_scr.at[j, rows], (mix_s, mix_r), i * 2 + j, partner)

    @pl.loop(0, 2)
    def _(i):
        rows = chunk_rows(i, chunk)
        fill_bias(bias_scr, colinfo, rowinfo, rows)

        @pl.loop(0, 2)
        def _(j):
            total = jnp.zeros((chunk, 3 * HD), F32)
            for h in range(3):
                lanes = head_lanes(chunk, h)
                qh = jnp.where(lanes, q_ref[j, rows, :], jnp.zeros((), BF))
                scores = mm_nt(qh, k_ref[j]) + bias_scr[...]
                top = jnp.max(scores, axis=-1, keepdims=True)
                expos = jnp.exp(scores - top)
                norm = jnp.sum(expos, axis=-1, keepdims=True)
                lse_ref[j * 3 + h, rows, :] = top + jnp.log(norm)
                probs = (expos * (1.0 / norm)).astype(BF)
                total = total + jnp.where(lanes, mm(probs, v_ref[j]), 0.0)
            mixed_ref[j, rows, :] = total.astype(BF)
            mix_copy(i, j).start()

    other = partner_of(t)

    @pl.loop(0, 2)
    def _(i):
        rows = chunk_rows(i, chunk)
        total = x_ref[rows, :].astype(F32)
        total = total + mm(mixed_ref[0, rows, :], wout_ref[t])
        total = total + mm(mixed_ref[1, rows, :], wout_ref[across_of(t)])
        for j in range(2):
            mix_copy(i, j).wait()
        total = total + mm(other_scr[0, rows, :], wout_ref[other])
        total = total + mm(other_scr[1, rows, :], wout_ref[across_of(other)])
        x1_ref[rows, :] = total


def attn_fwd(layer, cid, x, gain, colinfo, rowinfo, wout, w):
    count, width = x.shape
    tokens = colinfo.shape[1]
    part = w[0].shape[-1]
    chunk = count // 2
    dma = pltpu.SemaphoreType.DMA
    return pl.pallas_call(
        functools.partial(attn_fwd_kernel, layer),
        out_shape=(
            jax.ShapeDtypeStruct((count, width), F32),
            jax.ShapeDtypeStruct((2, count, part), BF),
            jax.ShapeDtypeStruct((2, tokens, part), BF),
            jax.ShapeDtypeStruct((2, tokens, part), BF),
            jax.ShapeDtypeStruct((2, count, part), BF),
            jax.ShapeDtypeStruct((6, count, 1), F32),
        ),
        in_specs=[pl.BlockSpec(memory_space=VMEM)] * 5 + [pl.BlockSpec(memory_space=ANY)] * 4,
        out_specs=[pl.BlockSpec(memory_space=VMEM)] * 6,
        scratch_shapes=[
            VMEM((2,) + w[0].shape, BF),
            VMEM((count, width), BF),
            VMEM((chunk, tokens), F32),
            VMEM((2, count, part), BF),
            dma((2,)),
            dma((4,)),
            dma((4,)),
            dma((4,)),
            dma((4,)),
        ],
        compiler_params=pltpu.CompilerParams(
            collective_id=cid, has_side_effects=True, vmem_limit_bytes=LIMIT
        ),
        cost_estimate=pl.CostEstimate(flops=20 * 10**9, bytes_accessed=10**7, transcendentals=0),
        name="attn_fwd%d" % layer,
    )(x, gain, colinfo, rowinfo, wout, *w)


def ffn_fwd_kernel(
    layer, x1_ref, gain_ref, ua, ub, uc, ud, da, db, dc, dd,
    y_ref, b_ref, acted_ref, slope_ref,
    up_scr, down_scr, own_scr, out_scr, in_scr, wsem, s_sem, r_sem,
):
    s, d, t = place()
    partner = (s, d, partner_of(t))
    count, width = x1_ref.shape
    units = ua.shape[1]
    refs = [(ua, uc), (ub, ud), (da, dc), (db, dd)]
    dsts = [
        up_scr.at[:, pl.ds(0, units)],
        up_scr.at[:, pl.ds(units, units)],
        down_scr.at[pl.ds(0, units)],
        down_scr.at[pl.ds(units, units)],
    ]
    pick_start(layer, refs, dsts, wsem)
    greet(partner)
    chunk = count // 2
    tile = 256

    def copy_of(i):
        rows = chunk_rows(i, chunk)
        return send(out_scr.at[rows], in_scr.at[rows], (s_sem, r_sem), i, partner)

    for n in range(4):
        pick_wait(refs, dsts, wsem, n)

    @pl.loop(0, 2)
    def _(i):
        rows = chunk_rows(i, chunk)
        normed, _ = normalize(x1_ref[rows, :])
        b_ref[rows, :] = (normed * gain_ref[...]).astype(BF)

        @pl.loop(0, 2 * units // tile)
        def _(n):
            cols = pl.ds(pl.multiple_of(n * tile, tile), tile)
            hidden = mm(b_ref[rows, :], up_scr[:, cols])
            cdf = 0.5 + 0.5 * lax.erf(hidden * 0.5**0.5)
            acted_ref[rows, cols] = (hidden * cdf).astype(BF)
            bell = jnp.exp(hidden * hidden * -0.5) * 0.3989422804014327
            slope_ref[rows, cols] = (cdf + hidden * bell).astype(BF)

        @pl.loop(0, width // tile)
        def _(n):
            cols = pl.ds(pl.multiple_of(n * tile, tile), tile)
            part = mm(acted_ref[rows, :], down_scr[:, cols])
            own_scr[rows, cols] = part
            out_scr[rows, cols] = part.astype(BF)

        copy_of(i).start()

    @pl.loop(0, 2)
    def _(i):
        rows = chunk_rows(i, chunk)
        copy_of(i).wait()
        y_ref[rows, :] = (x1_ref[rows, :] + own_scr[rows, :] + in_scr[rows, :].astype(F32)).astype(BF)


def ffn_fwd(layer, cid, x1, gain, up, down):
    count, width = x1.shape
    units = up[0].shape[1]
    dma = pltpu.SemaphoreType.DMA
    return pl.pallas_call(
        functools.partial(ffn_fwd_kernel, layer),
        out_shape=(
            jax.ShapeDtypeStruct((count, width), BF),
            jax.ShapeDtypeStruct((count, width), BF),
            jax.ShapeDtypeStruct((count, 2 * units), BF),
            jax.ShapeDtypeStruct((count, 2 * units), BF),
        ),
        in_specs=[pl.BlockSpec(memory_space=VMEM)] * 2 + [pl.BlockSpec(memory_space=ANY)] * 8,
        out_specs=[pl.BlockSpec(memory_space=VMEM)] * 4,
        scratch_shapes=[
            VMEM((width, 2 * units), BF),
            VMEM((2 * units, width), BF),
            VMEM((count, width), F32),
            VMEM((count, width), BF),
            VMEM((count, width), BF),
            dma((4,)),
            dma((2,)),
            dma((2,)),
        ],
        compiler_params=pltpu.CompilerParams(
            collective_id=cid, has_side_effects=True, vmem_limit_bytes=LIMIT
        ),
        cost_estimate=pl.CostEstimate(flops=20 * 10**9, bytes_accessed=10**7, transcendentals=0),
        name="ffn_fwd%d" % layer,
    )(x1, gain, *up, *down)


def ffn_bwd_kernel(
    layer, g_ref, x1_ref, gain_ref, b_ref, acted_ref, slope_ref, ua, ub, uc, ud, da, db, dc, dd,
    dx1_ref, dgain_ref, dup_ref, ddown_ref,
    up_scr, down_scr, own_scr, out_scr, in_scr, dh_scr, wsem, s_sem, r_sem,
):
    s, d, t = place()
    partner = (s, d, partner_of(t))
    count, width = x1_ref.shape
    units = ua.shape[1]
    refs = [(da, dc), (db, dd), (ua, uc), (ub, ud)]
    dsts = [
        down_scr.at[pl.ds(0, units)],
        down_scr.at[pl.ds(units, units)],
        up_scr.at[:, pl.ds(0, units)],
        up_scr.at[:, pl.ds(units, units)],
    ]
    pick_start(layer, refs, dsts, wsem)
    greet(partner)
    chunk = count // 2
    tile = 256

    def copy_of(i):
        rows = chunk_rows(i, chunk)
        return send(out_scr.at[rows], in_scr.at[rows], (s_sem, r_sem), i, partner)

    for n in range(4):
        pick_wait(refs, dsts, wsem, n)

    @pl.loop(0, 2)
    def _(i):
        rows = chunk_rows(i, chunk)

        @pl.loop(0, 2 * units // tile)
        def _(n):
            cols = pl.ds(pl.multiple_of(n * tile, tile), tile)
            du = mm_nt(g_ref[rows, :], down_scr[cols, :])
            dh_scr[rows, cols] = (du * slope_ref[rows, cols].astype(F32)).astype(BF)

        @pl.loop(0, width // tile)
        def _(n):
            cols = pl.ds(pl.multiple_of(n * tile, tile), tile)
            part = mm_nt(dh_scr[rows, :], up_scr[cols, :])
            own_scr[rows, cols] = part
            out_scr[rows, cols] = part.astype(BF)

        copy_of(i).start()

    for j in range(2):

        @pl.loop(0, units // tile)
        def _(n):
            here = pl.ds(pl.multiple_of(n * tile, tile), tile)
            cols = pl.ds(pl.multiple_of(n * tile, tile) + j * units, tile)
            ddown_ref[j, here, :] = mm_tn(acted_ref[:, cols], g_ref[...]).astype(BF)
            dup_ref[j, :, here] = mm_tn(b_ref[...], dh_scr[:, cols]).astype(BF)

    dgain_ref[...] = jnp.zeros_like(dgain_ref)

    @pl.loop(0, 2)
    def _(i):
        rows = chunk_rows(i, chunk)
        copy_of(i).wait()
        grad = own_scr[rows, :] + in_scr[rows, :].astype(F32)
        normed, inverse = normalize(x1_ref[rows, :])
        dgain_ref[...] += jnp.sum(grad * normed, axis=0, keepdims=True)
        dx1_ref[rows, :] = g_ref[rows, :].astype(F32) + normalize_back(
            grad, normed, inverse, gain_ref[...]
        )


def ffn_bwd(layer, cid, g, x1, gain, b, acted, slope, up, down):
    count, width = x1.shape
    units = up[0].shape[1]
    dma = pltpu.SemaphoreType.DMA
    return pl.pallas_call(
        functools.partial(ffn_bwd_kernel, layer),
        out_shape=(
            jax.ShapeDtypeStruct((count, width), F32),
            jax.ShapeDtypeStruct((1, width), F32),
            jax.ShapeDtypeStruct((2, width, units), BF),
            jax.ShapeDtypeStruct((2, units, width), BF),
        ),
        in_specs=[pl.BlockSpec(memory_space=VMEM)] * 6 + [pl.BlockSpec(memory_space=ANY)] * 8,
        out_specs=[pl.BlockSpec(memory_space=VMEM)] * 4,
        scratch_shapes=[
            VMEM((width, 2 * units), BF),
            VMEM((2 * units, width), BF),
            VMEM((count, width), F32),
            VMEM((count, width), BF),
            VMEM((count, width), BF),
            VMEM((count, 2 * units), BF),
            dma((4,)),
            dma((2,)),
            dma((2,)),
        ],
        compiler_params=pltpu.CompilerParams(
            collective_id=cid, has_side_effects=True, vmem_limit_bytes=LIMIT
        ),
        cost_estimate=pl.CostEstimate(flops=20 * 10**9, bytes_accessed=10**7, transcendentals=0),
        name="ffn_bwd%d" % layer,
    )(g, x1, gain, b, acted, slope, *up, *down)


def attn_bwd_kernel(
    layer, dx1_ref, x_ref, gain_ref, colinfo, rowinfo, wout_ref, q_ref, k_ref, v_ref, mixed_ref, lse_ref,
    wa, wb, wc, wd,
    dx_ref, dgain_ref, dqkv_ref, dout_ref,
    w_scr, a_scr, bias_scr, dc_scr, dmix_scr, dk_scr, dv_scr, dq_scr, part_scr, other_scr, d_scr,
    own_scr, out_scr, in_scr, wsem, kv_s, kv_r, s_sem, r_sem,
):
    s, d, t = place()
    partner = (s, d, partner_of(t))
    sibling = (1 - s, d, t)
    refs = [(wa, wc), (wb, wd)]
    dsts = [w_scr.at[0], w_scr.at[1]]
    pick_start(layer, refs, dsts, wsem)
    greet(partner, sibling)
    count, width = x_ref.shape
    chunk = count // 2
    tile = 256
    own = pl.ds(pl.multiple_of(s * count, 16), count)
    away = pl.ds(pl.multiple_of((1 - s) * count, 16), count)
    part = q_ref.shape[2]

    @pl.loop(0, 2)
    def _(i):
        rows = chunk_rows(i, chunk)
        normed, _ = normalize(x_ref[rows, :].astype(F32))
        a_scr[rows, :] = (normed * gain_ref[...]).astype(BF)
        dc_scr[rows, :] = dx1_ref[rows, :].astype(BF)

    dmix_scr[0] = mm_nt(dc_scr[...], wout_ref[t]).astype(BF)
    dmix_scr[1] = mm_nt(dc_scr[...], wout_ref[across_of(t)]).astype(BF)
    dk_scr[...] = jnp.zeros_like(dk_scr)
    dv_scr[...] = jnp.zeros_like(dv_scr)

    @pl.loop(0, 2)
    def _(i):
        rows = chunk_rows(i, chunk)
        fill_bias(bias_scr, colinfo, rowinfo, rows)

        @pl.loop(0, 2)
        def _(j):
            total = jnp.zeros((chunk, part), F32)
            for h in range(3):
                lanes = head_lanes(chunk, h)
                zero = jnp.zeros((), BF)
                qh = jnp.where(lanes, q_ref[j, rows, :], zero)
                dmh = jnp.where(lanes, dmix_scr[j, rows, :], zero)
                scores = mm_nt(qh, k_ref[j]) + bias_scr[...]
                probs = jnp.exp(scores - lse_ref[j * 3 + h, rows, :])
                dprobs = mm_nt(dmh, v_ref[j])
                inner = jnp.sum(probs * dprobs, axis=-1, keepdims=True)
                dscores = (probs * (dprobs - inner)).astype(BF)
                total = total + jnp.where(lanes, mm(dscores, k_ref[j]), 0.0)
                dk_scr[j] += mm_tn(dscores, qh)
                dv_scr[j] += mm_tn(probs.astype(BF), dmh)
            dq_scr[j, rows, :] = (total * HD**-0.5).astype(BF)

    part_scr[0] = dk_scr[:, away, :].astype(BF)
    part_scr[1] = dv_scr[:, away, :].astype(BF)
    copies = [send(part_scr.at[n], other_scr.at[n], (kv_s, kv_r), n, sibling) for n in range(2)]
    for copy in copies:
        copy.start()
    dout_ref[0] = mm_tn(mixed_ref[0], dc_scr[...]).astype(BF)
    dout_ref[1] = mm_tn(mixed_ref[1], dc_scr[...]).astype(BF)
    for j in range(2):
        pick_wait(refs, dsts, wsem, j)
    for copy in copies:
        copy.wait()
    d_scr[0] = dq_scr[...]
    d_scr[1] = (dk_scr[:, own, :] + other_scr[0].astype(F32)).astype(BF)
    d_scr[2] = (dv_scr[:, own, :] + other_scr[1].astype(F32)).astype(BF)

    def copy_of(i):
        rows = chunk_rows(i, chunk)
        return send(out_scr.at[rows], in_scr.at[rows], (s_sem, r_sem), i, partner)

    @pl.loop(0, 2)
    def _(i):
        rows = chunk_rows(i, chunk)

        @pl.loop(0, width // tile)
        def _(n):
            cols = pl.ds(pl.multiple_of(n * tile, tile), tile)
            total = jnp.zeros((chunk, tile), F32)
            for e in range(3):
                for j in range(2):
                    total = total + mm_nt(d_scr[e, j, rows, :], w_scr[j, e, cols, :])
            own_scr[rows, cols] = total
            out_scr[rows, cols] = total.astype(BF)

        copy_of(i).start()

    @pl.loop(0, 2)
    def _(j):
        for e in range(3):
            dqkv_ref[j, e] = mm_tn(a_scr[...], d_scr[e, j]).astype(BF)

    dgain_ref[...] = jnp.zeros_like(dgain_ref)

    @pl.loop(0, 2)
    def _(i):
        rows = chunk_rows(i, chunk)
        copy_of(i).wait()
        grad = own_scr[rows, :] + in_scr[rows, :].astype(F32)
        normed, inverse = normalize(x_ref[rows, :].astype(F32))
        dgain_ref[...] += jnp.sum(grad * normed, axis=0, keepdims=True)
        dx_ref[rows, :] = (
            dx1_ref[rows, :] + normalize_back(grad, normed, inverse, gain_ref[...])
        ).astype(BF)


def attn_bwd(layer, cid, dx1, x, gain, colinfo, rowinfo, wout, q, k, v, mixed, lse, w):
    count, width = x.shape
    tokens = colinfo.shape[1]
    part = w[0].shape[-1]
    chunk = count // 2
    dma = pltpu.SemaphoreType.DMA
    return pl.pallas_call(
        functools.partial(attn_bwd_kernel, layer),
        out_shape=(
            jax.ShapeDtypeStruct((count, width), BF),
            jax.ShapeDtypeStruct((1, width), F32),
            jax.ShapeDtypeStruct((2, 3, width, part), BF),
            jax.ShapeDtypeStruct((2, part, width), BF),
        ),
        in_specs=[pl.BlockSpec(memory_space=VMEM)] * 11 + [pl.BlockSpec(memory_space=ANY)] * 4,
        out_specs=[pl.BlockSpec(memory_space=VMEM)] * 4,
        scratch_shapes=[
            VMEM((2,) + w[0].shape, BF),
            VMEM((count, width), BF),
            VMEM((chunk, tokens), F32),
            VMEM((count, width), BF),
            VMEM((2, count, part), BF),
            VMEM((2, tokens, part), F32),
            VMEM((2, tokens, part), F32),
            VMEM((2, count, part), BF),
            VMEM((2, 2, count, part), BF),
            VMEM((2, 2, count, part), BF),
            VMEM((3, 2, count, part), BF),
            VMEM((count, width), F32),
            VMEM((count, width), BF),
            VMEM((count, width), BF),
            dma((2,)),
            dma((2,)),
            dma((2,)),
            dma((2,)),
            dma((2,)),
        ],
        compiler_params=pltpu.CompilerParams(
            collective_id=cid, has_side_effects=True, vmem_limit_bytes=LIMIT
        ),
        cost_estimate=pl.CostEstimate(flops=30 * 10**9, bytes_accessed=10**7, transcendentals=0),
        name="attn_bwd%d" % layer,
    )(dx1, x, gain, colinfo, rowinfo, wout, q, k, v, mixed, lse, *w)


BOTH = ("section", "tensor")


def route(block, pairs):
    return lax.ppermute(block, BOTH, pairs)


def after(block, *others):
    return lax.optimization_barrier((block,) + others)[0]


def token_info(size, length, offsets, core, count):
    patches = GRID * GRID
    tokens = jnp.arange(patches + QL, dtype=jnp.int32)
    is_patch = tokens < patches
    row, col = tokens // GRID, tokens % GRID
    live_patch = is_patch & (row < size[0]) & (col < size[1])
    live_answer = jnp.logical_not(is_patch) & (tokens - patches < length)
    window = (row + offsets[0]) // WIN * 8 + (col + offsets[1]) // WIN
    cw = jnp.where(live_patch, window, -1)
    ca = jnp.where(live_patch, -1, jnp.where(live_answer, tokens, 1 << 20))
    colinfo = jnp.stack([cw, ca, tokens] + [tokens] * 5)
    rw = jnp.where(is_patch, window, -2)
    ra = jnp.where(is_patch, -5, tokens)
    rowinfo = jnp.stack([rw, ra, tokens], axis=1)
    return colinfo, lax.dynamic_slice_in_dim(rowinfo, core * count, count, 0)


def on_device(inputs, cotangent, w_qkv, w_out, w_up, w_down, gains, image_sizes, lengths, shifts):
    core = lax.axis_index("section")
    t = lax.axis_index("tensor")
    dp = lax.axis_size("dp")
    pair = t // 2
    quarter, width = inputs.shape[1], inputs.shape[2]
    count = 2 * quarter

    def images_in(block):
        def one(i, j):
            pairs = [(k * 4 + 2 * c + j, c * 4 + 2 * i + k) for c in range(2) for k in range(2)]
            return route(block[i], pairs)

        parts = [jnp.where(pair == 0, one(0, j), one(1, j)) for j in range(2)]
        return jnp.concatenate(parts, axis=0)

    def images_out(rows, section):
        mine = lax.dynamic_slice_in_dim(rows, lax.rem(t, 2) * quarter, quarter, 0)
        return [
            route(mine, [(c * 4 + 2 * i + m, section * 4 + 2 * c + m) for c in range(2) for m in range(2)])
            for i in range(2)
        ]

    across = [[(c * 4 + i, c * 4 + (i + 2) % 4) for i in range(4)] for c in range(2)]
    cores = [(i, (i + 4) % 8) for i in range(8)]

    def fetch(block, anchor=None):
        if anchor is not None:
            block = after(block, anchor)
        far = route(block, across[0] + across[1])
        return [block, far, route(block, cores), route(far, cores)]

    x = images_in(inputs)
    qkv_ws = fetch(w_qkv[0])
    every_out = lax.all_gather(w_out[0], "tensor", axis=0)
    every_out = lax.all_gather(every_out, "section", axis=0)
    gain_all = lax.all_gather(gains[0], "section", axis=0)
    up_ws = fetch(w_up[0])
    down_ws = fetch(w_down[0])
    cot = images_in(cotangent)

    size = lax.dynamic_index_in_dim(image_sizes, pair, 0, keepdims=False)
    length = lax.dynamic_index_in_dim(lengths, pair, 0, keepdims=False)

    kept = []
    for layer in range(2):
        info = token_info(size, length, shifts * layer, core, count)
        one, two = gain_all[layer, 0][None], gain_all[layer, 1][None]
        x1, q, k, v, mixed, lse = attn_fwd(layer, layer, x, one, *info, every_out[layer], qkv_ws)
        y, b, acted, slope = ffn_fwd(layer, 2 + layer, x1, two, up_ws, down_ws)
        kept.append((x, x1, q, k, v, mixed, lse, b, acted, slope, info, one, two))
        x = y

    out_y = images_out(y, 1)

    def reduce_weights(layer, grad, dim):
        own, far = grad[0], grad[1]
        here, there = layer, 1 - layer
        far = far + route(far, [(here * 4 + i, there * 4 + i) for i in range(4)])
        own_more = route(own, [(there * 4 + i, here * 4 + i) for i in range(4)])
        far_more = route(far, [(there * 4 + i, here * 4 + (i + 2) % 4) for i in range(4)])
        total = own + own_more + far_more
        return lax.psum_scatter(total, "dp", scatter_dimension=dim, tiled=True).astype(F32)

    g = cot
    grads = [None, None]
    gain_grads = [None, None]
    for layer in (1, 0):
        x, x1, q, k, v, mixed, lse, b, acted, slope, info, one, two = kept[layer]
        dx1, dtwo, dup, ddown = ffn_bwd(layer, 4 + layer, g, x1, two, b, acted, slope, up_ws, down_ws)
        g_up = reduce_weights(layer, dup, 0)
        g_down = reduce_weights(layer, ddown, 0)
        g, done, dqkv, dout = attn_bwd(
            layer, 6 + layer, dx1, x, one, *info, every_out[layer], q, k, v, mixed, lse, qkv_ws
        )
        g_qkv = reduce_weights(layer, dqkv, 1)
        g_out = reduce_weights(layer, dout, 1)
        grads[layer] = (g_qkv, g_out, g_up, g_down)
        gain_grads[layer] = jnp.concatenate([done, dtwo], axis=0)

    out_g = images_out(g, 0)
    ends = jnp.stack([jnp.where(core == 0, a, b) for a, b in zip(out_g, out_y)])
    shares = [jnp.where(core == 0, a, b)[None] for a, b in zip(*grads)]
    gain_total = lax.psum(jnp.stack(gain_grads) * 0.5, ("section", "dp", "tensor"))
    mine = lax.dynamic_index_in_dim(gain_total, core, 0, keepdims=True)
    share = width // (dp * 4)
    slot = lax.axis_index("dp") * 4 + t
    gain_share = lax.dynamic_slice_in_dim(mine, slot * share, share, 2)
    return (ends[None], *shares, gain_share)


def solution(mesh):
    placed = (
        P("dp", "tensor", None),
        P("dp", "tensor", None),
        P("section", None, None, "tensor"),
        P("section", "tensor", None),
        P("section", None, "tensor"),
        P("section", "tensor", None),
        P("section", None, None),
        P("dp", None),
        P("dp"),
        P(),
    )
    return jax.shard_map(
        on_device,
        mesh=mesh,
        in_specs=placed,
        out_specs=(
            P("section", "dp", "tensor", None),
            P("section", None, "dp", "tensor"),
            P("section", "tensor", "dp"),
            P("section", "dp", "tensor"),
            P("section", ("tensor", "dp"), None),
            P("section", None, ("dp", "tensor")),
        ),
        check_vma=False,
    )
```

```python
import functools

import jax
import jax.numpy as jnp
from jax import lax
from jax.experimental import pallas as pl
from jax.experimental.pallas import tpu as pltpu
from jax.sharding import PartitionSpec as P

MESH = pl.DeviceIdType.MESH
VMEM = pltpu.VMEM
ANY = pl.ANY
BF = jnp.bfloat16
F32 = jnp.float32

HD = 64
WIN = 12
GRID = 24
QL = 512
EPS = 1e-05
OFF = -1e30
TILE = 256

NT = (((1,), (1,)), ((), ()))
TN = (((0,), (0,)), ((), ()))


def mm(a, b):
    return jnp.dot(a, b, preferred_element_type=F32)


def mm_nt(a, b):
    return lax.dot_general(a, b, NT, preferred_element_type=F32)


def mm_tn(a, b):
    return lax.dot_general(a, b, TN, preferred_element_type=F32)


def normalize(values):
    centered = values - jnp.mean(values, axis=-1, keepdims=True)
    inverse = lax.rsqrt(jnp.mean(centered * centered, axis=-1, keepdims=True) + EPS)
    return centered * inverse, inverse


def normalize_back(grad, normed, inverse, gain):
    t = grad * gain
    return inverse * (
        t
        - jnp.mean(t, axis=-1, keepdims=True)
        - normed * jnp.mean(t * normed, axis=-1, keepdims=True)
    )


def head_lanes(rows, h):
    lanes = lax.broadcasted_iota(jnp.int32, (rows, 3 * HD), 1)
    return (lanes >= h * HD) & (lanes < h * HD + HD)


def column_of(block, n):
    lanes = lax.broadcasted_iota(jnp.int32, block.shape, 1)
    return jnp.sum(jnp.where(lanes == n, block, 0.0), axis=-1, keepdims=True)


def tile_of(n, size=TILE):
    return pl.ds(pl.multiple_of(n * size, size), size)


BUFFERS = (
    ("x_v", lambda z: (2, z.count, z.width), BF),
    ("g_v", lambda z: (z.count, z.width), BF),
    ("gain_v", lambda z: (2, 2, z.width), F32),
    ("wa_v", lambda z: (2, 4, 2, z.width, z.part), BF),
    ("wf_v", lambda z: (2, 2, 2, z.width, z.width), BF),
    ("wo_v", lambda z: (2, 4, z.part, z.width), BF),
    ("q_v", lambda z: (2, 2, z.count, z.part), BF),
    ("k_v", lambda z: (2, 2, z.tokens, z.part), BF),
    ("v_v", lambda z: (2, 2, z.tokens, z.part), BF),
    ("mixed_v", lambda z: (2, 2, z.count, z.part), BF),
    ("mixr_v", lambda z: (2, z.count, z.part), BF),
    ("lse_v", lambda z: (2, z.count, 128), F32),
    ("x1_v", lambda z: (z.count, z.width), F32),
    ("dx1_v", lambda z: (z.count, z.width), F32),
    ("b_v", lambda z: (z.count, z.width), BF),
    ("acted_v", lambda z: (z.count, 2 * z.width), BF),
    ("slope_v", lambda z: (z.count, 2 * z.width), BF),
    ("a_v", lambda z: (z.count, z.width), BF),
    ("dc_v", lambda z: (z.count, z.width), BF),
    ("out_v", lambda z: (z.count, z.width), BF),
    ("in_v", lambda z: (2, z.count, z.width), BF),
    ("yout_v", lambda z: (z.quarter, z.width), BF),
    ("yin_v", lambda z: (z.quarter, z.width), BF),
    ("bias_v", lambda z: (z.quarter, z.tokens), F32),
    ("dk_v", lambda z: (2, z.tokens, z.part), F32),
    ("dv_v", lambda z: (2, z.tokens, z.part), F32),
    ("dmix_v", lambda z: (2, z.count, z.part), BF),
    ("part_v", lambda z: (2, 2, z.count, z.part), BF),
    ("other_v", lambda z: (2, 2, z.count, z.part), BF),
    ("dkv_v", lambda z: (2, 2, z.count, z.part), BF),
    ("crecv_f", lambda z: (2, z.width, z.width), BF),
    ("yrecv_f", lambda z: (z.width, z.width), BF),
    ("zsend_f", lambda z: (z.dp, z.rows, z.width), BF),
    ("crecv_a", lambda z: (2, 2, z.width, z.part), BF),
    ("yrecv_a", lambda z: (2, z.width, z.part), BF),
    ("zsend_a", lambda z: (2, z.dp, z.rows, z.part), BF),
    ("gain_g", lambda z: (2, 2, z.width), F32),
    ("gain_i", lambda z: (8, 2, 2, z.width), F32),
    ("gain_z", lambda z: (z.dp, 2, 2, z.width), F32),
)

PAIRS = (
    ("xs", lambda z: 2),
    ("cs", lambda z: 2),
    ("gs", lambda z: 1),
    ("wsib", lambda z: 6),
    ("wy", lambda z: 6),
    ("wfwd", lambda z: 6),
    ("wo", lambda z: 16),
    ("kv", lambda z: 8),
    ("mix", lambda z: 4),
    ("ar", lambda z: 4),
    ("yy", lambda z: 1),
    ("pt", lambda z: 2),
    ("cf", lambda z: 1),
    ("ca", lambda z: 1),
    ("yf", lambda z: 1),
    ("ya", lambda z: 1),
    ("zf", lambda z: 2 * z.dp),
    ("za", lambda z: 4 * z.dp),
    ("en", lambda z: 4),
    ("ga", lambda z: 8),
    ("gz", lambda z: z.dp),
)
LOCALS = (("lw", 8), ("lx", 4), ("lh", 4), ("lz", 2), ("le", 2))
CREDITS = ("free_pt", "free_cf", "free_ca", "free_yf", "free_ya")


class Sizes:
    pass


def kernel(z, *refs):
    names = (
        ["inputs", "cotangent", "w_qkv", "w_out", "w_up", "w_down", "gains", "colinfo", "rowinfo"]
        + ["ends", "zf_o", "za_o", "dgain", "h_x1", "h_b", "h_acted", "h_slope"]
        + [n for n, _, _ in BUFFERS]
        + [n + e for n, _ in PAIRS for e in ("_s", "_r")]
        + [n for n, _ in LOCALS]
        + list(CREDITS)
    )
    r = Sizes()
    for name, ref in zip(names, refs, strict=True):
        setattr(r, name, ref)

    c, d, t = lax.axis_index("section"), lax.axis_index("dp"), lax.axis_index("tensor")
    m, p = lax.rem(t, 2), t // 2
    px, ax = t + 1 - 2 * m, lax.rem(t + 2, 4)
    dx = ax + 1 - 2 * m
    sib, par, acr, dia = (1 - c, d, t), (c, d, px), (c, d, ax), (c, d, dx)
    quarter, count, width, dp = z.quarter, z.count, z.width, z.dp

    def remote(src, dst, name, n, device, rn=None):
        return pltpu.make_async_remote_copy(
            src_ref=src,
            dst_ref=dst,
            send_sem=getattr(r, name + "_s").at[n],
            recv_sem=getattr(r, name + "_r").at[n if rn is None else rn],
            device_id=device,
            device_id_type=MESH,
        )

    def local(src, dst, name, n):
        return pltpu.make_async_copy(src, dst, getattr(r, name).at[n])

    def rows_of(i):
        return pl.ds(pl.multiple_of(i * quarter, 16), quarter)

    mine = pl.ds(pl.multiple_of(c * count, 16), count)
    away = pl.ds(pl.multiple_of((1 - c) * count, 16), count)

    def own_weights(n):
        src = (r.w_qkv, r.w_up, r.w_down, r.w_out, r.gains)[n]
        dst = (
            lambda: r.wa_v.at[c, pl.ds(0, 3), 0],
            lambda: r.wf_v.at[c, 0, 0],
            lambda: r.wf_v.at[c, 1, 0],
            lambda: r.wo_v.at[c, t],
            lambda: r.gain_v.at[c],
        )[n]
        return local(src, dst(), "lw", n)

    for n in range(5):
        own_weights(n).start()

    barrier = pltpu.get_barrier_semaphore()

    def hello(device):
        pl.semaphore_signal(barrier, inc=1, device_id=device, device_id_type=MESH)

    for e in range(4):
        @pl.when(e != t)
        def _():
            hello((c, d, e))

        hello((1 - c, d, e))

    @pl.loop(0, dp)
    def _(e):
        @pl.when(e != d)
        def _():
            hello((c, e, t))
            hello((1 - c, e, t))

    pl.semaphore_wait(barrier, 7 + 2 * (dp - 1))

    def spread(src, dst, name, base):
        def copies(i):
            there = (p, d, 2 * i + c)
            stays = (c == p) & (t == 2 * i + c)

            def far():
                return remote(src.at[i], dst.at[rows_of(m)], name, i, there, rn=m)

            def near():
                return local(src.at[i], dst.at[rows_of(m)], "lx", base + i)

            return stays, far, near

        def start():
            for i in range(2):
                stays, far, near = copies(i)
                pl.when(stays)(lambda: near().start())
                pl.when(jnp.logical_not(stays))(lambda: far().start())

        def wait():
            for i in range(2):
                stays, far, near = copies(i)
                pl.when(stays)(lambda: near().wait())
                pl.when(jnp.logical_not(stays))(lambda: far().wait_send())
            for j in range(2):
                came = jnp.logical_not((c == m) & (t == 2 * c + j))

                @pl.when(came)
                def _():
                    remote(src.at[0], dst.at[rows_of(j)], name, j, par).wait_recv()

        return start, wait

    x_start, x_wait = spread(r.inputs, r.x_v.at[0], "xs", 0)
    c_start, c_wait = spread(r.cotangent, r.g_v, "cs", 2)
    x_start()

    gain_copy = remote(r.gains, r.gain_v.at[c], "gs", 0, sib)
    gain_copy.start()

    sources = (r.w_qkv, r.w_up, r.w_down)

    def slot(layer, piece, j):
        if piece == 0:
            return r.wa_v.at[layer, pl.ds(0, 3), j]
        return r.wf_v.at[layer, piece - 1, j]

    def to_sib(layer, piece):
        return remote(sources[piece], slot(layer, piece, 0), "wsib", layer * 3 + piece, sib)

    def to_acr(layer, piece):
        return remote(sources[piece], slot(layer, piece, 1), "wy", layer * 3 + piece, acr)

    def forward(layer, piece):
        far = slot(layer, piece, 1)
        return remote(far, far, "wfwd", layer * 3 + piece, sib)

    def owner_starts(layer, make, pieces):
        @pl.when(c == layer)
        def _():
            for piece in pieces:
                make(layer, piece).start()

    def need_own(layer, piece):
        @pl.when(c == layer)
        def _():
            own_weights(piece).wait()

        @pl.when(c != layer)
        def _():
            to_sib(layer, piece).wait_recv()

    def need_far(layer, piece):
        @pl.when(c == layer)
        def _():
            to_acr(layer, piece).wait()
            forward(layer, piece).start()

        @pl.when(c != layer)
        def _():
            forward(layer, piece).wait_recv()

    def wo_copy(layer, e, device, n):
        here = r.wo_v.at[layer, e]
        return remote(r.w_out, here, "wo", n, device, rn=layer * 4 + e)

    def wo_start(layer):
        @pl.when(c == layer)
        def _():
            for n, device in enumerate((par, acr, dia, sib)):
                wo_copy(layer, t, device, layer * 8 + n).start()

    def wo_pass(layer, n):
        e = (px, ax, dx)[n]
        here = r.wo_v.at[layer, e]
        return remote(here, here, "wo", layer * 8 + 4 + n, sib, rn=layer * 4 + e)

    def need_wo(layer):
        @pl.when(c == layer)
        def _():
            own_weights(3).wait()
            for n in range(3):
                e = (px, ax, dx)[n]
                wo_copy(layer, e, par, 0).wait_recv()
                wo_pass(layer, n).start()

        @pl.when(c != layer)
        def _():
            for e in (t, px, ax, dx):
                wo_copy(layer, e, par, 0).wait_recv()

    def finish_weights(layer):
        @pl.when(c == layer)
        def _():
            for piece in range(3):
                to_sib(layer, piece).wait_send()
                forward(layer, piece).wait_send()
            for n, device in enumerate((par, acr, dia, sib)):
                wo_copy(layer, t, device, layer * 8 + n).wait_send()
            for n in range(3):
                wo_pass(layer, n).wait_send()

    for layer in range(2):
        owner_starts(layer, to_sib, (0,))
    owner_starts(0, to_acr, (0,))
    wo_start(0)
    own_weights(4).wait()
    gain_copy.wait()

    def kv_copy(layer, j, n):
        here = (r.k_v, r.v_v)[n].at[layer, j, mine]
        return remote(here, here, "kv", layer * 4 + j * 2 + n, sib)

    def mix_copy(layer, i, j):
        return remote(
            r.mixed_v.at[layer, j, rows_of(i)], r.mixr_v.at[j, rows_of(i)], "mix", i * 2 + j, par
        )

    def fill_bias(layer, i):
        info = r.rowinfo[layer, rows_of(i), :]
        cw, ca, cj = (r.colinfo[layer, n : n + 1, :] for n in range(3))
        rw, ra, ri = info[:, 0:1], info[:, 1:2], info[:, 2:3]
        allowed = (cw == rw) | (ca < ra) | (cj == ri)
        r.bias_v[...] = jnp.where(allowed, 0.0, OFF)

    def make_a(layer):
        @pl.loop(0, 2)
        def _(i):
            rows = rows_of(i)
            normed, _ = normalize(r.x_v[layer, rows, :].astype(F32))
            r.a_v[rows, :] = (normed * r.gain_v[layer, 0:1, :]).astype(BF)

    def attention(layer):
        make_a(layer)
        for j in range(2):
            if j == 0:
                need_own(layer, 0)
            else:
                need_far(layer, 0)
                if layer == 0:
                    owner_starts(0, to_sib, (1, 2))
                    owner_starts(1, to_sib, (1, 2))
                    owner_starts(0, to_acr, (1, 2))
                    c_start()
                else:
                    owner_starts(1, to_acr, (1, 2))
            r.k_v[layer, j, mine, :] = mm(r.a_v[...], r.wa_v[layer, 1, j]).astype(BF)
            kv_copy(layer, j, 0).start()
            r.v_v[layer, j, mine, :] = mm(r.a_v[...], r.wa_v[layer, 2, j]).astype(BF)
            kv_copy(layer, j, 1).start()
            r.q_v[layer, j] = (mm(r.a_v[...], r.wa_v[layer, 0, j]) * HD**-0.5).astype(BF)
        for j in range(2):
            for n in range(2):
                kv_copy(layer, j, n).wait()

        @pl.loop(0, 2)
        def _(i):
            rows = rows_of(i)
            fill_bias(layer, i)
            r.lse_v[layer, rows, :] = jnp.zeros((quarter, 128), F32)

            @pl.loop(0, 2)
            def _(j):
                total = jnp.zeros((quarter, z.part), F32)
                lane = lax.broadcasted_iota(jnp.int32, (quarter, 128), 1)
                for h in range(3):
                    lanes = head_lanes(quarter, h)
                    qh = jnp.where(lanes, r.q_v[layer, j, rows, :], jnp.zeros((), BF))
                    scores = mm_nt(qh, r.k_v[layer, j]) + r.bias_v[...]
                    top = jnp.max(scores, axis=-1, keepdims=True)
                    expos = jnp.exp(scores - top)
                    norm = jnp.sum(expos, axis=-1, keepdims=True)
                    r.lse_v[layer, rows, :] = jnp.where(
                        lane == j * 3 + h, top + jnp.log(norm), r.lse_v[layer, rows, :]
                    )
                    probs = (expos * (1.0 / norm)).astype(BF)
                    total = total + jnp.where(lanes, mm(probs, r.v_v[layer, j]), 0.0)
                r.mixed_v[layer, j, rows, :] = total.astype(BF)
                mix_copy(layer, i, j).start()

    def project(layer, i):
        rows = rows_of(i)
        total = r.x_v[layer, rows, :].astype(F32)
        total = total + mm(r.mixed_v[layer, 0, rows, :], r.wo_v[layer, t])
        total = total + mm(r.mixed_v[layer, 1, rows, :], r.wo_v[layer, ax])
        for j in range(2):
            mix_copy(layer, i, j).wait()
        total = total + mm(r.mixr_v[0, rows, :], r.wo_v[layer, px])
        total = total + mm(r.mixr_v[1, rows, :], r.wo_v[layer, dx])
        r.x1_v[rows, :] = total
        normed, _ = normalize(total)
        r.b_v[rows, :] = (normed * r.gain_v[layer, 1:2, :]).astype(BF)

    def ar_copy(n, i):
        return remote(
            r.out_v.at[rows_of(i)], r.in_v.at[n % 2, rows_of(i)], "ar", (n % 2) * 2 + i, par
        )

    def summed(n, rows):
        return r.out_v[rows, :].astype(F32) + r.in_v[n % 2, rows, :].astype(F32)

    def hidden_of(layer, i, n):
        j, here = n // (width // TILE), tile_of(lax.rem(n, width // TILE))
        hidden = mm(r.b_v[rows_of(i), :], r.wf_v[layer, 0, j, :, here])
        cdf = 0.5 + 0.5 * lax.erf(hidden * 0.5**0.5)
        bell = jnp.exp(hidden * hidden * -0.5) * 0.3989422804014327
        return hidden * cdf, cdf + hidden * bell

    def down_tile(layer, rows, n):
        here = tile_of(n)
        return mm(r.acted_v[rows, pl.ds(0, width)], r.wf_v[layer, 1, 0, :, here]) + mm(
            r.acted_v[rows, pl.ds(width, width)], r.wf_v[layer, 1, 1, :, here]
        )

    def dhidden_of(layer, i, n):
        j, here = n // (width // TILE), tile_of(lax.rem(n, width // TILE))
        return mm_nt(r.g_v[rows_of(i), :], r.wf_v[layer, 1, j, here, :])

    def up_back_tile(layer, rows, n):
        here = tile_of(n)
        return mm_nt(r.slope_v[rows, pl.ds(0, width)], r.wf_v[layer, 0, 0, here, :]) + mm_nt(
            r.slope_v[rows, pl.ds(width, width)], r.wf_v[layer, 0, 1, here, :]
        )

    units = 2 * width // TILE

    x_wait()
    attention(0)
    need_wo(0)
    for piece in (1, 2):
        need_own(0, piece)
        need_far(0, piece)
    owner_starts(1, to_acr, (0,))
    wo_start(1)

    @pl.loop(0, 2)
    def _(i):
        rows = rows_of(i)
        project(0, i)

        @pl.loop(0, units)
        def _(n):
            acted, slope = hidden_of(0, i, n)
            r.acted_v[rows, tile_of(n)] = acted.astype(BF)
            r.slope_v[rows, tile_of(n)] = slope.astype(BF)

        @pl.loop(0, width // TILE)
        def _(n):
            r.out_v[rows, tile_of(n)] = down_tile(0, rows, n).astype(BF)

        ar_copy(0, i).start()

    kept = [
        (r.x1_v, r.h_x1),
        (r.b_v, r.h_b),
        (r.acted_v, r.h_acted),
        (r.slope_v, r.h_slope),
    ]
    for n, (here, there) in enumerate(kept):
        local(here, there, "lh", n).start()

    @pl.loop(0, 2)
    def _(i):
        rows = rows_of(i)
        ar_copy(0, i).wait()
        r.x_v[1, rows, :] = (r.x1_v[rows, :] + summed(0, rows)).astype(BF)

    attention(1)
    need_wo(1)
    for piece in (1, 2):
        need_own(1, piece)
        need_far(1, piece)
    c_wait()
    for n, (here, there) in enumerate(kept):
        local(here, there, "lh", n).wait()

    @pl.loop(0, 2)
    def _(i):
        rows = rows_of(i)
        project(1, i)

        @pl.loop(0, units)
        def _(n):
            acted, slope = hidden_of(1, i, n)
            r.acted_v[rows, tile_of(n)] = acted.astype(BF)
            r.slope_v[rows, tile_of(n)] = (dhidden_of(1, i, n) * slope).astype(BF)

        @pl.loop(0, width // TILE)
        def _(n):
            r.out_v[rows, tile_of(n)] = up_back_tile(1, rows, n).astype(BF)

        ar_copy(1, i).start()

    own_rows, par_rows = rows_of(m), rows_of(1 - m)

    @pl.loop(0, width // TILE)
    def _(n):
        r.yout_v[:, tile_of(n)] = down_tile(1, par_rows, n).astype(BF)

    y_copy = remote(r.yout_v, r.yin_v, "yy", 0, par)
    y_copy.start()

    @pl.loop(0, width // TILE)
    def _(n):
        cols = tile_of(n)
        r.dx1_v[pl.ds(0, quarter), cols] = down_tile(1, own_rows, n) + r.x1_v[own_rows, cols]

    def end_copies(src, section):
        stays = (c == section) & (p == section)

        def far():
            return remote(src, r.ends.at[p], "en", section * 2, (section, d, 2 * c + m), rn=p)

        return stays, far, lambda: local(src, r.ends.at[p], "le", section)

    def end_start(src, section):
        stays, far, near = end_copies(src, section)
        pl.when(stays)(lambda: near().start())
        pl.when(jnp.logical_not(stays))(lambda: far().start())

    def end_sent(src, section):
        stays, far, near = end_copies(src, section)
        pl.when(stays)(lambda: near().wait())
        pl.when(jnp.logical_not(stays))(lambda: far().wait_send())

    def end_arrived(src):
        for i in range(2):
            came = jnp.logical_not((c == p) & (i == c))

            @pl.when(came)
            def _():
                remote(src, r.ends.at[i], "en", i, par).wait_recv()

    def grad_f(layer):
        for j in range(2):

            @pl.loop(0, width // TILE)
            def _(n):
                here = tile_of(n)
                cols = pl.ds(pl.multiple_of(n * TILE, TILE) + j * width, TILE)
                r.wf_v[layer, 0, j, :, here] = mm_tn(r.b_v[...], r.slope_v[:, cols]).astype(BF)
                r.wf_v[layer, 1, j, here, :] = mm_tn(r.acted_v[:, cols], r.g_v[...]).astype(BF)

    def core_f(layer):
        return remote(r.wf_v.at[layer, 1 - c], r.crecv_f, "cf", 0, sib)

    def core_a(layer):
        return remote(
            r.wa_v.at[layer, pl.ds(2 * (1 - c), 2)], r.crecv_a, "ca", 0, sib
        )

    y_f = remote(r.crecv_f.at[1], r.yrecv_f, "yf", 0, acr)
    y_a = remote(r.crecv_a.at[:, 1], r.yrecv_a, "ya", 0, acr)

    def credit(name, device):
        pl.semaphore_signal(getattr(r, name), inc=1, device_id=device, device_id_type=MESH)

    def spend(name):
        pl.semaphore_wait(getattr(r, name), 1)

    def z_copies(layer, which, item, e):
        zsend = r.zsend_f if which == "zf" else r.zsend_a.at[item]
        land = r.zf_o.at[c, d] if which == "zf" else r.za_o.at[2 * c + item, d]
        index = e if which == "zf" else item * dp + e
        return remote(zsend.at[e], land, which, index, (layer, e, t), rn=zr(which, c, item, d))

    def zr(which, core, item, e):
        return core * dp + e if which == "zf" else (2 * core + item) * dp + e

    group = 1 if z.rows % 16 == 0 else 2

    def stage2_f(layer):
        core_f(layer).wait()

        @pl.loop(0, width // 128)
        def _(n):
            rows = tile_of(n, 128)
            r.crecv_f[1, rows, :] = (
                r.crecv_f[1, rows, :].astype(F32) + r.wf_v[layer, c, 1, rows, :].astype(F32)
            ).astype(BF)

        if layer == 0:
            spend("free_yf")
        y_f.start()

    def stage2_a(layer):
        core_a(layer).wait()
        for item in range(2):

            @pl.loop(0, width // 128)
            def _(n):
                rows = tile_of(n, 128)
                r.crecv_a[item, 1, rows, :] = (
                    r.crecv_a[item, 1, rows, :].astype(F32)
                    + r.wa_v[layer, 2 * c + item, 1, rows, :].astype(F32)
                ).astype(BF)

        if layer == 0:
            spend("free_ya")
        y_a.start()

    def z_wait_sends(layer, which):
        for item in range(1 if which == "zf" else 2):

            @pl.loop(0, dp)
            def _(e):
                @pl.when((c != layer) | (e != d))
                def _():
                    z_copies(layer, which, item, e).wait_send()

    def z_near(which, item):
        zsend = r.zsend_f if which == "zf" else r.zsend_a.at[item]
        land = r.zf_o.at[c, d] if which == "zf" else r.za_o.at[2 * c + item, d]
        return local(zsend.at[d], land, "lz", item)

    def z_send(layer, which):
        for item in range(1 if which == "zf" else 2):

            @pl.loop(0, dp)
            def _(e):
                @pl.when((c != layer) | (e != d))
                def _():
                    z_copies(layer, which, item, e).start()

            @pl.when(c == layer)
            def _():
                near = z_near(which, item)
                near.start()
                near.wait()

    def z_arrived(which):
        for core in range(2):
            for item in range(1 if which == "zf" else 2):

                @pl.loop(0, dp)
                def _(e):
                    @pl.when((core != c) | (e != d))
                    def _():
                        z_arrival(which, core, item, e).wait_recv()

    def z_arrival(which, core, item, e):
        zsend = r.zsend_f if which == "zf" else r.zsend_a.at[item]
        land = r.zf_o.at[core, e] if which == "zf" else r.za_o.at[2 * core + item, e]
        return remote(zsend.at[0], land, which, 0, par, rn=zr(which, core, item, e))

    def stage3_f(layer):
        y_f.wait()
        if layer == 0:
            z_wait_sends(1, "zf")

        @pl.loop(0, dp // group)
        def _(e):
            rows = tile_of(e, group * z.rows)
            total = (
                r.crecv_f[0, rows, :].astype(F32)
                + r.wf_v[layer, c, 0, rows, :].astype(F32)
                + r.yrecv_f[rows, :].astype(F32)
            )
            r.zsend_f[pl.ds(e * group, group)] = total.reshape(group, z.rows, width).astype(BF)

        if layer == 1:
            credit("free_cf", sib)
            credit("free_yf", acr)
        z_send(layer, "zf")

    def stage3_a(layer):
        y_a.wait()
        if layer == 0:
            z_wait_sends(1, "za")
        for item in range(2):

            @pl.loop(0, dp // group)
            def _(e):
                rows = tile_of(e, group * z.rows)
                total = (
                    r.crecv_a[item, 0, rows, :].astype(F32)
                    + r.wa_v[layer, 2 * c + item, 0, rows, :].astype(F32)
                    + r.yrecv_a[item, rows, :].astype(F32)
                )
                r.zsend_a[item, pl.ds(e * group, group)] = total.reshape(
                    group, z.rows, z.part
                ).astype(BF)

        if layer == 1:
            credit("free_ca", sib)
            credit("free_ya", acr)
        z_send(layer, "za")

    r.gain_g[...] = jnp.zeros_like(r.gain_g)

    def gain_grad(layer, n, i, grad, normed):
        share = jnp.where(i == m, 1.0, 0.0)
        r.gain_g[layer, n : n + 1, :] += share * jnp.sum(grad * normed, axis=0, keepdims=True)

    def after_ffn(layer, n):
        @pl.loop(0, 2)
        def _(i):
            rows = rows_of(i)
            ar_copy(n, i).wait()
            grad = summed(n, rows)
            normed, inverse = normalize(r.x1_v[rows, :])
            gain_grad(layer, 1, i, grad, normed)
            back = normalize_back(grad, normed, inverse, r.gain_v[layer, 1:2, :])
            dx1 = r.g_v[rows, :].astype(F32) + back
            r.dx1_v[rows, :] = dx1
            r.dc_v[rows, :] = dx1.astype(BF)

    def pt_copy(n):
        return remote(r.part_v.at[n], r.other_v.at[n], "pt", n, sib)

    def attention_back(layer, middle):
        r.dmix_v[0] = mm_nt(r.dc_v[...], r.wo_v[layer, t]).astype(BF)
        r.dmix_v[1] = mm_nt(r.dc_v[...], r.wo_v[layer, ax]).astype(BF)
        r.dk_v[...] = jnp.zeros_like(r.dk_v)
        r.dv_v[...] = jnp.zeros_like(r.dv_v)

        @pl.loop(0, 2)
        def _(i):
            rows = rows_of(i)
            fill_bias(layer, i)

            @pl.loop(0, 2)
            def _(j):
                total = jnp.zeros((quarter, z.part), F32)
                zero = jnp.zeros((), BF)
                for h in range(3):
                    lanes = head_lanes(quarter, h)
                    qh = jnp.where(lanes, r.q_v[layer, j, rows, :], zero)
                    dmh = jnp.where(lanes, r.dmix_v[j, rows, :], zero)
                    scores = mm_nt(qh, r.k_v[layer, j]) + r.bias_v[...]
                    probs = jnp.exp(scores - column_of(r.lse_v[layer, rows, :], j * 3 + h))
                    dprobs = mm_nt(dmh, r.v_v[layer, j])
                    inner = jnp.sum(probs * dprobs, axis=-1, keepdims=True)
                    dscores = (probs * (dprobs - inner)).astype(BF)
                    total = total + jnp.where(lanes, mm(dscores, r.k_v[layer, j]), 0.0)
                    r.dk_v[j] += mm_tn(dscores, qh)
                    r.dv_v[j] += mm_tn(probs.astype(BF), dmh)
                r.q_v[layer, j, rows, :] = (total * HD**-0.5).astype(BF)

        r.part_v[0] = r.dk_v[:, away, :].astype(BF)
        r.part_v[1] = r.dv_v[:, away, :].astype(BF)
        if layer == 0:
            spend("free_pt")
        for n in range(2):
            pt_copy(n).start()
        make_a(layer)
        middle()
        for n in range(2):
            pt_copy(n).wait()
        r.dkv_v[0] = (r.dk_v[:, mine, :] + r.other_v[0].astype(F32)).astype(BF)
        r.dkv_v[1] = (r.dv_v[:, mine, :] + r.other_v[1].astype(F32)).astype(BF)
        if layer == 1:
            credit("free_pt", sib)

    def da_chunk(layer, rows):
        @pl.loop(0, width // TILE)
        def _(n):
            here = tile_of(n)
            total = jnp.zeros((quarter, TILE), F32)
            for j in range(2):
                total = total + mm_nt(r.q_v[layer, j, rows, :], r.wa_v[layer, 0, j, here, :])
                for e in range(2):
                    total = total + mm_nt(r.dkv_v[e, j, rows, :], r.wa_v[layer, 1 + e, j, here, :])
            r.out_v[rows, here] = total.astype(BF)

    def grad_a(layer):
        @pl.loop(0, 2)
        def _(j):
            r.wa_v[layer, 0, j] = mm_tn(r.a_v[...], r.q_v[layer, j]).astype(BF)
            for e in range(2):
                r.wa_v[layer, 1 + e, j] = mm_tn(r.a_v[...], r.dkv_v[e, j]).astype(BF)
            r.wa_v[layer, 3, j] = mm_tn(r.dc_v[...], r.mixed_v[layer, j]).astype(BF)

    finish_weights(1)
    grad_f(1)
    core_f(1).start()
    y_copy.wait()
    r.yout_v[...] = (r.dx1_v[pl.ds(0, quarter), :] + r.yin_v[...].astype(F32)).astype(BF)
    end_start(r.yout_v, 1)
    after_ffn(1, 1)
    for n, (here, there) in enumerate(kept):
        local(there, here, "lh", n).start()
    attention_back(1, lambda: stage2_f(1))

    @pl.loop(0, 2)
    def _(i):
        da_chunk(1, rows_of(i))
        ar_copy(2, i).start()

    grad_a(1)
    core_a(1).start()

    @pl.loop(0, 2)
    def _(i):
        rows = rows_of(i)
        ar_copy(2, i).wait()
        grad = summed(2, rows)
        normed, inverse = normalize(r.x_v[1, rows, :].astype(F32))
        gain_grad(1, 0, i, grad, normed)
        back = normalize_back(grad, normed, inverse, r.gain_v[1, 0:1, :])
        r.g_v[rows, :] = (r.dx1_v[rows, :] + back).astype(BF)

    for n, (here, there) in enumerate(kept):
        local(there, here, "lh", n).wait()

    @pl.loop(0, 2)
    def _(i):
        rows = rows_of(i)

        @pl.loop(0, units)
        def _(n):
            cols = tile_of(n)
            du = dhidden_of(0, i, n)
            r.slope_v[rows, cols] = (du * r.slope_v[rows, cols].astype(F32)).astype(BF)

        @pl.loop(0, width // TILE)
        def _(n):
            r.out_v[rows, tile_of(n)] = up_back_tile(0, rows, n).astype(BF)

        ar_copy(3, i).start()

    stage3_f(1)
    stage2_a(1)
    finish_weights(0)
    grad_f(0)
    spend("free_cf")
    core_f(0).start()
    after_ffn(0, 3)
    attention_back(0, lambda: (stage3_a(1), stage2_f(0)))

    da_chunk(0, par_rows)
    dx_copy = remote(r.out_v.at[par_rows], r.in_v.at[0, par_rows], "ar", 0, par)
    dx_copy.start()
    da_chunk(0, own_rows)
    grad_a(0)
    spend("free_ca")
    core_a(0).start()
    dx_copy.wait()
    grad = summed(0, own_rows)
    normed, inverse = normalize(r.x_v[0, own_rows, :].astype(F32))
    gain_grad(0, 0, m, grad, normed)
    back = normalize_back(grad, normed, inverse, r.gain_v[0, 0:1, :])
    r.yin_v[...] = (r.dx1_v[own_rows, :] + back).astype(BF)
    end_start(r.yin_v, 0)

    me = c * 4 + t

    def gain_group(e, f):
        return remote(r.gain_g, r.gain_i.at[me], "ga", e * 4 + f, (e, d, f), rn=me)

    def gain_over_z(e):
        return remote(r.gain_g, r.gain_z.at[d], "gz", e, (c, e, t), rn=d)

    def others(then):
        for e in range(2):
            for f in range(4):

                @pl.when((e != c) | (f != t))
                def _():
                    then(e, f)

    others(lambda e, f: gain_group(e, f).start())

    stage3_f(0)
    stage2_a(0)

    r.gain_i[me] = r.gain_g[...]
    others(lambda e, f: gain_group(e, f).wait_send())
    others(lambda e, f: remote(r.gain_g, r.gain_i.at[0], "ga", 0, par, rn=e * 4 + f).wait_recv())
    r.gain_g[...] = jnp.sum(r.gain_i[...], axis=0)

    def other_z(then):
        @pl.loop(0, dp)
        def _(e):
            @pl.when(e != d)
            def _():
                then(e)

    other_z(lambda e: gain_over_z(e).start())
    stage3_a(0)
    r.gain_z[d] = r.gain_g[...]
    other_z(lambda e: gain_over_z(e).wait_send())
    other_z(lambda e: remote(r.gain_g, r.gain_z.at[0], "gz", 0, par, rn=e).wait_recv())
    r.dgain[...] = jnp.sum(r.gain_z[...], axis=0)
    z_wait_sends(0, "zf")
    z_wait_sends(0, "za")
    z_arrived("zf")
    z_arrived("za")
    end_sent(r.yout_v, 1)
    end_sent(r.yin_v, 0)
    end_arrived(r.yin_v)


def whole(z, inputs, cotangent, w_qkv, w_out, w_up, w_down, gains, colinfo, rowinfo):
    dma, regular = pltpu.SemaphoreType.DMA, pltpu.SemaphoreType.REGULAR
    shape = jax.ShapeDtypeStruct
    scratch = [VMEM(of(z), kind) for _, of, kind in BUFFERS]
    for _, of in PAIRS:
        scratch += [dma((of(z),)), dma((of(z),))]
    scratch += [dma((n,)) for _, n in LOCALS]
    scratch += [regular for _ in CREDITS]
    any_spec, vmem_spec = pl.BlockSpec(memory_space=ANY), pl.BlockSpec(memory_space=VMEM)
    return pl.pallas_call(
        functools.partial(kernel, z),
        out_shape=(
            shape((2, z.quarter, z.width), BF),
            shape((2, z.dp, z.rows, z.width), BF),
            shape((4, z.dp, z.rows, z.part), BF),
            shape((2, 2, z.width), F32),
            shape((z.count, z.width), F32),
            shape((z.count, z.width), BF),
            shape((z.count, 2 * z.width), BF),
            shape((z.count, 2 * z.width), BF),
        ),
        in_specs=[any_spec] * 6 + [vmem_spec] * 3,
        out_specs=[any_spec] * 3 + [vmem_spec] + [any_spec] * 4,
        scratch_shapes=scratch,
        compiler_params=pltpu.CompilerParams(
            collective_id=0, has_side_effects=True, vmem_limit_bytes=64 * 2**20
        ),
        cost_estimate=pl.CostEstimate(flops=10**11, bytes_accessed=10**8, transcendentals=0),
        name="two_layers",
    )(inputs, cotangent, w_qkv, w_out, w_up, w_down, gains, colinfo, rowinfo)


def token_info(size, length, offsets, core, count):
    patches = GRID * GRID
    tokens = jnp.arange(patches + QL, dtype=jnp.int32)
    is_patch = tokens < patches
    row, col = tokens // GRID, tokens % GRID
    live_patch = is_patch & (row < size[0]) & (col < size[1])
    live_answer = jnp.logical_not(is_patch) & (tokens - patches < length)
    window = (row + offsets[0]) // WIN * 8 + (col + offsets[1]) // WIN
    cw = jnp.where(live_patch, window, -1)
    ca = jnp.where(live_patch, -1, jnp.where(live_answer, tokens, 1 << 20))
    colinfo = jnp.stack([cw, ca, tokens] + [tokens] * 5)
    rw = jnp.where(is_patch, window, -2)
    ra = jnp.where(is_patch, -5, tokens)
    rowinfo = jnp.stack([rw, ra, tokens], axis=1)
    return colinfo, lax.dynamic_slice_in_dim(rowinfo, core * count, count, 0)


def on_device(inputs, cotangent, w_qkv, w_out, w_up, w_down, gains, image_sizes, lengths, shifts):
    core = lax.axis_index("section")
    t = lax.axis_index("tensor")
    z = Sizes()
    z.dp = lax.axis_size("dp")
    z.quarter, z.width = inputs.shape[1], inputs.shape[2]
    z.count, z.tokens = 2 * z.quarter, 4 * z.quarter
    z.part = w_qkv.shape[-1]
    z.rows = z.width // z.dp

    size = lax.dynamic_index_in_dim(image_sizes, t // 2, 0, keepdims=False)
    length = lax.dynamic_index_in_dim(lengths, t // 2, 0, keepdims=False)
    infos = [token_info(size, length, shifts * layer, core, z.count) for layer in range(2)]
    colinfo = jnp.stack([info[0] for info in infos])
    rowinfo = jnp.stack([info[1] for info in infos])

    ends, zf, za, dgain = whole(
        z, inputs, cotangent, w_qkv[0], w_out[0], w_up[0], w_down[0], gains[0], colinfo, rowinfo
    )[:4]
    f_sum = jnp.sum(zf.astype(F32), axis=1)
    a_sum = jnp.sum(za.astype(F32), axis=1)
    mine = lax.dynamic_index_in_dim(dgain, core, 0, keepdims=True)
    share = z.width // (z.dp * 4)
    slot = lax.axis_index("dp") * 4 + t
    gain_share = lax.dynamic_slice_in_dim(mine, slot * share, share, 2)
    return (
        ends[None],
        a_sum[None, :3],
        a_sum[3].T[None],
        f_sum[None, 0],
        f_sum[None, 1],
        gain_share,
    )


def solution(mesh):
    placed = (
        P("dp", "tensor", None),
        P("dp", "tensor", None),
        P("section", None, None, "tensor"),
        P("section", "tensor", None),
        P("section", None, "tensor"),
        P("section", "tensor", None),
        P("section", None, None),
        P("dp", None),
        P("dp"),
        P(),
    )
    return jax.shard_map(
        on_device,
        mesh=mesh,
        in_specs=placed,
        out_specs=(
            P("section", "dp", "tensor", None),
            P("section", None, "dp", "tensor"),
            P("section", "tensor", "dp"),
            P("section", "dp", "tensor"),
            P("section", ("tensor", "dp"), None),
            P("section", None, ("dp", "tensor")),
        ),
        check_vma=False,
    )
```

```python
import functools

import jax
import jax.numpy as jnp
from jax import lax
from jax.experimental import pallas as pl
from jax.experimental.pallas import tpu as pltpu
from jax.sharding import PartitionSpec as P

MESH = pl.DeviceIdType.MESH
VMEM = pltpu.VMEM
ANY = pl.ANY
BF = jnp.bfloat16
F32 = jnp.float32

HD = 64
WIN = 12
GRID = 24
QL = 512
PATCHES = GRID * GRID
EPS = 1e-05
OFF = -1e30
TILE = 256

NT = (((1,), (1,)), ((), ()))
TN = (((0,), (0,)), ((), ()))


def mm(a, b):
    return jnp.dot(a, b, preferred_element_type=F32)


def mm_nt(a, b):
    return lax.dot_general(a, b, NT, preferred_element_type=F32)


def mm_tn(a, b):
    return lax.dot_general(a, b, TN, preferred_element_type=F32)


def normalize(values):
    centered = values - jnp.mean(values, axis=-1, keepdims=True)
    inverse = lax.rsqrt(jnp.mean(centered * centered, axis=-1, keepdims=True) + EPS)
    return centered * inverse, inverse


def normalize_back(grad, normed, inverse, gain):
    t = grad * gain
    return inverse * (
        t
        - jnp.mean(t, axis=-1, keepdims=True)
        - normed * jnp.mean(t * normed, axis=-1, keepdims=True)
    )


def head_lanes(rows, h):
    lanes = lax.broadcasted_iota(jnp.int32, (rows, 3 * HD), 1)
    return (lanes >= h * HD) & (lanes < h * HD + HD)


def column_of(block, n):
    lanes = lax.broadcasted_iota(jnp.int32, block.shape, 1)
    return jnp.sum(jnp.where(lanes == n, block, 0.0), axis=-1, keepdims=True)


def tile_of(n, size=TILE):
    return pl.ds(pl.multiple_of(n * size, size), size)


BUFFERS = (
    ("x_v", lambda z: (2, z.count, z.width), BF),
    ("g_v", lambda z: (z.count, z.width), BF),
    ("gain_v", lambda z: (2, 2, z.width), F32),
    ("wa_v", lambda z: (2, 4, 2, z.width, z.part), BF),
    ("wf_v", lambda z: (2, 2, 2, z.width, z.width), BF),
    ("wo_v", lambda z: (2, 4, z.part, z.width), BF),
    ("q_v", lambda z: (2, 2, z.count, z.part), BF),
    ("k_v", lambda z: (2, 2, z.tokens, z.part), BF),
    ("v_v", lambda z: (2, 2, z.tokens, z.part), BF),
    ("mixed_v", lambda z: (2, 2, z.count, z.part), BF),
    ("mixr_v", lambda z: (2, z.count, z.part), BF),
    ("lse_v", lambda z: (2, z.count, 128), F32),
    ("x1_v", lambda z: (z.count, z.width), F32),
    ("b_v", lambda z: (z.count, z.width), BF),
    ("acted_v", lambda z: (z.count, 2 * z.width), BF),
    ("slope_v", lambda z: (z.count, 2 * z.width), BF),
    ("a_v", lambda z: (z.count, z.width), BF),
    ("out_v", lambda z: (z.count, z.width), BF),
    ("in_v", lambda z: (2, z.count, z.width), BF),
    ("yout_v", lambda z: (z.quarter, z.width), BF),
    ("yin_v", lambda z: (z.quarter, z.width), BF),
    ("yown_v", lambda z: (z.quarter, z.width), BF),
    ("bias_v", lambda z: (z.count, z.tokens), F32),
    ("dkv_t", lambda z: (2, 2, z.part, z.tokens), F32),
    ("dmix_v", lambda z: (2, z.count, z.part), BF),
    ("dkv_v", lambda z: (2, 2, z.tokens, z.part), BF),
    ("other_v", lambda z: (2, 2, z.count, z.part), BF),
    ("crecv_f", lambda z: (2, z.width, z.width), BF),
    ("yrecv_f", lambda z: (z.width, z.width), BF),
    ("zsend_f", lambda z: (z.dp, z.rows, z.width), BF),
    ("crecv_a", lambda z: (2, 2, z.width, z.part), BF),
    ("yrecv_a", lambda z: (2, z.width, z.part), BF),
    ("zsend_a", lambda z: (2, z.dp, z.rows, z.part), BF),
    ("gain_g", lambda z: (2, 2, z.width), F32),
    ("gain_i", lambda z: (8, 2, 2, z.width), F32),
    ("gain_z", lambda z: (z.dp, 2, 2, z.width), F32),
)

PAIRS = (
    ("xs", lambda z: 2),
    ("cs", lambda z: 2),
    ("gs", lambda z: 1),
    ("wsib", lambda z: 6),
    ("wy", lambda z: 12),
    ("wz", lambda z: 6),
    ("wf", lambda z: 6),
    ("wg", lambda z: 6),
    ("wo", lambda z: 16),
    ("kv", lambda z: 16),
    ("mix", lambda z: 4),
    ("ar", lambda z: 4),
    ("yy", lambda z: 1),
    ("pt", lambda z: 2),
    ("cf", lambda z: 2),
    ("ca", lambda z: 2),
    ("yf", lambda z: 4),
    ("ya", lambda z: 4),
    ("zf", lambda z: 2 * z.dp),
    ("za", lambda z: 4 * z.dp),
    ("en", lambda z: 4),
    ("ga", lambda z: 8),
    ("gz", lambda z: z.dp),
)
LOCALS = (("lw", 8), ("lx", 4), ("lh", 4), ("lz", 2), ("le", 2))
CREDITS = ("free_pt", "free_cf", "free_ca", "free_yf", "free_ya")


class Sizes:
    pass


def kernel(z, *refs):
    names = (
        ["inputs", "cotangent", "w_qkv", "w_out", "w_up", "w_down", "gains", "sizes", "lengths", "shifts"]
        + ["ends", "zf_o", "za_o", "dgain", "h_x1", "h_b", "h_acted", "h_slope"]
        + [n for n, _, _ in BUFFERS]
        + [n + e for n, _ in PAIRS for e in ("_s", "_r")]
        + [n for n, _ in LOCALS]
        + list(CREDITS)
    )
    r = Sizes()
    for name, ref in zip(names, refs, strict=True):
        setattr(r, name, ref)

    c, d, t = lax.axis_index("section"), lax.axis_index("dp"), lax.axis_index("tensor")
    m, p = lax.rem(t, 2), t // 2
    px, ax = t + 1 - 2 * m, lax.rem(t + 2, 4)
    dx = ax + 1 - 2 * m
    sib, par, acr, dia = (1 - c, d, t), (c, d, px), (c, d, ax), (c, d, dx)
    quarter, count, width, dp = z.quarter, z.count, z.width, z.dp

    def remote(src, dst, name, n, device, rn=None):
        return pltpu.make_async_remote_copy(
            src_ref=src,
            dst_ref=dst,
            send_sem=getattr(r, name + "_s").at[n],
            recv_sem=getattr(r, name + "_r").at[n if rn is None else rn],
            device_id=device,
            device_id_type=MESH,
        )

    def local(src, dst, name, n):
        return pltpu.make_async_copy(src, dst, getattr(r, name).at[n])

    def rows_of(i):
        return pl.ds(pl.multiple_of(i * quarter, 16), quarter)

    mine = pl.ds(pl.multiple_of(c * count, 16), count)
    away = pl.ds(pl.multiple_of((1 - c) * count, 16), count)

    def own_weights(n):
        src = (r.w_qkv, r.w_up, r.w_down, r.w_out, r.gains)[n]
        dst = (
            lambda: r.wa_v.at[c, pl.ds(0, 3), 0],
            lambda: r.wf_v.at[c, 0, 0],
            lambda: r.wf_v.at[c, 1, 0],
            lambda: r.wo_v.at[c, t],
            lambda: r.gain_v.at[c],
        )[n]
        return local(src, dst(), "lw", n)

    for n in range(5):
        own_weights(n).start()

    barrier = pltpu.get_barrier_semaphore()

    def hello(device):
        pl.semaphore_signal(barrier, inc=1, device_id=device, device_id_type=MESH)

    for e in range(4):
        @pl.when(e != t)
        def _():
            hello((c, d, e))

        hello((1 - c, d, e))

    @pl.loop(0, dp)
    def _(e):
        @pl.when(e != d)
        def _():
            hello((c, e, t))
            hello((1 - c, e, t))

    pl.semaphore_wait(barrier, 7 + 2 * (dp - 1))

    home = c == p

    def spread(src, dst, name, base):
        here, there = rows_of(m), rows_of(1 - m)

        def kept():
            return local(src.at[p], dst.at[here], "lx", base)

        def from_home():
            return remote(src.at[p], dst.at[here], name, 0, par)

        def to_away():
            return remote(src.at[1 - p], dst.at[here], name, 1, acr)

        def from_away():
            return remote(dst.at[here], dst.at[here], name, 0, par)

        def start():
            @pl.when(home)
            def _():
                to_away().start()
                from_home().start()
                kept().start()

        def passed():
            @pl.when(jnp.logical_not(home))
            def _():
                to_away().wait_recv()
                from_away().start()

        def wait():
            @pl.when(home)
            def _():
                to_away().wait_send()
                from_home().wait_send()
                kept().wait()

            @pl.when(jnp.logical_not(home))
            def _():
                from_away().wait_send()

            remote(dst.at[there], dst.at[there], name, 0, par).wait_recv()

        return start, passed, wait

    x_start, x_pass, x_wait = spread(r.inputs, r.x_v.at[0], "xs", 0)
    c_start, c_pass, c_wait = spread(r.cotangent, r.g_v, "cs", 1)
    x_start()

    gain_copy = remote(r.gains, r.gain_v.at[c], "gs", 0, sib)
    gain_copy.start()

    sources = (r.w_qkv, r.w_up, r.w_down)

    def slot(layer, piece, j):
        if piece == 0:
            return r.wa_v.at[layer, pl.ds(0, 3), j]
        return r.wf_v.at[layer, piece - 1, j]

    def to_sib(layer, piece):
        return remote(sources[piece], slot(layer, piece, 0), "wsib", layer * 3 + piece, sib)

    half = lax.rem(d, 2)
    zpar = (c, d + 1 - 2 * half, t)

    def sub(ref, piece, e, core):
        rows = pl.ds(pl.multiple_of((2 * e + core) * (width // 4), 16), width // 4)
        return ref.at[:, rows] if piece == 0 else ref.at[rows]

    def to_acr(layer, piece, core):
        return remote(
            sub(sources[piece], piece, half, core),
            sub(slot(layer, piece, 1), piece, half, core),
            "wy",
            (layer * 3 + piece) * 2 + core,
            (core, d, ax),
            rn=layer * 3 + piece,
        )

    def far_copy(layer, piece, e, name, device):
        here = sub(slot(layer, piece, 1), piece, e, c)
        return remote(here, here, name, layer * 3 + piece, device)

    def owner_starts(layer, pieces):
        @pl.when(c == layer)
        def _():
            for piece in pieces:
                for core in range(2):
                    to_acr(layer, piece, core).start()

    def sib_starts(pieces):
        for piece in pieces:
            for layer in range(2):

                @pl.when(c == layer)
                def _():
                    to_sib(layer, piece).start()

    def need_own(layer, piece):
        @pl.when(c == layer)
        def _():
            own_weights(piece).wait()

        @pl.when(c != layer)
        def _():
            to_sib(layer, piece).wait_recv()

    def step_y(layer, piece):
        far_copy(layer, piece, half, "wy", sib).wait_recv()
        far_copy(layer, piece, half, "wz", zpar).start()
        far_copy(layer, piece, half, "wf", sib).start()

    def step_z(layer, piece):
        far_copy(layer, piece, 1 - half, "wz", zpar).wait_recv()
        far_copy(layer, piece, 1 - half, "wg", sib).start()

    def need_far(layer, piece):
        far_copy(layer, piece, half, "wf", sib).wait_recv()
        far_copy(layer, piece, 1 - half, "wg", sib).wait_recv()

    def wo_copy(layer, e, device, n):
        here = r.wo_v.at[layer, e]
        return remote(r.w_out, here, "wo", n, device, rn=layer * 4 + e)

    def wo_start(layer):
        @pl.when(c == layer)
        def _():
            for n, device in enumerate((par, acr, dia, sib)):
                wo_copy(layer, t, device, layer * 8 + n).start()

    def wo_pass(layer, n):
        e = (px, ax, dx)[n]
        here = r.wo_v.at[layer, e]
        return remote(here, here, "wo", layer * 8 + 4 + n, sib, rn=layer * 4 + e)

    def step_wo(layer):
        @pl.when(c == layer)
        def _():
            own_weights(3).wait()
            for n in range(3):
                e = (px, ax, dx)[n]
                wo_copy(layer, e, par, 0).wait_recv()
                wo_pass(layer, n).start()

    def need_wo(layer):
        @pl.when(c != layer)
        def _():
            for e in (t, px, ax, dx):
                wo_copy(layer, e, par, 0).wait_recv()

    def finish_weights(layer):
        for piece in range(3):
            far_copy(layer, piece, half, "wz", zpar).wait_send()
            far_copy(layer, piece, half, "wf", sib).wait_send()
            far_copy(layer, piece, 1 - half, "wg", sib).wait_send()

        @pl.when(c == layer)
        def _():
            for piece in range(3):
                to_sib(layer, piece).wait_send()
                for core in range(2):
                    to_acr(layer, piece, core).wait_send()
            for n, device in enumerate((par, acr, dia, sib)):
                wo_copy(layer, t, device, layer * 8 + n).wait_send()
            for n in range(3):
                wo_pass(layer, n).wait_send()

    sib_starts((0,))
    own_weights(4).wait()
    gain_copy.wait()

    def kv_copy(layer, i, j, n):
        rows = pl.ds(pl.multiple_of(c * count + i * quarter, 16), quarter)
        here = (r.k_v, r.v_v)[n].at[layer, j, rows]
        return remote(here, here, "kv", layer * 8 + i * 4 + j * 2 + n, sib)

    def mix_copy(layer, i, j):
        return remote(
            r.mixed_v.at[layer, j, rows_of(i)], r.mixr_v.at[j, rows_of(i)], "mix", i * 2 + j, par
        )

    def fill_bias(layer):
        high, wide, length = r.sizes[p, 0], r.sizes[p, 1], r.lengths[p]

        def windows(tokens):
            row = (tokens * 2731) >> 16
            col = tokens - row * GRID
            down, right = row + r.shifts[0] * layer, col + r.shifts[1] * layer
            return row, col, ((down * 5462) >> 16) * 8 + ((right * 5462) >> 16)

        cj = lax.broadcasted_iota(jnp.int32, (1, z.tokens), 1)
        row, col, window = windows(cj)
        is_patch = cj < PATCHES
        live_patch = is_patch & (row < high) & (col < wide)
        live_answer = jnp.logical_not(is_patch) & (cj - PATCHES < length)
        cw = jnp.where(live_patch, window, -1)
        ca = jnp.where(live_patch, -1, jnp.where(live_answer, cj, 1 << 20))
        ri = lax.broadcasted_iota(jnp.int32, (count, 1), 0) + c * count
        _, _, window = windows(ri)
        rw = jnp.where(ri < PATCHES, window, -2)
        ra = jnp.where(ri < PATCHES, -5, ri)
        allowed = (cw == rw) | (ca < ra) | (cj == ri)
        r.bias_v[...] = jnp.where(allowed, 0.0, OFF)

    def make_a(layer, rows):
        normed, _ = normalize(r.x_v[layer, rows, :].astype(F32))
        r.a_v[rows, :] = (normed * r.gain_v[layer, 0:1, :]).astype(BF)

    def project_qkv(layer, i, j):
        rows = rows_of(i)
        there = pl.ds(pl.multiple_of(c * count + i * quarter, 16), quarter)
        a = r.a_v[rows, :]
        r.k_v[layer, j, there, :] = mm(a, r.wa_v[layer, 1, j]).astype(BF)
        kv_copy(layer, i, j, 0).start()
        r.v_v[layer, j, there, :] = mm(a, r.wa_v[layer, 2, j]).astype(BF)
        kv_copy(layer, i, j, 1).start()
        r.q_v[layer, j, rows, :] = (mm(a, r.wa_v[layer, 0, j]) * HD**-0.5).astype(BF)

    near_keys = PATCHES
    views = (
        lambda i: c == 0,
        lambda i: (c == 1) & (i == 0),
        lambda i: (c == 1) & (i == 1),
    )
    seen = (near_keys, 3 * quarter, z.tokens)

    def attend(layer, i, j, keys):
        rows = rows_of(i)
        lane = lax.broadcasted_iota(jnp.int32, (quarter, 128), 1)
        stats = r.lse_v[layer, rows, :]
        total = jnp.zeros((quarter, z.part), F32)
        some = pl.ds(0, keys)
        scores = []
        for h in range(3):
            lanes = head_lanes(quarter, h)
            qh = jnp.where(lanes, r.q_v[layer, j, rows, :], jnp.zeros((), BF))
            scores.append(mm_nt(qh, r.k_v[layer, j, some, :]) + r.bias_v[rows, some])
        for h in range(3):
            top = jnp.max(scores[h], axis=-1, keepdims=True)
            expos = jnp.exp(scores[h] - top)
            norm = jnp.sum(expos, axis=-1, keepdims=True)
            stats = jnp.where(lane == j * 3 + h, top + jnp.log(norm), stats)
            part = mm(expos.astype(BF), r.v_v[layer, j, some, :]) * (1.0 / norm)
            total = total + jnp.where(head_lanes(quarter, h), part, 0.0)
        r.lse_v[layer, rows, :] = stats
        r.mixed_v[layer, j, rows, :] = total.astype(BF)

    def attention(layer, between):
        fill_bias(layer)
        r.lse_v[layer] = jnp.zeros((count, 128), F32)

        @pl.loop(0, 2)
        def _(j):
            @pl.loop(0, 2)
            def _(i):
                between(j, i)

                @pl.when(i == 0)
                def _():
                    for e in range(2):
                        for n in range(2):
                            kv_copy(layer, e, j, n).wait()

                for when, keys in zip(views, seen):
                    pl.when(when(i))(functools.partial(attend, layer, i, j, keys))
                mix_copy(layer, i, j).start()

    def at(j, i, there, do):
        pl.when((j == there[0]) & (i == there[1]))(do)

    def project(layer, i):
        rows = rows_of(i)
        total = r.x_v[layer, rows, :].astype(F32)
        total = total + mm(r.mixed_v[layer, 0, rows, :], r.wo_v[layer, t])
        total = total + mm(r.mixed_v[layer, 1, rows, :], r.wo_v[layer, ax])
        for j in range(2):
            mix_copy(layer, i, j).wait()
        total = total + mm(r.mixr_v[0, rows, :], r.wo_v[layer, px])
        total = total + mm(r.mixr_v[1, rows, :], r.wo_v[layer, dx])
        r.x1_v[rows, :] = total
        normed, _ = normalize(total)
        r.b_v[rows, :] = (normed * r.gain_v[layer, 1:2, :]).astype(BF)

    def ar_copy(n, i):
        return remote(
            r.out_v.at[rows_of(i)], r.in_v.at[n % 2, rows_of(i)], "ar", (n % 2) * 2 + i, par
        )

    def summed(n, rows):
        return r.out_v[rows, :].astype(F32) + r.in_v[n % 2, rows, :].astype(F32)

    def hidden_of(layer, i, n):
        j, here = n // (width // TILE), tile_of(lax.rem(n, width // TILE))
        hidden = mm(r.b_v[rows_of(i), :], r.wf_v[layer, 0, j, :, here])
        cdf = 0.5 + 0.5 * lax.erf(hidden * 0.5**0.5)
        bell = jnp.exp(hidden * hidden * -0.5) * 0.3989422804014327
        return hidden * cdf, cdf + hidden * bell

    def down_tile(layer, rows, n):
        here = tile_of(n)
        return mm(r.acted_v[rows, pl.ds(0, width)], r.wf_v[layer, 1, 0, :, here]) + mm(
            r.acted_v[rows, pl.ds(width, width)], r.wf_v[layer, 1, 1, :, here]
        )

    def dhidden_of(layer, i, n):
        j, here = n // (width // TILE), tile_of(lax.rem(n, width // TILE))
        return mm_nt(r.g_v[rows_of(i), :], r.wf_v[layer, 1, j, here, :])

    def up_back_tile(layer, rows, n):
        here = tile_of(n)
        return mm_nt(r.slope_v[rows, pl.ds(0, width)], r.wf_v[layer, 0, 0, here, :]) + mm_nt(
            r.slope_v[rows, pl.ds(width, width)], r.wf_v[layer, 0, 1, here, :]
        )

    units = 2 * width // TILE

    x_pass()
    owner_starts(0, (0,))
    sib_starts((1, 2))
    x_wait()
    owner_starts(0, (1, 2))
    wo_start(0)
    need_own(0, 0)

    @pl.loop(0, 2)
    def _(i):
        make_a(0, rows_of(i))
        project_qkv(0, i, 0)

    step_y(0, 0)

    def between_0(j, i):
        @functools.partial(at, j, i, (0, 1))
        def _():
            step_z(0, 0)
            need_far(0, 0)
            project_qkv(0, 0, 1)
            project_qkv(0, 1, 1)

        @functools.partial(at, j, i, (1, 0))
        def _():
            step_y(0, 1)
            step_wo(0)

        @functools.partial(at, j, i, (1, 1))
        def _():
            step_z(0, 1)
            step_y(0, 2)
            owner_starts(1, (0,))

    attention(0, between_0)
    step_z(0, 2)
    need_wo(0)
    for piece in (1, 2):
        need_own(0, piece)
        need_far(0, piece)

    @pl.loop(0, 2)
    def _(i):
        rows = rows_of(i)
        project(0, i)

        @pl.loop(0, units)
        def _(n):
            acted, slope = hidden_of(0, i, n)
            r.acted_v[rows, tile_of(n)] = acted.astype(BF)
            r.slope_v[rows, tile_of(n)] = slope.astype(BF)

        @pl.loop(0, width // TILE)
        def _(n):
            r.out_v[rows, tile_of(n)] = down_tile(0, rows, n).astype(BF)

        ar_copy(0, i).start()

    kept = [
        (r.x1_v, r.h_x1),
        (r.b_v, r.h_b),
        (r.acted_v, r.h_acted),
        (r.slope_v, r.h_slope),
    ]
    for n, (here, there) in enumerate(kept):
        local(here, there, "lh", n).start()
    step_y(1, 0)
    owner_starts(1, (1, 2))
    wo_start(1)
    step_z(1, 0)
    need_own(1, 0)
    need_far(1, 0)

    @pl.loop(0, 2)
    def _(i):
        rows = rows_of(i)
        ar_copy(0, i).wait()
        r.x_v[1, rows, :] = (r.x1_v[rows, :] + summed(0, rows)).astype(BF)
        make_a(1, rows)
        for j in range(2):
            project_qkv(1, i, j)

    c_start()

    def between_1(j, i):
        @functools.partial(at, j, i, (0, 0))
        def _():
            step_y(1, 1)
            step_wo(1)

        @functools.partial(at, j, i, (0, 1))
        def _():
            step_z(1, 1)
            step_y(1, 2)

        @functools.partial(at, j, i, (1, 0))
        def _():
            step_z(1, 2)
            c_pass()

    attention(1, between_1)
    need_wo(1)
    for piece in (1, 2):
        need_own(1, piece)
        need_far(1, piece)
    c_wait()
    for n, (here, there) in enumerate(kept):
        local(here, there, "lh", n).wait()

    @pl.loop(0, 2)
    def _(i):
        rows = rows_of(i)
        project(1, i)

        @pl.loop(0, units)
        def _(n):
            acted, slope = hidden_of(1, i, n)
            r.acted_v[rows, tile_of(n)] = acted.astype(BF)
            r.slope_v[rows, tile_of(n)] = (dhidden_of(1, i, n) * slope).astype(BF)

        @pl.loop(0, width // TILE)
        def _(n):
            r.out_v[rows, tile_of(n)] = up_back_tile(1, rows, n).astype(BF)

        ar_copy(1, i).start()

    own_rows, par_rows = rows_of(m), rows_of(1 - m)

    @pl.loop(0, width // TILE)
    def _(n):
        r.yout_v[:, tile_of(n)] = down_tile(1, par_rows, n).astype(BF)

    y_copy = remote(r.yout_v, r.yin_v, "yy", 0, par)
    y_copy.start()

    @pl.loop(0, width // TILE)
    def _(n):
        cols = tile_of(n)
        r.yown_v[:, cols] = down_tile(1, own_rows, n).astype(BF)

    def end_copies(src, section):
        stays = (c == section) & (p == section)

        def far():
            return remote(src, r.ends.at[p], "en", section * 2, (section, d, 2 * c + m), rn=p)

        return stays, far, lambda: local(src, r.ends.at[p], "le", section)

    def end_start(src, section):
        stays, far, near = end_copies(src, section)
        pl.when(stays)(lambda: near().start())
        pl.when(jnp.logical_not(stays))(lambda: far().start())

    def end_sent(src, section):
        stays, far, near = end_copies(src, section)
        pl.when(stays)(lambda: near().wait())
        pl.when(jnp.logical_not(stays))(lambda: far().wait_send())

    def end_arrived(src):
        for i in range(2):
            came = jnp.logical_not((c == p) & (i == c))

            @pl.when(came)
            def _():
                remote(src, r.ends.at[i], "en", i, par).wait_recv()

    def grad_f(layer, j):
        @pl.loop(0, width // TILE)
        def _(n):
            here = tile_of(n)
            cols = pl.ds(pl.multiple_of(n * TILE, TILE) + j * width, TILE)
            r.wf_v[layer, 0, j, :, here] = mm_tn(r.b_v[...], r.slope_v[:, cols]).astype(BF)
            r.wf_v[layer, 1, j, here, :] = mm_tn(r.acted_v[:, cols], r.g_v[...]).astype(BF)

    def core_f(layer, j):
        return remote(r.wf_v.at[layer, 1 - c, j], r.crecv_f.at[j], "cf", j, sib)

    def core_a(layer, j):
        return remote(
            r.wa_v.at[layer, pl.ds(2 * (1 - c), 2), j], r.crecv_a.at[:, j], "ca", j, sib
        )

    STEP = width // 4

    def y_f(n):
        rows = tile_of(n, STEP)
        return remote(r.crecv_f.at[1, rows], r.yrecv_f.at[rows], "yf", n, acr)

    def y_a(n):
        rows = tile_of(n, STEP)
        return remote(r.crecv_a.at[:, 1, rows], r.yrecv_a.at[:, rows], "ya", n, acr)

    def credit(name, device):
        pl.semaphore_signal(getattr(r, name), inc=1, device_id=device, device_id_type=MESH)

    def spend(name):
        pl.semaphore_wait(getattr(r, name), 1)

    def z_copies(layer, which, item, e):
        zsend = r.zsend_f if which == "zf" else r.zsend_a.at[item]
        land = r.zf_o.at[c, d] if which == "zf" else r.za_o.at[2 * c + item, d]
        index = e if which == "zf" else item * dp + e
        return remote(zsend.at[e], land, which, index, (layer, e, t), rn=zr(which, c, item, d))

    def zr(which, core, item, e):
        return core * dp + e if which == "zf" else (2 * core + item) * dp + e

    group = 1 if z.rows % 16 == 0 else 2

    def stage2_f(layer):
        core_f(layer, 1).wait()
        if layer == 0:
            spend("free_yf")

        @pl.loop(0, 4)
        def _(n):
            rows = tile_of(n, STEP)
            r.crecv_f[1, rows, :] = (
                r.crecv_f[1, rows, :].astype(F32) + r.wf_v[layer, c, 1, rows, :].astype(F32)
            ).astype(BF)
            y_f(n).start()

    def stage2_a(layer):
        core_a(layer, 1).wait()
        if layer == 0:
            spend("free_ya")

        @pl.loop(0, 4)
        def _(n):
            rows = tile_of(n, STEP)
            for item in range(2):
                r.crecv_a[item, 1, rows, :] = (
                    r.crecv_a[item, 1, rows, :].astype(F32)
                    + r.wa_v[layer, 2 * c + item, 1, rows, :].astype(F32)
                ).astype(BF)
            y_a(n).start()

    def z_wait_sends(layer, which):
        for item in range(1 if which == "zf" else 2):

            @pl.loop(0, dp)
            def _(e):
                @pl.when((c != layer) | (e != d))
                def _():
                    z_copies(layer, which, item, e).wait_send()

    def z_near(which, item):
        zsend = r.zsend_f if which == "zf" else r.zsend_a.at[item]
        land = r.zf_o.at[c, d] if which == "zf" else r.za_o.at[2 * c + item, d]
        return local(zsend.at[d], land, "lz", item)

    def z_send(layer, which, n):
        for item in range(1 if which == "zf" else 2):

            @pl.loop(n * (dp // 4), (n + 1) * (dp // 4))
            def _(e):
                @pl.when((c != layer) | (e != d))
                def _():
                    z_copies(layer, which, item, e).start()

                @pl.when((c == layer) & (e == d))
                def _():
                    near = z_near(which, item)
                    near.start()
                    near.wait()

    def z_arrived(which):
        for core in range(2):
            for item in range(1 if which == "zf" else 2):

                @pl.loop(0, dp)
                def _(e):
                    @pl.when((core != c) | (e != d))
                    def _():
                        z_arrival(which, core, item, e).wait_recv()

    def z_arrival(which, core, item, e):
        zsend = r.zsend_f if which == "zf" else r.zsend_a.at[item]
        land = r.zf_o.at[core, e] if which == "zf" else r.za_o.at[2 * core + item, e]
        return remote(zsend.at[0], land, which, 0, par, rn=zr(which, core, item, e))

    def stage3_f(layer, n):
        if n == 0:
            core_f(layer, 0).wait()
            if layer == 0:
                z_wait_sends(1, "zf")
        y_f(n).wait()

        @pl.loop(0, dp // 4 // group)
        def _(e):
            first = n * (dp // 4) + e * group
            rows = pl.ds(pl.multiple_of(first * z.rows, group * z.rows), group * z.rows)
            total = (
                r.crecv_f[0, rows, :].astype(F32)
                + r.wf_v[layer, c, 0, rows, :].astype(F32)
                + r.yrecv_f[rows, :].astype(F32)
            )
            r.zsend_f[pl.ds(first, group)] = total.reshape(group, z.rows, width).astype(BF)

        if layer == 1 and n == 3:
            credit("free_cf", sib)
            credit("free_yf", acr)
        z_send(layer, "zf", n)

    def stage3_a(layer, n):
        if n == 0:
            core_a(layer, 0).wait()
            if layer == 0:
                z_wait_sends(1, "za")
        y_a(n).wait()
        for item in range(2):

            @pl.loop(0, dp // 4 // group)
            def _(e):
                first = n * (dp // 4) + e * group
                rows = pl.ds(pl.multiple_of(first * z.rows, group * z.rows), group * z.rows)
                total = (
                    r.crecv_a[item, 0, rows, :].astype(F32)
                    + r.wa_v[layer, 2 * c + item, 0, rows, :].astype(F32)
                    + r.yrecv_a[item, rows, :].astype(F32)
                )
                r.zsend_a[item, pl.ds(first, group)] = total.reshape(
                    group, z.rows, z.part
                ).astype(BF)

        if layer == 1 and n == 3:
            credit("free_ca", sib)
            credit("free_ya", acr)
        z_send(layer, "za", n)

    r.gain_g[...] = jnp.zeros_like(r.gain_g)

    def gain_grad(layer, n, i, grad, normed):
        share = jnp.where(i == m, 1.0, 0.0)
        r.gain_g[layer, n : n + 1, :] += share * jnp.sum(grad * normed, axis=0, keepdims=True)

    def after_ffn(layer, n):
        @pl.loop(0, 2)
        def _(i):
            rows = rows_of(i)
            ar_copy(n, i).wait()
            grad = summed(n, rows)
            normed, inverse = normalize(r.x1_v[rows, :])
            gain_grad(layer, 1, i, grad, normed)
            back = normalize_back(grad, normed, inverse, r.gain_v[layer, 1:2, :])
            dx1 = r.g_v[rows, :].astype(F32) + back
            dc = dx1.astype(BF)
            r.x1_v[rows, :] = dx1
            r.dmix_v[0, rows, :] = mm_nt(dc, r.wo_v[layer, t]).astype(BF)
            r.dmix_v[1, rows, :] = mm_nt(dc, r.wo_v[layer, ax]).astype(BF)

    def pt_copy(n):
        return remote(r.dkv_v.at[n, :, away], r.other_v.at[n], "pt", n, sib)

    def attend_back(layer, j, keys):
        some = pl.ds(0, keys)
        zero = jnp.zeros((), BF)
        q, dmix = r.q_v[layer, j], r.dmix_v[j]
        q_t, dmix_t = q.T, dmix.T
        k, v = r.k_v[layer, j, some, :], r.v_v[layer, j, some, :]
        product = dmix.astype(F32) * r.mixed_v[layer, j].astype(F32)
        total = jnp.zeros((count, z.part), F32)
        for h in range(3):
            lanes = head_lanes(count, h)
            heads = pl.ds(h * HD, HD)
            scores = mm_nt(jnp.where(lanes, q, zero), k) + r.bias_v[:, some]
            dprobs = mm_nt(jnp.where(lanes, dmix, zero), v)
            probs = jnp.exp(scores - column_of(r.lse_v[layer], j * 3 + h))
            inner = jnp.sum(jnp.where(lanes, product, 0.0), axis=-1, keepdims=True)
            r.dkv_t[1, j, heads, some] = mm(dmix_t[h * HD : h * HD + HD], probs.astype(BF))
            dscores = (probs * (dprobs - inner)).astype(BF)
            total = total + jnp.where(lanes, mm(dscores, k), 0.0)
            r.dkv_t[0, j, heads, some] = mm(q_t[h * HD : h * HD + HD], dscores)
        r.q_v[layer, j] = (total * HD**-0.5).astype(BF)

    def attention_back(layer, between):
        fill_bias(layer)
        r.dkv_t[...] = jnp.zeros_like(r.dkv_t)

        @pl.loop(0, 2)
        def _(j):
            between(j)
            pl.when(c == 0)(functools.partial(attend_back, layer, j, near_keys))
            pl.when(c == 1)(functools.partial(attend_back, layer, j, z.tokens))

        for n in range(2):
            for j in range(2):
                r.dkv_v[n, j] = r.dkv_t[n, j].T.astype(BF)
        if layer == 0:
            spend("free_pt")
        for n in range(2):
            pt_copy(n).start()
        for i in range(2):
            make_a(layer, rows_of(i))
        between(2)
        for n in range(2):
            pt_copy(n).wait()
            r.dkv_v[n, :, mine, :] = (
                r.dkv_v[n, :, mine, :].astype(F32) + r.other_v[n].astype(F32)
            ).astype(BF)
        if layer == 1:
            credit("free_pt", sib)

    def in_all(rows):
        return pl.ds(pl.multiple_of(c * count + rows.start, 16), quarter)

    def da_chunk(layer, rows):
        @pl.loop(0, width // TILE)
        def _(n):
            here = tile_of(n)
            total = jnp.zeros((quarter, TILE), F32)
            for j in range(2):
                total = total + mm_nt(r.q_v[layer, j, rows, :], r.wa_v[layer, 0, j, here, :])
                for e in range(2):
                    total = total + mm_nt(
                        r.dkv_v[e, j, in_all(rows), :], r.wa_v[layer, 1 + e, j, here, :]
                    )
            r.out_v[rows, here] = total.astype(BF)

    def grad_a(layer):
        @pl.loop(0, 2)
        def _(n):
            j = 1 - n
            r.wa_v[layer, 0, j] = mm_tn(r.a_v[...], r.q_v[layer, j]).astype(BF)
            for e in range(2):
                r.wa_v[layer, 1 + e, j] = mm_tn(r.a_v[...], r.dkv_v[e, j, mine, :]).astype(BF)
            r.wa_v[layer, 3, j] = mm_tn(r.x1_v[...].astype(BF), r.mixed_v[layer, j]).astype(BF)
            core_a(layer, j).start()

    finish_weights(1)
    for j in (1, 0):
        grad_f(1, j)
        core_f(1, j).start()
    y_copy.wait()
    r.yown_v[...] = (
        r.x1_v[own_rows, :] + r.yown_v[...].astype(F32) + r.yin_v[...].astype(F32)
    ).astype(BF)
    end_start(r.yown_v, 1)
    stage2_f(1)
    after_ffn(1, 1)
    for n, (here, there) in enumerate(kept[1:]):
        local(there, here, "lh", n).start()

    def between_back_1(j):
        if isinstance(j, int):
            stage3_f(1, 1)
        else:
            pl.when(j == 1)(functools.partial(stage3_f, 1, 0))

    attention_back(1, between_back_1)

    @pl.loop(0, 2)
    def _(i):
        da_chunk(1, rows_of(i))
        ar_copy(2, i).start()

    stage3_f(1, 2)
    grad_a(1)
    stage3_f(1, 3)
    stage2_a(1)
    for n, (here, there) in enumerate(kept[1:]):
        local(there, here, "lh", n).wait()

    @pl.loop(0, 2)
    def _(i):
        rows = rows_of(i)
        ar_copy(2, i).wait()
        grad = summed(2, rows)
        normed, inverse = normalize(r.x_v[1, rows, :].astype(F32))
        gain_grad(1, 0, i, grad, normed)
        back = normalize_back(grad, normed, inverse, r.gain_v[1, 0:1, :])
        r.g_v[rows, :] = (r.x1_v[rows, :] + back).astype(BF)

        @pl.loop(0, units)
        def _(n):
            cols = tile_of(n)
            du = dhidden_of(0, i, n)
            r.slope_v[rows, cols] = (du * r.slope_v[rows, cols].astype(F32)).astype(BF)

        @pl.loop(0, width // TILE)
        def _(n):
            r.out_v[rows, tile_of(n)] = up_back_tile(0, rows, n).astype(BF)

        ar_copy(3, i).start()

    local(r.h_x1, r.x1_v, "lh", 3).start()
    finish_weights(0)
    spend("free_cf")
    for j in (1, 0):
        grad_f(0, j)
        core_f(0, j).start()
    stage3_a(1, 0)
    stage2_f(0)
    for n in range(1, 4):
        stage3_a(1, n)
    local(r.h_x1, r.x1_v, "lh", 3).wait()
    after_ffn(0, 3)

    def between_back_0(j):
        if isinstance(j, int):
            stage3_f(0, 1)
        else:
            pl.when(j == 1)(functools.partial(stage3_f, 0, 0))

    attention_back(0, between_back_0)
    da_chunk(0, par_rows)
    dx_copy = remote(r.out_v.at[par_rows], r.in_v.at[0, par_rows], "ar", 0, par)
    dx_copy.start()
    da_chunk(0, own_rows)
    spend("free_ca")
    grad_a(0)
    stage2_a(0)
    stage3_f(0, 2)
    dx_copy.wait()
    grad = summed(0, own_rows)
    normed, inverse = normalize(r.x_v[0, own_rows, :].astype(F32))
    gain_grad(0, 0, m, grad, normed)
    back = normalize_back(grad, normed, inverse, r.gain_v[0, 0:1, :])
    r.yin_v[...] = (r.x1_v[own_rows, :] + back).astype(BF)
    end_start(r.yin_v, 0)

    me = c * 4 + t

    def gain_group(e, f):
        return remote(r.gain_g, r.gain_i.at[me], "ga", e * 4 + f, (e, d, f), rn=me)

    def gain_over_z(e):
        return remote(r.gain_g, r.gain_z.at[d], "gz", e, (c, e, t), rn=d)

    def others(then):
        for e in range(2):
            for f in range(4):

                @pl.when((e != c) | (f != t))
                def _():
                    then(e, f)

    others(lambda e, f: gain_group(e, f).start())
    stage3_f(0, 3)

    r.gain_i[me] = r.gain_g[...]
    others(lambda e, f: gain_group(e, f).wait_send())
    others(lambda e, f: remote(r.gain_g, r.gain_i.at[0], "ga", 0, par, rn=e * 4 + f).wait_recv())
    r.gain_g[...] = jnp.sum(r.gain_i[...], axis=0)

    def other_z(then):
        @pl.loop(0, dp)
        def _(e):
            @pl.when(e != d)
            def _():
                then(e)

    other_z(lambda e: gain_over_z(e).start())
    for n in range(4):
        stage3_a(0, n)
    r.gain_z[d] = r.gain_g[...]
    other_z(lambda e: gain_over_z(e).wait_send())
    other_z(lambda e: remote(r.gain_g, r.gain_z.at[0], "gz", 0, par, rn=e).wait_recv())
    r.dgain[...] = jnp.sum(r.gain_z[...], axis=0)
    z_wait_sends(0, "zf")
    z_wait_sends(0, "za")
    z_arrived("zf")
    z_arrived("za")
    end_sent(r.yown_v, 1)
    end_sent(r.yin_v, 0)
    end_arrived(r.yin_v)


def whole(z, *args):
    dma, regular = pltpu.SemaphoreType.DMA, pltpu.SemaphoreType.REGULAR
    shape = jax.ShapeDtypeStruct
    scratch = [VMEM(of(z), kind) for _, of, kind in BUFFERS]
    for _, of in PAIRS:
        scratch += [dma((of(z),)), dma((of(z),))]
    scratch += [dma((n,)) for _, n in LOCALS]
    scratch += [regular for _ in CREDITS]
    any_spec, vmem_spec = pl.BlockSpec(memory_space=ANY), pl.BlockSpec(memory_space=VMEM)
    return pl.pallas_call(
        functools.partial(kernel, z),
        out_shape=(
            shape((2, z.quarter, z.width), BF),
            shape((2, z.dp, z.rows, z.width), BF),
            shape((4, z.dp, z.rows, z.part), BF),
            shape((2, 2, z.width), F32),
            shape((z.count, z.width), F32),
            shape((z.count, z.width), BF),
            shape((z.count, 2 * z.width), BF),
            shape((z.count, 2 * z.width), BF),
        ),
        in_specs=[any_spec] * 6 + [vmem_spec] + [pl.BlockSpec(memory_space=pltpu.SMEM)] * 3,
        out_specs=[any_spec] * 3 + [vmem_spec] + [any_spec] * 4,
        scratch_shapes=scratch,
        compiler_params=pltpu.CompilerParams(
            collective_id=0, has_side_effects=True, vmem_limit_bytes=64 * 2**20
        ),
        cost_estimate=pl.CostEstimate(flops=10**11, bytes_accessed=10**8, transcendentals=0),
        name="two_layers",
    )(*args)


def on_device(inputs, cotangent, w_qkv, w_out, w_up, w_down, gains, image_sizes, lengths, shifts):
    core = lax.axis_index("section")
    t = lax.axis_index("tensor")
    z = Sizes()
    z.dp = lax.axis_size("dp")
    z.quarter, z.width = inputs.shape[1], inputs.shape[2]
    z.count, z.tokens = 2 * z.quarter, 4 * z.quarter
    z.part = w_qkv.shape[-1]
    z.rows = z.width // z.dp

    ends, zf, za, dgain = whole(
        z, inputs, cotangent, w_qkv[0], w_out[0], w_up[0], w_down[0], gains[0], image_sizes, lengths, shifts
    )[:4]
    f_sum = jnp.sum(zf.astype(F32), axis=1)
    a_sum = jnp.sum(za.astype(F32), axis=1)
    mine = lax.dynamic_index_in_dim(dgain, core, 0, keepdims=True)
    share = z.width // (z.dp * 4)
    slot = lax.axis_index("dp") * 4 + t
    gain_share = lax.dynamic_slice_in_dim(mine, slot * share, share, 2)
    return (
        ends[None],
        a_sum[None, :3],
        a_sum[3].T[None],
        f_sum[None, 0],
        f_sum[None, 1],
        gain_share,
    )


def solution(mesh):
    placed = (
        P("dp", "tensor", None),
        P("dp", "tensor", None),
        P("section", None, None, "tensor"),
        P("section", "tensor", None),
        P("section", None, "tensor"),
        P("section", "tensor", None),
        P("section", None, None),
        P("dp", None),
        P("dp"),
        P(),
    )
    return jax.shard_map(
        on_device,
        mesh=mesh,
        in_specs=placed,
        out_specs=(
            P("section", "dp", "tensor", None),
            P("section", None, "dp", "tensor"),
            P("section", "tensor", "dp"),
            P("section", "dp", "tensor"),
            P("section", ("tensor", "dp"), None),
            P("section", None, ("dp", "tensor")),
        ),
        check_vma=False,
    )
```

```python
import functools

import jax
import jax.numpy as jnp
from jax import lax
from jax.experimental import pallas as pl
from jax.experimental.pallas import tpu as pltpu
from jax.sharding import PartitionSpec as P

MESH = pl.DeviceIdType.MESH
VMEM = pltpu.VMEM
ANY = pl.ANY
BF = jnp.bfloat16
F32 = jnp.float32

HD = 64
WIN = 12
GRID = 24
QL = 512
PATCHES = GRID * GRID
EPS = 1e-05
OFF = -1e30
TILE = 256

NT = (((1,), (1,)), ((), ()))
TN = (((0,), (0,)), ((), ()))


def mm(a, b):
    return jnp.dot(a, b, preferred_element_type=F32)


def mm_nt(a, b):
    return lax.dot_general(a, b, NT, preferred_element_type=F32)


def mm_tn(a, b):
    return lax.dot_general(a, b, TN, preferred_element_type=F32)


def normalize(values):
    centered = values - jnp.mean(values, axis=-1, keepdims=True)
    inverse = lax.rsqrt(jnp.mean(centered * centered, axis=-1, keepdims=True) + EPS)
    return centered * inverse, inverse


def normalize_back(grad, normed, inverse, gain):
    t = grad * gain
    return inverse * (
        t
        - jnp.mean(t, axis=-1, keepdims=True)
        - normed * jnp.mean(t * normed, axis=-1, keepdims=True)
    )


def head_lanes(rows, h):
    lanes = lax.broadcasted_iota(jnp.int32, (rows, 3 * HD), 1)
    return (lanes >= h * HD) & (lanes < h * HD + HD)


def column_of(block, n):
    lanes = lax.broadcasted_iota(jnp.int32, block.shape, 1)
    return jnp.sum(jnp.where(lanes == n, block, 0.0), axis=-1, keepdims=True)


def tile_of(n, size=TILE):
    return pl.ds(pl.multiple_of(n * size, size), size)


BUFFERS = (
    ("x_v", lambda z: (2, z.count, z.width), BF),
    ("g_v", lambda z: (z.count, z.width), BF),
    ("gain_v", lambda z: (2, 2, z.width), F32),
    ("wa_v", lambda z: (2, 3, 2, z.part, z.width), BF),
    ("dwa_v", lambda z: (2, 2, z.width, 2 * z.part), BF),
    ("wf_v", lambda z: (2, 2, 2, z.width, z.width), BF),
    ("wo_v", lambda z: (2, 4, z.part, z.width), BF),
    ("q_v", lambda z: (2, 2, z.count, z.part), BF),
    ("k_v", lambda z: (2, 2, z.tokens, z.part), BF),
    ("v_v", lambda z: (2, 2, z.tokens, z.part), BF),
    ("mixed_v", lambda z: (2, 2, z.count, z.part), BF),
    ("mixr_v", lambda z: (2, z.count, z.part), BF),
    ("lse_v", lambda z: (2, z.count, 128), F32),
    ("x1_v", lambda z: (z.count, z.width), F32),
    ("b_v", lambda z: (z.count, z.width), BF),
    ("acted_v", lambda z: (z.count, 2 * z.width), BF),
    ("slope_v", lambda z: (z.count, 2 * z.width), BF),
    ("a_v", lambda z: (z.count, z.width), BF),
    ("out_v", lambda z: (z.count, z.width), BF),
    ("in_v", lambda z: (2, z.count, z.width), BF),
    ("yout_v", lambda z: (z.quarter, z.width), BF),
    ("yin_v", lambda z: (z.quarter, z.width), BF),
    ("yown_v", lambda z: (z.quarter, z.width), BF),
    ("bias_v", lambda z: (z.count, z.tokens), F32),
    ("dkv_t", lambda z: (2, 2, z.part, z.tokens), F32),
    ("dmix_v", lambda z: (2, z.count, z.part), BF),
    ("dkv_v", lambda z: (2, 2, z.tokens, z.part), BF),
    ("other_v", lambda z: (2, 2, z.count, z.part), BF),
    ("crecv_f", lambda z: (2, z.width, z.width), BF),
    ("yrecv_f", lambda z: (z.width, z.width), BF),
    ("zsend_f", lambda z: (z.dp, z.rows, z.width), BF),
    ("crecv_a", lambda z: (2, z.width, 2 * z.part), BF),
    ("yrecv_a", lambda z: (z.width, 2 * z.part), BF),
    ("zsend_a", lambda z: (z.dp, z.rows, 2 * z.part), BF),
    ("gain_g", lambda z: (2, 2, z.width), F32),
    ("gain_i", lambda z: (8, 2, 2, z.width), F32),
    ("gain_z", lambda z: (z.dp, 2, 2, z.width), F32),
)

PAIRS = (
    ("xs", lambda z: 4),
    ("cs", lambda z: 4),
    ("gs", lambda z: 1),
    ("wsib", lambda z: 6),
    ("wy", lambda z: 12),
    ("wz", lambda z: 6),
    ("wf", lambda z: 6),
    ("wg", lambda z: 6),
    ("wo", lambda z: 16),
    ("kv", lambda z: 16),
    ("mix", lambda z: 4),
    ("ar", lambda z: 4),
    ("yy", lambda z: 1),
    ("pt", lambda z: 2),
    ("cf", lambda z: 2),
    ("ca", lambda z: 2),
    ("yf", lambda z: 4),
    ("ya", lambda z: 4),
    ("zf", lambda z: 2 * z.dp),
    ("za", lambda z: 2 * z.dp),
    ("en", lambda z: 4),
    ("ga", lambda z: 8),
    ("gz", lambda z: z.dp),
)
LOCALS = (("lw", 8), ("lx", 4), ("lh", 4), ("lz", 2), ("le", 2))
CREDITS = ("free_pt", "free_cf", "free_ca", "free_yf", "free_ya")


class Sizes:
    pass


def kernel(z, *refs):
    names = (
        ["inputs", "cotangent", "w_qkv", "w_out", "w_up", "w_down", "gains", "sizes", "lengths", "shifts"]
        + ["ends", "zf_o", "za_o", "dgain", "h_x1", "h_b", "h_acted", "h_slope"]
        + [n for n, _, _ in BUFFERS]
        + [n + e for n, _ in PAIRS for e in ("_s", "_r")]
        + [n for n, _ in LOCALS]
        + list(CREDITS)
    )
    r = Sizes()
    for name, ref in zip(names, refs, strict=True):
        setattr(r, name, ref)

    c, d, t = lax.axis_index("section"), lax.axis_index("dp"), lax.axis_index("tensor")
    m, p = lax.rem(t, 2), t // 2
    px, ax = t + 1 - 2 * m, lax.rem(t + 2, 4)
    dx = ax + 1 - 2 * m
    sib, par, acr = (1 - c, d, t), (c, d, px), (c, d, ax)
    quarter, count, width, dp = z.quarter, z.count, z.width, z.dp

    def remote(src, dst, name, n, device, rn=None):
        return pltpu.make_async_remote_copy(
            src_ref=src,
            dst_ref=dst,
            send_sem=getattr(r, name + "_s").at[n],
            recv_sem=getattr(r, name + "_r").at[n if rn is None else rn],
            device_id=device,
            device_id_type=MESH,
        )

    def local(src, dst, name, n):
        return pltpu.make_async_copy(src, dst, getattr(r, name).at[n])

    def rows_of(i):
        return pl.ds(pl.multiple_of(i * quarter, 16), quarter)

    mine = pl.ds(pl.multiple_of(c * count, 16), count)
    away = pl.ds(pl.multiple_of((1 - c) * count, 16), count)

    def own_weights(n):
        src = (r.w_qkv, r.w_up, r.w_down, r.w_out, r.gains)[n]
        dst = (
            lambda: r.wa_v.at[c, pl.ds(0, 3), 0],
            lambda: r.wf_v.at[c, 0, 0],
            lambda: r.wf_v.at[c, 1, 0],
            lambda: r.wo_v.at[c, t],
            lambda: r.gain_v.at[c],
        )[n]
        return local(src, dst(), "lw", n)

    for n in range(5):
        own_weights(n).start()

    barrier = pltpu.get_barrier_semaphore()

    def hello(device):
        pl.semaphore_signal(barrier, inc=1, device_id=device, device_id_type=MESH)

    for e in range(4):
        @pl.when(e != t)
        def _():
            hello((c, d, e))

        hello((1 - c, d, e))

    @pl.loop(0, dp)
    def _(e):
        @pl.when(e != d)
        def _():
            hello((c, e, t))
            hello((1 - c, e, t))

    pl.semaphore_wait(barrier, 7 + 2 * (dp - 1))

    home = c == p

    first = (quarter // 2 + 15) // 16 * 16
    cuts = ((0, first), (first, quarter - first))

    def spread(src, dst, name, base):
        def piece(ref, n, which=None):
            start = cuts[n][0] if which is None else which * quarter + cuts[n][0]
            return ref.at[pl.ds(start if which is None else pl.multiple_of(start, 16), cuts[n][1])]

        def kept():
            return local(src.at[p], dst.at[rows_of(m)], "lx", base)

        def from_home(n):
            return remote(piece(src.at[p], n), piece(dst, n, m), name, n, par)

        def to_away(n):
            return remote(piece(src.at[1 - p], n), piece(dst, n, m), name, 2 + n, acr)

        def from_away(n):
            return remote(piece(dst, n, m), piece(dst, n, m), name, n, par)

        def start():
            @pl.when(home)
            def _():
                for n in range(2):
                    to_away(n).start()
                kept().start()
                for n in range(2):
                    from_home(n).start()

        def passed():
            @pl.when(jnp.logical_not(home))
            def _():
                for n in range(2):
                    to_away(n).wait_recv()
                    from_away(n).start()

        def wait():
            @pl.when(home)
            def _():
                for n in range(2):
                    to_away(n).wait_send()
                    from_home(n).wait_send()
                kept().wait()

            @pl.when(jnp.logical_not(home))
            def _():
                for n in range(2):
                    from_away(n).wait_send()

            for n in range(2):
                there = piece(dst, n, 1 - m)
                remote(there, there, name, n, par).wait_recv()

        return start, passed, wait

    x_start, x_pass, x_wait = spread(r.inputs, r.x_v.at[0], "xs", 0)
    c_start, c_pass, c_wait = spread(r.cotangent, r.g_v, "cs", 1)
    x_start()

    gain_copy = remote(r.gains, r.gain_v.at[c], "gs", 0, sib)
    gain_copy.start()

    sources = (r.w_qkv, r.w_up, r.w_down)

    def slot(layer, piece, j):
        if piece == 0:
            return r.wa_v.at[layer, pl.ds(0, 3), j]
        return r.wf_v.at[layer, piece - 1, j]

    def to_sib(layer, piece):
        return remote(sources[piece], slot(layer, piece, 0), "wsib", layer * 3 + piece, sib)

    half = lax.rem(d, 2)
    zpar = (c, d + 1 - 2 * half, t)

    def sub(ref, piece, e, core):
        size = (z.part if piece == 0 else width) // 4
        rows = pl.ds(pl.multiple_of((2 * e + core) * size, 16), size)
        return ref.at[:, rows] if piece == 0 else ref.at[rows]

    def to_acr(layer, piece, core):
        return remote(
            sub(sources[piece], piece, half, core),
            sub(slot(layer, piece, 1), piece, half, core),
            "wy",
            (layer * 3 + piece) * 2 + core,
            (core, d, ax),
            rn=layer * 3 + piece,
        )

    def far_copy(layer, piece, e, name, device):
        here = sub(slot(layer, piece, 1), piece, e, c)
        return remote(here, here, name, layer * 3 + piece, device)

    def owner_starts(layer, pieces):
        @pl.when(c == layer)
        def _():
            for piece in pieces:
                for core in range(2):
                    to_acr(layer, piece, core).start()

    def sib_starts(pieces):
        for piece in pieces:
            for layer in range(2):

                @pl.when(c == layer)
                def _():
                    to_sib(layer, piece).start()

    def need_own(layer, piece):
        @pl.when(c == layer)
        def _():
            own_weights(piece).wait()

        @pl.when(c != layer)
        def _():
            to_sib(layer, piece).wait_recv()

    def step_y(layer, piece):
        far_copy(layer, piece, half, "wy", sib).wait_recv()
        far_copy(layer, piece, half, "wz", zpar).start()
        far_copy(layer, piece, half, "wf", sib).start()

    def step_z(layer, piece):
        far_copy(layer, piece, 1 - half, "wz", zpar).wait_recv()
        far_copy(layer, piece, 1 - half, "wg", sib).start()

    def need_far(layer, piece):
        far_copy(layer, piece, half, "wf", sib).wait_recv()
        far_copy(layer, piece, 1 - half, "wg", sib).wait_recv()

    def wo_copy(layer, e, device, n, first=False):
        here = r.wo_v.at[layer, e]
        return remote(r.w_out if first else here, here, "wo", layer * 8 + n, device, rn=layer * 4 + e)

    def wo_sends(layer, n):
        e, device, first = (
            (t, acr, True),
            (t, par, True),
            (t, sib, True),
            (ax, par, False),
            (ax, sib, False),
            (px, sib, False),
            (dx, sib, False),
        )[n]
        return wo_copy(layer, e, device, n, first)

    def wo_arrived(layer, e):
        wo_copy(layer, e, sib, 0).wait_recv()

    def wo_start(layer):
        @pl.when(c == layer)
        def _():
            for n in range(3):
                wo_sends(layer, n).start()

    def step_wo(layer):
        @pl.when(c == layer)
        def _():
            own_weights(3).wait()
            wo_arrived(layer, ax)
            wo_sends(layer, 3).start()
            wo_sends(layer, 4).start()
            wo_arrived(layer, px)
            wo_sends(layer, 5).start()

    def last_wo(layer):
        @pl.when(c == layer)
        def _():
            wo_arrived(layer, dx)
            wo_sends(layer, 6).start()

    def need_wo(layer):
        @pl.when(c != layer)
        def _():
            for e in (t, px, ax, dx):
                wo_arrived(layer, e)

    def finish_weights(layer):
        for piece in range(3):
            far_copy(layer, piece, half, "wz", zpar).wait_send()
            far_copy(layer, piece, half, "wf", sib).wait_send()
            far_copy(layer, piece, 1 - half, "wg", sib).wait_send()

        @pl.when(c == layer)
        def _():
            for piece in range(3):
                to_sib(layer, piece).wait_send()
                for core in range(2):
                    to_acr(layer, piece, core).wait_send()
            for n in range(7):
                wo_sends(layer, n).wait_send()

    sib_starts((0,))
    own_weights(4).wait()
    gain_copy.wait()

    def kv_copy(layer, i, j, n):
        rows = pl.ds(pl.multiple_of(c * count + i * quarter, 16), quarter)
        here = (r.k_v, r.v_v)[n].at[layer, j, rows]
        return remote(here, here, "kv", layer * 8 + i * 4 + j * 2 + n, sib)

    def mix_copy(layer, i, j):
        return remote(
            r.mixed_v.at[layer, j, rows_of(i)], r.mixr_v.at[j, rows_of(i)], "mix", i * 2 + j, par
        )

    def fill_bias(layer):
        high, wide, length = r.sizes[p, 0], r.sizes[p, 1], r.lengths[p]

        def windows(tokens):
            row = (tokens * 2731) >> 16
            col = tokens - row * GRID
            down, right = row + r.shifts[0] * layer, col + r.shifts[1] * layer
            return row, col, ((down * 5462) >> 16) * 8 + ((right * 5462) >> 16)

        cj = lax.broadcasted_iota(jnp.int32, (1, z.tokens), 1)
        row, col, window = windows(cj)
        is_patch = cj < PATCHES
        live_patch = is_patch & (row < high) & (col < wide)
        live_answer = jnp.logical_not(is_patch) & (cj - PATCHES < length)
        cw = jnp.where(live_patch, window, -1)
        ca = jnp.where(live_patch, -1, jnp.where(live_answer, cj, 1 << 20))
        ri = lax.broadcasted_iota(jnp.int32, (count, 1), 0) + c * count
        _, _, window = windows(ri)
        rw = jnp.where(ri < PATCHES, window, -2)
        ra = jnp.where(ri < PATCHES, -5, ri)
        allowed = (cw == rw) | (ca < ra) | (cj == ri)
        r.bias_v[...] = jnp.where(allowed, 0.0, OFF)

    def make_a(layer, rows):
        normed, _ = normalize(r.x_v[layer, rows, :].astype(F32))
        r.a_v[rows, :] = (normed * r.gain_v[layer, 0:1, :]).astype(BF)

    def project_qkv(layer, i, j):
        rows = rows_of(i)
        there = pl.ds(pl.multiple_of(c * count + i * quarter, 16), quarter)
        a = r.a_v[rows, :]
        r.k_v[layer, j, there, :] = mm_nt(a, r.wa_v[layer, 1, j]).astype(BF)
        kv_copy(layer, i, j, 0).start()
        r.v_v[layer, j, there, :] = mm_nt(a, r.wa_v[layer, 2, j]).astype(BF)
        kv_copy(layer, i, j, 1).start()
        r.q_v[layer, j, rows, :] = (mm_nt(a, r.wa_v[layer, 0, j]) * HD**-0.5).astype(BF)

    near_keys = PATCHES
    views = (
        lambda i: c == 0,
        lambda i: (c == 1) & (i == 0),
        lambda i: (c == 1) & (i == 1),
    )
    seen = (near_keys, 3 * quarter, z.tokens)

    def attend(layer, i, j, keys):
        rows = rows_of(i)
        lane = lax.broadcasted_iota(jnp.int32, (quarter, 128), 1)
        stats = r.lse_v[layer, rows, :]
        total = jnp.zeros((quarter, z.part), F32)
        some = pl.ds(0, keys)
        scores = []
        for h in range(3):
            lanes = head_lanes(quarter, h)
            qh = jnp.where(lanes, r.q_v[layer, j, rows, :], jnp.zeros((), BF))
            scores.append(mm_nt(qh, r.k_v[layer, j, some, :]) + r.bias_v[rows, some])
        for h in range(3):
            top = jnp.max(scores[h], axis=-1, keepdims=True)
            expos = jnp.exp(scores[h] - top)
            norm = jnp.sum(expos, axis=-1, keepdims=True)
            stats = jnp.where(lane == j * 3 + h, top + jnp.log(norm), stats)
            part = mm(expos.astype(BF), r.v_v[layer, j, some, :]) * (1.0 / norm)
            total = total + jnp.where(head_lanes(quarter, h), part, 0.0)
        r.lse_v[layer, rows, :] = stats
        r.mixed_v[layer, j, rows, :] = total.astype(BF)

    def attention(layer, between):
        fill_bias(layer)
        r.lse_v[layer] = jnp.zeros((count, 128), F32)

        @pl.loop(0, 2)
        def _(j):
            @pl.loop(0, 2)
            def _(i):
                between(j, i)

                @pl.when(i == 0)
                def _():
                    for e in range(2):
                        for n in range(2):
                            kv_copy(layer, e, j, n).wait()

                for when, keys in zip(views, seen):
                    pl.when(when(i))(functools.partial(attend, layer, i, j, keys))
                mix_copy(layer, i, j).start()

    def at(j, i, there, do):
        pl.when((j == there[0]) & (i == there[1]))(do)

    def project(layer, i):
        rows = rows_of(i)
        total = r.x_v[layer, rows, :].astype(F32)
        total = total + mm(r.mixed_v[layer, 0, rows, :], r.wo_v[layer, t])
        total = total + mm(r.mixed_v[layer, 1, rows, :], r.wo_v[layer, ax])
        for j in range(2):
            mix_copy(layer, i, j).wait()
        total = total + mm(r.mixr_v[0, rows, :], r.wo_v[layer, px])
        total = total + mm(r.mixr_v[1, rows, :], r.wo_v[layer, dx])
        r.x1_v[rows, :] = total
        normed, _ = normalize(total)
        r.b_v[rows, :] = (normed * r.gain_v[layer, 1:2, :]).astype(BF)

    def ar_copy(n, i):
        return remote(
            r.out_v.at[rows_of(i)], r.in_v.at[n % 2, rows_of(i)], "ar", (n % 2) * 2 + i, par
        )

    def summed(n, rows):
        return r.out_v[rows, :].astype(F32) + r.in_v[n % 2, rows, :].astype(F32)

    def hidden_of(layer, i, j):
        hidden = mm(r.b_v[rows_of(i), :], r.wf_v[layer, 0, j])
        cdf = 0.5 + 0.5 * lax.erf(hidden * 0.5**0.5)
        bell = jnp.exp(hidden * hidden * -0.5) * 0.3989422804014327
        return hidden * cdf, cdf + hidden * bell

    def units_of(j):
        return pl.ds(pl.multiple_of(j * width, width), width)

    def over_units(rows, ref, item, layer, product):
        return product(ref[rows, pl.ds(0, width)], r.wf_v[layer, item, 0]) + product(
            ref[rows, pl.ds(width, width)], r.wf_v[layer, item, 1]
        )

    def down(layer, rows):
        return over_units(rows, r.acted_v, 1, layer, mm).astype(BF)

    def up_back(layer, rows):
        return over_units(rows, r.slope_v, 0, layer, mm_nt).astype(BF)

    def dhidden_of(layer, i, j):
        return mm_nt(r.g_v[rows_of(i), :], r.wf_v[layer, 1, j])

    def activate(i, j):
        acted, slope = hidden_of(0, i, j)
        r.acted_v[rows_of(i), units_of(j)] = acted.astype(BF)
        r.slope_v[rows_of(i), units_of(j)] = slope.astype(BF)

    x_pass()
    owner_starts(0, (0,))
    sib_starts((1, 2))
    x_wait()
    owner_starts(0, (1, 2))
    wo_start(0)
    need_own(0, 0)

    @pl.loop(0, 2)
    def _(i):
        make_a(0, rows_of(i))
        project_qkv(0, i, 0)

    step_y(0, 0)

    def between_0(j, i):
        @functools.partial(at, j, i, (0, 1))
        def _():
            step_z(0, 0)
            need_far(0, 0)
            project_qkv(0, 0, 1)
            project_qkv(0, 1, 1)

        @functools.partial(at, j, i, (1, 0))
        def _():
            step_y(0, 1)
            step_wo(0)

        @functools.partial(at, j, i, (1, 1))
        def _():
            step_z(0, 1)
            step_y(0, 2)

    attention(0, between_0)
    last_wo(0)
    step_z(0, 2)
    need_wo(0)
    need_own(0, 1)

    @pl.loop(0, 2)
    def _(i):
        project(0, i)
        activate(i, 0)

    for piece in (1, 2):
        need_far(0, piece)
    need_own(0, 2)
    owner_starts(1, (0,))

    @pl.loop(0, 2)
    def _(i):
        rows = rows_of(i)
        activate(i, 1)
        r.out_v[rows, :] = down(0, rows)
        ar_copy(0, i).start()

    kept = [
        (r.x1_v, r.h_x1),
        (r.b_v, r.h_b),
        (r.acted_v, r.h_acted),
        (r.slope_v, r.h_slope),
    ]
    for n, (here, there) in enumerate(kept):
        local(here, there, "lh", n).start()
    step_y(1, 0)
    c_start()
    owner_starts(1, (1, 2))
    step_z(1, 0)
    need_own(1, 0)
    need_far(1, 0)

    @pl.loop(0, 2)
    def _(i):
        rows = rows_of(i)
        ar_copy(0, i).wait()
        r.x_v[1, rows, :] = (r.x1_v[rows, :] + summed(0, rows)).astype(BF)
        make_a(1, rows)
        for j in range(2):
            project_qkv(1, i, j)

    c_pass()
    wo_start(1)

    def between_1(j, i):
        @functools.partial(at, j, i, (0, 0))
        def _():
            step_y(1, 1)

        @functools.partial(at, j, i, (0, 1))
        def _():
            step_z(1, 1)
            step_y(1, 2)
            step_wo(1)

        @functools.partial(at, j, i, (1, 0))
        def _():
            step_z(1, 2)

    attention(1, between_1)
    last_wo(1)
    need_wo(1)
    for piece in (1, 2):
        need_own(1, piece)
        need_far(1, piece)
    c_wait()
    for n, (here, there) in enumerate(kept):
        local(here, there, "lh", n).wait()

    @pl.loop(0, 2)
    def _(i):
        rows = rows_of(i)
        project(1, i)

        @pl.loop(0, 2)
        def _(j):
            acted, slope = hidden_of(1, i, j)
            r.acted_v[rows, units_of(j)] = acted.astype(BF)
            r.slope_v[rows, units_of(j)] = (dhidden_of(1, i, j) * slope).astype(BF)

        r.out_v[rows, :] = up_back(1, rows)
        ar_copy(1, i).start()

    own_rows, par_rows = rows_of(m), rows_of(1 - m)

    r.yout_v[...] = down(1, par_rows)
    y_copy = remote(r.yout_v, r.yin_v, "yy", 0, par)
    r.yown_v[...] = down(1, own_rows)

    def end_copies(src, section):
        stays = (c == section) & (p == section)

        def far():
            return remote(src, r.ends.at[p], "en", section * 2, (section, d, 2 * c + m), rn=p)

        return stays, far, lambda: local(src, r.ends.at[p], "le", section)

    def end_start(src, section):
        stays, far, near = end_copies(src, section)
        pl.when(stays)(lambda: near().start())
        pl.when(jnp.logical_not(stays))(lambda: far().start())

    def end_sent(src, section):
        stays, far, near = end_copies(src, section)
        pl.when(stays)(lambda: near().wait())
        pl.when(jnp.logical_not(stays))(lambda: far().wait_send())

    def end_arrived(src):
        for i in range(2):
            came = jnp.logical_not((c == p) & (i == c))

            @pl.when(came)
            def _():
                remote(src, r.ends.at[i], "en", i, par).wait_recv()

    def grad_f(layer, j):
        @pl.loop(0, width // TILE)
        def _(n):
            here = tile_of(n)
            cols = pl.ds(pl.multiple_of(n * TILE, TILE) + j * width, TILE)
            r.wf_v[layer, 0, j, :, here] = mm_tn(r.b_v[...], r.slope_v[:, cols]).astype(BF)
            r.wf_v[layer, 1, j, here, :] = mm_tn(r.acted_v[:, cols], r.g_v[...]).astype(BF)

    def held(which, layer, item):
        return r.wf_v.at[layer, item] if which == "f" else r.dwa_v.at[item]

    def crecv(which):
        return r.crecv_f if which == "f" else r.crecv_a

    def yrecv(which):
        return r.yrecv_f if which == "f" else r.yrecv_a

    def zsend(which):
        return r.zsend_f if which == "f" else r.zsend_a

    def zland(which):
        return r.zf_o if which == "f" else r.za_o

    def core_copy(which, layer, j):
        return remote(held(which, layer, 1 - c).at[j], crecv(which).at[j], "c" + which, j, sib)

    STEP = width // 4
    place_z = d // (dp // 4)

    def group_at(n):
        return (
            3 - place_z,
            lax.rem(place_z + 2, 4),
            place_z + 1 - 2 * lax.rem(place_z, 2),
            place_z,
        )[n]

    def y_copy_of(which, n):
        rows = tile_of(group_at(n), STEP)
        return remote(crecv(which).at[1, rows], yrecv(which).at[rows], "y" + which, n, acr)

    def credit(name, device):
        pl.semaphore_signal(getattr(r, name), inc=1, device_id=device, device_id_type=MESH)

    def spend(name):
        pl.semaphore_wait(getattr(r, name), 1)

    group = 1 if z.rows % 16 == 0 else 2

    def z_copy(layer, which, e):
        return remote(
            zsend(which).at[e], zland(which).at[c, d], "z" + which, e, (layer, e, t), rn=c * dp + d
        )

    def stage2(which, layer):
        core_copy(which, layer, 1).wait()
        if layer == 0:
            spend("free_y" + which)
        got = crecv(which)
        for n in range(4):
            rows = tile_of(group_at(n), STEP)
            got[1, rows, :] = (
                got[1, rows, :].astype(F32) + held(which, layer, c)[1, rows, :].astype(F32)
            ).astype(BF)
            y_copy_of(which, n).start()

    def z_wait_sends(layer, which):
        @pl.loop(0, dp)
        def _(e):
            @pl.when((c != layer) | (e != d))
            def _():
                z_copy(layer, which, e).wait_send()

    def z_send(layer, which, n):
        first = group_at(n) * (dp // 4)

        @pl.loop(0, dp // 4)
        def _(f):
            e = first + f

            @pl.when((c != layer) | (e != d))
            def _():
                z_copy(layer, which, e).start()

            @pl.when((c == layer) & (e == d))
            def _():
                near = local(zsend(which).at[d], zland(which).at[c, d], "lz", 0)
                near.start()
                near.wait()

    def z_arrived(which):
        for core in range(2):

            @pl.loop(0, dp)
            def _(e):
                @pl.when((core != c) | (e != d))
                def _():
                    remote(
                        zsend(which).at[0], zland(which).at[core, e], "z" + which, 0, par, rn=core * dp + e
                    ).wait_recv()

    def stage3(which, layer, n):
        if n == 0:
            core_copy(which, layer, 0).wait()
            if layer == 0:
                z_wait_sends(1, which)
        y_copy_of(which, n).wait()
        got, more, out = crecv(which), yrecv(which), zsend(which)

        @pl.loop(0, dp // 4 // group)
        def _(e):
            first = group_at(n) * (dp // 4) + e * group
            rows = pl.ds(pl.multiple_of(first * z.rows, group * z.rows), group * z.rows)
            total = (
                got[0, rows, :].astype(F32)
                + held(which, layer, c)[0, rows, :].astype(F32)
                + more[rows, :].astype(F32)
            )
            out[pl.ds(first, group)] = total.reshape(group, z.rows, total.shape[-1]).astype(BF)

        if layer == 1 and n == 3:
            credit("free_c" + which, sib)
            credit("free_y" + which, acr)
        z_send(layer, which, n)

    r.gain_g[...] = jnp.zeros_like(r.gain_g)

    def gain_grad(layer, n, i, grad, normed):
        share = jnp.where(i == m, 1.0, 0.0)
        r.gain_g[layer, n : n + 1, :] += share * jnp.sum(grad * normed, axis=0, keepdims=True)

    def after_ffn(layer, n):
        @pl.loop(0, 2)
        def _(i):
            rows = rows_of(i)
            ar_copy(n, i).wait()
            grad = summed(n, rows)
            normed, inverse = normalize(r.x1_v[rows, :])
            gain_grad(layer, 1, i, grad, normed)
            back = normalize_back(grad, normed, inverse, r.gain_v[layer, 1:2, :])
            dx1 = r.g_v[rows, :].astype(F32) + back
            dc = dx1.astype(BF)
            r.x1_v[rows, :] = dx1
            r.dmix_v[0, rows, :] = mm_nt(dc, r.wo_v[layer, t]).astype(BF)
            r.dmix_v[1, rows, :] = mm_nt(dc, r.wo_v[layer, ax]).astype(BF)

    def pt_copy(n):
        return remote(r.dkv_v.at[n, :, away], r.other_v.at[n], "pt", n, sib)

    def attend_back(layer, j, keys):
        some = pl.ds(0, keys)
        zero = jnp.zeros((), BF)
        q, dmix = r.q_v[layer, j], r.dmix_v[j]
        q_t, dmix_t = q.T, dmix.T
        k, v = r.k_v[layer, j, some, :], r.v_v[layer, j, some, :]
        product = dmix.astype(F32) * r.mixed_v[layer, j].astype(F32)
        total = jnp.zeros((count, z.part), F32)
        for h in range(3):
            lanes = head_lanes(count, h)
            heads = pl.ds(h * HD, HD)
            scores = mm_nt(jnp.where(lanes, q, zero), k) + r.bias_v[:, some]
            dprobs = mm_nt(jnp.where(lanes, dmix, zero), v)
            probs = jnp.exp(scores - column_of(r.lse_v[layer], j * 3 + h))
            inner = jnp.sum(jnp.where(lanes, product, 0.0), axis=-1, keepdims=True)
            r.dkv_t[1, j, heads, some] = mm(dmix_t[h * HD : h * HD + HD], probs.astype(BF))
            dscores = (probs * (dprobs - inner)).astype(BF)
            total = total + jnp.where(lanes, mm(dscores, k), 0.0)
            r.dkv_t[0, j, heads, some] = mm(q_t[h * HD : h * HD + HD], dscores)
        r.q_v[layer, j] = (total * HD**-0.5).astype(BF)

    def attention_back(layer, between):
        fill_bias(layer)
        r.dkv_t[...] = jnp.zeros_like(r.dkv_t)

        @pl.loop(0, 2)
        def _(j):
            between(j)
            pl.when(c == 0)(functools.partial(attend_back, layer, j, near_keys))
            pl.when(c == 1)(functools.partial(attend_back, layer, j, z.tokens))

        for n in range(2):
            for j in range(2):
                r.dkv_v[n, j] = r.dkv_t[n, j].T.astype(BF)
        if layer == 0:
            spend("free_pt")
        for n in range(2):
            pt_copy(n).start()
        for i in range(2):
            make_a(layer, rows_of(i))
        between(2)
        for n in range(2):
            pt_copy(n).wait()
            r.dkv_v[n, :, mine, :] = (
                r.dkv_v[n, :, mine, :].astype(F32) + r.other_v[n].astype(F32)
            ).astype(BF)
        if layer == 1:
            credit("free_pt", sib)

    def in_all(rows):
        return pl.ds(pl.multiple_of(c * count + rows.start, 16), quarter)

    def da_chunk(layer, rows):
        total = jnp.zeros((quarter, width), F32)
        for j in range(2):
            total = total + mm(r.q_v[layer, j, rows, :], r.wa_v[layer, 0, j])
            for e in range(2):
                total = total + mm(r.dkv_v[e, j, in_all(rows), :], r.wa_v[layer, 1 + e, j])
        r.out_v[rows, :] = total.astype(BF)

    def grad_a(layer):
        @pl.loop(0, 2)
        def _(n):
            j = 1 - n
            pair = jnp.concatenate([r.q_v[layer, j], r.dkv_v[0, j, mine, :]], axis=1)
            r.dwa_v[0, j] = mm_tn(r.a_v[...], pair).astype(BF)
            of_v = mm_tn(r.a_v[...], r.dkv_v[1, j, mine, :])
            of_out = mm_tn(r.x1_v[...].astype(BF), r.mixed_v[layer, j])
            r.dwa_v[1, j] = jnp.concatenate([of_v, of_out], axis=1).astype(BF)
            core_copy("a", layer, j).start()

    finish_weights(1)
    for j in (1, 0):
        grad_f(1, j)
        core_copy("f", 1, j).start()
    stage2("f", 1)
    r.yown_v[...] = (r.x1_v[own_rows, :] + r.yown_v[...].astype(F32)).astype(BF)
    after_ffn(1, 1)
    y_copy.start()
    for n, (here, there) in enumerate(kept[1:]):
        local(there, here, "lh", n).start()

    def between_back_1(j):
        if isinstance(j, int):
            stage3("f", 1, 1)
            y_copy.wait()
            r.yown_v[...] = (r.yown_v[...].astype(F32) + r.yin_v[...].astype(F32)).astype(BF)
            end_start(r.yown_v, 1)
        else:
            pl.when(j == 1)(functools.partial(stage3, "f", 1, 0))

    attention_back(1, between_back_1)

    @pl.loop(0, 2)
    def _(i):
        da_chunk(1, rows_of(i))
        ar_copy(2, i).start()

    stage3("f", 1, 2)
    grad_a(1)
    stage3("f", 1, 3)
    stage2("a", 1)
    for n, (here, there) in enumerate(kept[1:]):
        local(there, here, "lh", n).wait()

    @pl.loop(0, 2)
    def _(i):
        rows = rows_of(i)
        ar_copy(2, i).wait()
        grad = summed(2, rows)
        normed, inverse = normalize(r.x_v[1, rows, :].astype(F32))
        gain_grad(1, 0, i, grad, normed)
        back = normalize_back(grad, normed, inverse, r.gain_v[1, 0:1, :])
        r.g_v[rows, :] = (r.x1_v[rows, :] + back).astype(BF)

        @pl.loop(0, 2)
        def _(j):
            cols = units_of(j)
            du = dhidden_of(0, i, j)
            r.slope_v[rows, cols] = (du * r.slope_v[rows, cols].astype(F32)).astype(BF)

        r.out_v[rows, :] = up_back(0, rows)
        ar_copy(3, i).start()

    local(r.h_x1, r.x1_v, "lh", 3).start()
    finish_weights(0)
    spend("free_cf")
    for j in (1, 0):
        grad_f(0, j)
        core_copy("f", 0, j).start()
    stage3("a", 1, 0)
    stage2("f", 0)
    for n in range(1, 4):
        stage3("a", 1, n)
    local(r.h_x1, r.x1_v, "lh", 3).wait()
    after_ffn(0, 3)

    def between_back_0(j):
        if isinstance(j, int):
            stage3("f", 0, 1)
        else:
            pl.when(j == 1)(functools.partial(stage3, "f", 0, 0))

    attention_back(0, between_back_0)
    da_chunk(0, par_rows)
    dx_copy = remote(r.out_v.at[par_rows], r.in_v.at[0, par_rows], "ar", 0, par)
    dx_copy.start()
    spend("free_ca")
    da_chunk(0, own_rows)
    grad_a(0)
    stage2("a", 0)
    stage3("f", 0, 2)
    dx_copy.wait()
    grad = summed(0, own_rows)
    normed, inverse = normalize(r.x_v[0, own_rows, :].astype(F32))
    gain_grad(0, 0, m, grad, normed)
    back = normalize_back(grad, normed, inverse, r.gain_v[0, 0:1, :])
    r.yin_v[...] = (r.x1_v[own_rows, :] + back).astype(BF)
    end_start(r.yin_v, 0)

    me = c * 4 + t

    def gain_group(e, f):
        return remote(r.gain_g, r.gain_i.at[me], "ga", e * 4 + f, (e, d, f), rn=me)

    def gain_over_z(e):
        return remote(r.gain_g, r.gain_z.at[d], "gz", e, (c, e, t), rn=d)

    def others(then):
        for e in range(2):
            for f in range(4):

                @pl.when((e != c) | (f != t))
                def _():
                    then(e, f)

    others(lambda e, f: gain_group(e, f).start())
    stage3("f", 0, 3)

    r.gain_i[me] = r.gain_g[...]
    others(lambda e, f: gain_group(e, f).wait_send())
    others(lambda e, f: remote(r.gain_g, r.gain_i.at[0], "ga", 0, par, rn=e * 4 + f).wait_recv())
    r.gain_g[...] = jnp.sum(r.gain_i[...], axis=0)

    def other_z(then):
        @pl.loop(0, dp)
        def _(e):
            @pl.when(e != d)
            def _():
                then(e)

    other_z(lambda e: gain_over_z(e).start())
    for n in range(4):
        stage3("a", 0, n)
    r.gain_z[d] = r.gain_g[...]
    other_z(lambda e: gain_over_z(e).wait_send())
    other_z(lambda e: remote(r.gain_g, r.gain_z.at[0], "gz", 0, par, rn=e).wait_recv())
    r.dgain[...] = jnp.sum(r.gain_z[...], axis=0)
    z_wait_sends(0, "f")
    z_wait_sends(0, "a")
    z_arrived("f")
    z_arrived("a")
    end_sent(r.yown_v, 1)
    end_sent(r.yin_v, 0)
    end_arrived(r.yin_v)


def whole(z, *args):
    dma, regular = pltpu.SemaphoreType.DMA, pltpu.SemaphoreType.REGULAR
    shape = jax.ShapeDtypeStruct
    scratch = [VMEM(of(z), kind) for _, of, kind in BUFFERS]
    for _, of in PAIRS:
        scratch += [dma((of(z),)), dma((of(z),))]
    scratch += [dma((n,)) for _, n in LOCALS]
    scratch += [regular for _ in CREDITS]
    any_spec, vmem_spec = pl.BlockSpec(memory_space=ANY), pl.BlockSpec(memory_space=VMEM)
    return pl.pallas_call(
        functools.partial(kernel, z),
        out_shape=(
            shape((2, z.quarter, z.width), BF),
            shape((2, z.dp, z.rows, z.width), BF),
            shape((2, z.dp, z.rows, 2 * z.part), BF),
            shape((2, 2, z.width), F32),
            shape((z.count, z.width), F32),
            shape((z.count, z.width), BF),
            shape((z.count, 2 * z.width), BF),
            shape((z.count, 2 * z.width), BF),
        ),
        in_specs=[any_spec] * 6 + [vmem_spec] + [pl.BlockSpec(memory_space=pltpu.SMEM)] * 3,
        out_specs=[any_spec] * 3 + [vmem_spec] + [any_spec] * 4,
        scratch_shapes=scratch,
        compiler_params=pltpu.CompilerParams(
            collective_id=0, has_side_effects=True, vmem_limit_bytes=64 * 2**20
        ),
        cost_estimate=pl.CostEstimate(flops=10**11, bytes_accessed=10**8, transcendentals=0),
        name="two_layers",
    )(*args)


def on_device(inputs, cotangent, w_qkv, w_out, w_up, w_down, gains, image_sizes, lengths, shifts):
    core = lax.axis_index("section")
    t = lax.axis_index("tensor")
    z = Sizes()
    z.dp = lax.axis_size("dp")
    z.quarter, z.width = inputs.shape[1], inputs.shape[2]
    z.count, z.tokens = 2 * z.quarter, 4 * z.quarter
    z.part = w_qkv.shape[-1]
    z.rows = z.width // z.dp

    ends, zf, za, dgain = whole(
        z, inputs, cotangent, jnp.swapaxes(w_qkv[0], 1, 2), w_out[0], w_up[0], w_down[0], gains[0], image_sizes, lengths, shifts
    )[:4]
    f_sum = jnp.sum(zf.astype(F32), axis=1)
    a_sum = jnp.sum(za.astype(F32), axis=1)
    mine = lax.dynamic_index_in_dim(dgain, core, 0, keepdims=True)
    share = z.width // (z.dp * 4)
    slot = lax.axis_index("dp") * 4 + t
    gain_share = lax.dynamic_slice_in_dim(mine, slot * share, share, 2)
    return (
        ends[None],
        jnp.stack([a_sum[0, :, : z.part], a_sum[0, :, z.part :], a_sum[1, :, : z.part]])[None],
        a_sum[1, :, z.part :].T[None],
        f_sum[None, 0],
        f_sum[None, 1],
        gain_share,
    )


def solution(mesh):
    placed = (
        P("dp", "tensor", None),
        P("dp", "tensor", None),
        P("section", None, None, "tensor"),
        P("section", "tensor", None),
        P("section", None, "tensor"),
        P("section", "tensor", None),
        P("section", None, None),
        P("dp", None),
        P("dp"),
        P(),
    )
    return jax.shard_map(
        on_device,
        mesh=mesh,
        in_specs=placed,
        out_specs=(
            P("section", "dp", "tensor", None),
            P("section", None, "dp", "tensor"),
            P("section", "tensor", "dp"),
            P("section", "dp", "tensor"),
            P("section", ("tensor", "dp"), None),
            P("section", None, ("dp", "tensor")),
        ),
        check_vma=False,
    )
```

```python
import functools

import jax
import jax.numpy as jnp
from jax import lax
from jax.experimental import pallas as pl
from jax.experimental.pallas import tpu as pltpu
from jax.sharding import PartitionSpec as P

MESH = pl.DeviceIdType.MESH
VMEM = pltpu.VMEM
ANY = pl.ANY
BF = jnp.bfloat16
F32 = jnp.float32

HD = 64
WIN = 12
GRID = 24
QL = 512
PATCHES = GRID * GRID
EPS = 1e-05
OFF = -1e30
TILE = 256

NT = (((1,), (1,)), ((), ()))
TN = (((0,), (0,)), ((), ()))


def mm(a, b):
    return jnp.dot(a, b, preferred_element_type=F32)


def mm_nt(a, b):
    return lax.dot_general(a, b, NT, preferred_element_type=F32)


def mm_tn(a, b):
    return lax.dot_general(a, b, TN, preferred_element_type=F32)


def normalize(values):
    centered = values - jnp.mean(values, axis=-1, keepdims=True)
    inverse = lax.rsqrt(jnp.mean(centered * centered, axis=-1, keepdims=True) + EPS)
    return centered * inverse, inverse


def normalize_back(grad, normed, inverse, gain):
    t = grad * gain
    return inverse * (
        t
        - jnp.mean(t, axis=-1, keepdims=True)
        - normed * jnp.mean(t * normed, axis=-1, keepdims=True)
    )


def head_lanes(rows, h):
    lanes = lax.broadcasted_iota(jnp.int32, (rows, 3 * HD), 1)
    return (lanes >= h * HD) & (lanes < h * HD + HD)


def column_of(block, n):
    lanes = lax.broadcasted_iota(jnp.int32, block.shape, 1)
    return jnp.sum(jnp.where(lanes == n, block, 0.0), axis=-1, keepdims=True)


def tile_of(n, size=TILE):
    return pl.ds(pl.multiple_of(n * size, size), size)


BUFFERS = (
    ("x_v", lambda z: (2, z.count, z.width), BF),
    ("g_v", lambda z: (z.count, z.width), BF),
    ("gain_v", lambda z: (2, 2, z.width), F32),
    ("wa_v", lambda z: (2, 3, 2, z.part, z.width), BF),
    ("dwa_v", lambda z: (2, 2, z.width, 2 * z.part), BF),
    ("wf_v", lambda z: (2, 2, 2, z.width, z.width), BF),
    ("wo_v", lambda z: (2, 4, z.part, z.width), BF),
    ("q_v", lambda z: (2, 2, z.count, z.part), BF),
    ("k_v", lambda z: (2, 2, z.tokens, z.part), BF),
    ("v_v", lambda z: (2, 2, z.tokens, z.part), BF),
    ("mixed_v", lambda z: (2, 2, z.count, z.part), BF),
    ("mixr_v", lambda z: (2, z.count, z.part), BF),
    ("lse_v", lambda z: (2, z.count, 128), F32),
    ("x1_v", lambda z: (z.count, z.width), F32),
    ("b_v", lambda z: (z.count, z.width), BF),
    ("acted_v", lambda z: (z.count, 2 * z.width), BF),
    ("slope_v", lambda z: (z.count, 2 * z.width), BF),
    ("a_v", lambda z: (z.count, z.width), BF),
    ("out_v", lambda z: (z.count, z.width), BF),
    ("in_v", lambda z: (2, z.count, z.width), BF),
    ("yout_v", lambda z: (z.quarter, z.width), BF),
    ("yin_v", lambda z: (z.quarter, z.width), BF),
    ("yown_v", lambda z: (z.quarter, z.width), BF),
    ("bias_v", lambda z: (z.count, z.tokens), F32),
    ("dkv_t", lambda z: (2, 2, z.part, z.tokens), F32),
    ("dmix_v", lambda z: (2, z.count, z.part), BF),
    ("dkv_v", lambda z: (2, 2, z.tokens, z.part), BF),
    ("other_v", lambda z: (2, 2, z.count, z.part), BF),
    ("crecv_f", lambda z: (2, z.width, z.width), BF),
    ("yrecv_f", lambda z: (z.width, z.width), BF),
    ("zsend_f", lambda z: (z.dp, z.rows, z.width), BF),
    ("crecv_a", lambda z: (2, z.width, 2 * z.part), BF),
    ("yrecv_a", lambda z: (z.width, 2 * z.part), BF),
    ("zsend_a", lambda z: (z.dp, z.rows, 2 * z.part), BF),
    ("zswap_f", lambda z: (z.dp // 4, z.rows, z.width), BF),
    ("zswap_a", lambda z: (z.dp // 4, z.rows, 2 * z.part), BF),
    ("gain_g", lambda z: (2, 2, z.width), F32),
    ("gain_i", lambda z: (8, 2, 2, z.width), F32),
    ("gain_z", lambda z: (z.dp, 2, 2, z.width), F32),
)

PAIRS = (
    ("xs", lambda z: 8),
    ("cs", lambda z: 8),
    ("gs", lambda z: 1),
    ("wsib", lambda z: 6),
    ("wy", lambda z: 12),
    ("wz", lambda z: 6),
    ("wf", lambda z: 6),
    ("wg", lambda z: 6),
    ("wo", lambda z: 16),
    ("kv", lambda z: 16),
    ("mix", lambda z: 4),
    ("ar", lambda z: 4),
    ("yy", lambda z: 1),
    ("pt", lambda z: 2),
    ("cf", lambda z: 2),
    ("ca", lambda z: 2),
    ("yf", lambda z: 4),
    ("ya", lambda z: 4),
    ("zf", lambda z: 2 * z.dp),
    ("za", lambda z: 2 * z.dp),
    ("sf", lambda z: 1),
    ("sa", lambda z: 1),
    ("en", lambda z: 4),
    ("ga", lambda z: 8),
    ("gz", lambda z: z.dp),
)
LOCALS = (("lw", 8), ("lx", 4), ("lh", 4), ("lz", 2), ("le", 2))
CREDITS = ("free_pt", "free_cf", "free_ca", "free_yf", "free_ya", "free_sf", "free_sa")


class Sizes:
    pass


def kernel(z, *refs):
    names = (
        ["inputs", "cotangent", "w_qkv", "w_out", "w_up", "w_down", "gains", "sizes", "lengths", "shifts"]
        + ["ends", "zf_o", "za_o", "dgain", "h_x1", "h_b", "h_acted", "h_slope"]
        + [n for n, _, _ in BUFFERS]
        + [n + e for n, _ in PAIRS for e in ("_s", "_r")]
        + [n for n, _ in LOCALS]
        + list(CREDITS)
    )
    r = Sizes()
    for name, ref in zip(names, refs, strict=True):
        setattr(r, name, ref)

    c, d, t = lax.axis_index("section"), lax.axis_index("dp"), lax.axis_index("tensor")
    m, p = lax.rem(t, 2), t // 2
    px, ax = t + 1 - 2 * m, lax.rem(t + 2, 4)
    dx = ax + 1 - 2 * m
    sib, par, acr = (1 - c, d, t), (c, d, px), (c, d, ax)
    quarter, count, width, dp = z.quarter, z.count, z.width, z.dp

    def remote(src, dst, name, n, device, rn=None):
        return pltpu.make_async_remote_copy(
            src_ref=src,
            dst_ref=dst,
            send_sem=getattr(r, name + "_s").at[n],
            recv_sem=getattr(r, name + "_r").at[n if rn is None else rn],
            device_id=device,
            device_id_type=MESH,
        )

    def local(src, dst, name, n):
        return pltpu.make_async_copy(src, dst, getattr(r, name).at[n])

    def rows_of(i):
        return pl.ds(pl.multiple_of(i * quarter, 16), quarter)

    mine = pl.ds(pl.multiple_of(c * count, 16), count)
    away = pl.ds(pl.multiple_of((1 - c) * count, 16), count)

    def own_weights(n):
        src = (r.w_qkv, r.w_up, r.w_down, r.w_out, r.gains)[n]
        dst = (
            lambda: r.wa_v.at[c, pl.ds(0, 3), 0],
            lambda: r.wf_v.at[c, 0, 0],
            lambda: r.wf_v.at[c, 1, 0],
            lambda: r.wo_v.at[c, t],
            lambda: r.gain_v.at[c],
        )[n]
        return local(src, dst(), "lw", n)

    for n in range(5):
        own_weights(n).start()

    barrier = pltpu.get_barrier_semaphore()

    def hello(device):
        pl.semaphore_signal(barrier, inc=1, device_id=device, device_id_type=MESH)

    for e in range(4):
        @pl.when(e != t)
        def _():
            hello((c, d, e))

        hello((1 - c, d, e))

    @pl.loop(0, dp)
    def _(e):
        @pl.when(e != d)
        def _():
            hello((c, e, t))
            hello((1 - c, e, t))

    pl.semaphore_wait(barrier, 7 + 2 * (dp - 1))

    home = c == p

    PIECES = 4
    edges = [n * (quarter // 16) // PIECES * 16 for n in range(PIECES)] + [quarter]
    cuts = [(a, b - a) for a, b in zip(edges, edges[1:])]

    def spread(src, dst, name, base):
        def piece(ref, n, which=None):
            start = cuts[n][0] if which is None else which * quarter + cuts[n][0]
            return ref.at[pl.ds(start if which is None else pl.multiple_of(start, 16), cuts[n][1])]

        def kept():
            return local(src.at[p], dst.at[rows_of(m)], "lx", base)

        def from_home(n):
            return remote(piece(src.at[p], n), piece(dst, n, m), name, n, par)

        def to_away(n):
            return remote(piece(src.at[1 - p], n), piece(dst, n, m), name, PIECES + n, acr)

        def from_away(n):
            return remote(piece(dst, n, m), piece(dst, n, m), name, n, par)

        def start():
            @pl.when(home)
            def _():
                for n in range(PIECES):
                    to_away(n).start()
                kept().start()
                for n in range(PIECES):
                    from_home(n).start()

        def passed():
            @pl.when(jnp.logical_not(home))
            def _():
                for n in range(PIECES):
                    to_away(n).wait_recv()
                    from_away(n).start()

        def wait():
            @pl.when(home)
            def _():
                for n in range(PIECES):
                    to_away(n).wait_send()
                    from_home(n).wait_send()
                kept().wait()

            @pl.when(jnp.logical_not(home))
            def _():
                for n in range(PIECES):
                    from_away(n).wait_send()

            for n in range(PIECES):
                there = piece(dst, n, 1 - m)
                remote(there, there, name, n, par).wait_recv()

        return start, passed, wait

    x_start, x_pass, x_wait = spread(r.inputs, r.x_v.at[0], "xs", 0)
    c_start, c_pass, c_wait = spread(r.cotangent, r.g_v, "cs", 1)
    x_start()

    gain_copy = remote(r.gains, r.gain_v.at[c], "gs", 0, sib)
    gain_copy.start()

    sources = (r.w_qkv, r.w_up, r.w_down)

    def slot(layer, piece, j):
        if piece == 0:
            return r.wa_v.at[layer, pl.ds(0, 3), j]
        return r.wf_v.at[layer, piece - 1, j]

    def to_sib(layer, piece):
        return remote(sources[piece], slot(layer, piece, 0), "wsib", layer * 3 + piece, sib)

    half = lax.rem(d, 2)
    zpar = (c, d + 1 - 2 * half, t)

    def sub(ref, piece, e, core):
        size = (z.part if piece == 0 else width) // 4
        rows = pl.ds(pl.multiple_of((2 * e + core) * size, 16), size)
        return ref.at[:, rows] if piece == 0 else ref.at[rows]

    def to_acr(layer, piece, core):
        return remote(
            sub(sources[piece], piece, half, core),
            sub(slot(layer, piece, 1), piece, half, core),
            "wy",
            (layer * 3 + piece) * 2 + core,
            (core, d, ax),
            rn=layer * 3 + piece,
        )

    def far_copy(layer, piece, e, name, device):
        here = sub(slot(layer, piece, 1), piece, e, c)
        return remote(here, here, name, layer * 3 + piece, device)

    def owner_starts(layer, pieces):
        @pl.when(c == layer)
        def _():
            for piece in pieces:
                for core in range(2):
                    to_acr(layer, piece, core).start()

    def sib_starts(pieces):
        for piece in pieces:
            for layer in range(2):

                @pl.when(c == layer)
                def _():
                    to_sib(layer, piece).start()

    def need_own(layer, piece):
        @pl.when(c == layer)
        def _():
            own_weights(piece).wait()

        @pl.when(c != layer)
        def _():
            to_sib(layer, piece).wait_recv()

    def step_y(layer, piece):
        far_copy(layer, piece, half, "wy", sib).wait_recv()
        far_copy(layer, piece, half, "wz", zpar).start()
        far_copy(layer, piece, half, "wf", sib).start()

    def step_z(layer, piece):
        far_copy(layer, piece, 1 - half, "wz", zpar).wait_recv()
        far_copy(layer, piece, 1 - half, "wg", sib).start()

    def need_far(layer, piece):
        far_copy(layer, piece, half, "wf", sib).wait_recv()
        far_copy(layer, piece, 1 - half, "wg", sib).wait_recv()

    def wo_copy(layer, e, device, n, first=False):
        here = r.wo_v.at[layer, e]
        return remote(r.w_out if first else here, here, "wo", layer * 8 + n, device, rn=layer * 4 + e)

    def wo_sends(layer, n):
        e, device, first = (
            (t, acr, True),
            (t, par, True),
            (t, sib, True),
            (ax, par, False),
            (ax, sib, False),
            (px, sib, False),
            (dx, sib, False),
        )[n]
        return wo_copy(layer, e, device, n, first)

    def wo_arrived(layer, e):
        wo_copy(layer, e, sib, 0).wait_recv()

    def wo_start(layer):
        @pl.when(c == layer)
        def _():
            for n in range(3):
                wo_sends(layer, n).start()

    def step_wo(layer):
        @pl.when(c == layer)
        def _():
            own_weights(3).wait()
            wo_arrived(layer, ax)
            wo_sends(layer, 3).start()
            wo_sends(layer, 4).start()
            wo_arrived(layer, px)
            wo_sends(layer, 5).start()

    def last_wo(layer):
        @pl.when(c == layer)
        def _():
            wo_arrived(layer, dx)
            wo_sends(layer, 6).start()

    def need_wo(layer):
        @pl.when(c != layer)
        def _():
            for e in (t, px, ax, dx):
                wo_arrived(layer, e)

    def finish_weights(layer):
        for piece in range(3):
            far_copy(layer, piece, half, "wz", zpar).wait_send()
            far_copy(layer, piece, half, "wf", sib).wait_send()
            far_copy(layer, piece, 1 - half, "wg", sib).wait_send()

        @pl.when(c == layer)
        def _():
            for piece in range(3):
                to_sib(layer, piece).wait_send()
                for core in range(2):
                    to_acr(layer, piece, core).wait_send()
            for n in range(7):
                wo_sends(layer, n).wait_send()

    sib_starts((0,))
    own_weights(4).wait()
    gain_copy.wait()

    def kv_copy(layer, i, j, n):
        rows = pl.ds(pl.multiple_of(c * count + i * quarter, 16), quarter)
        here = (r.k_v, r.v_v)[n].at[layer, j, rows]
        return remote(here, here, "kv", layer * 8 + i * 4 + j * 2 + n, sib)

    def mix_copy(layer, i, j):
        return remote(
            r.mixed_v.at[layer, j, rows_of(i)], r.mixr_v.at[j, rows_of(i)], "mix", i * 2 + j, par
        )

    def fill_bias(layer):
        high, wide, length = r.sizes[p, 0], r.sizes[p, 1], r.lengths[p]

        def windows(tokens):
            row = (tokens * 2731) >> 16
            col = tokens - row * GRID
            down, right = row + r.shifts[0] * layer, col + r.shifts[1] * layer
            return row, col, ((down * 5462) >> 16) * 8 + ((right * 5462) >> 16)

        cj = lax.broadcasted_iota(jnp.int32, (1, z.tokens), 1)
        row, col, window = windows(cj)
        is_patch = cj < PATCHES
        live_patch = is_patch & (row < high) & (col < wide)
        live_answer = jnp.logical_not(is_patch) & (cj - PATCHES < length)
        cw = jnp.where(live_patch, window, -1)
        ca = jnp.where(live_patch, -1, jnp.where(live_answer, cj, 1 << 20))
        ri = lax.broadcasted_iota(jnp.int32, (count, 1), 0) + c * count
        _, _, window = windows(ri)
        rw = jnp.where(ri < PATCHES, window, -2)
        ra = jnp.where(ri < PATCHES, -5, ri)
        allowed = (cw == rw) | (ca < ra) | (cj == ri)
        r.bias_v[...] = jnp.where(allowed, 0.0, OFF)

    def make_a(layer, rows):
        normed, _ = normalize(r.x_v[layer, rows, :].astype(F32))
        r.a_v[rows, :] = (normed * r.gain_v[layer, 0:1, :]).astype(BF)

    def project_qkv(layer, i, j):
        rows = rows_of(i)
        there = pl.ds(pl.multiple_of(c * count + i * quarter, 16), quarter)
        a = r.a_v[rows, :]
        r.k_v[layer, j, there, :] = mm_nt(a, r.wa_v[layer, 1, j]).astype(BF)
        kv_copy(layer, i, j, 0).start()
        r.v_v[layer, j, there, :] = mm_nt(a, r.wa_v[layer, 2, j]).astype(BF)
        kv_copy(layer, i, j, 1).start()
        r.q_v[layer, j, rows, :] = (mm_nt(a, r.wa_v[layer, 0, j]) * HD**-0.5).astype(BF)

    near_keys = PATCHES
    views = (
        lambda i: c == 0,
        lambda i: (c == 1) & (i == 0),
        lambda i: (c == 1) & (i == 1),
    )
    seen = (near_keys, 3 * quarter, z.tokens)

    def attend(layer, i, j, keys):
        rows = rows_of(i)
        lane = lax.broadcasted_iota(jnp.int32, (quarter, 128), 1)
        stats = r.lse_v[layer, rows, :]
        total = jnp.zeros((quarter, z.part), F32)
        some = pl.ds(0, keys)
        scores = []
        for h in range(3):
            lanes = head_lanes(quarter, h)
            qh = jnp.where(lanes, r.q_v[layer, j, rows, :], jnp.zeros((), BF))
            scores.append(mm_nt(qh, r.k_v[layer, j, some, :]) + r.bias_v[rows, some])
        for h in range(3):
            top = jnp.max(scores[h], axis=-1, keepdims=True)
            expos = jnp.exp(scores[h] - top)
            norm = jnp.sum(expos, axis=-1, keepdims=True)
            stats = jnp.where(lane == j * 3 + h, top + jnp.log(norm), stats)
            part = mm(expos.astype(BF), r.v_v[layer, j, some, :]) * (1.0 / norm)
            total = total + jnp.where(head_lanes(quarter, h), part, 0.0)
        r.lse_v[layer, rows, :] = stats
        r.mixed_v[layer, j, rows, :] = total.astype(BF)

    def attention(layer, between):
        @pl.loop(0, 2)
        def _(j):
            @pl.loop(0, 2)
            def _(i):
                between(j, i)

                @pl.when(i == 0)
                def _():
                    for e in range(2):
                        for n in range(2):
                            kv_copy(layer, e, j, n).wait()

                for when, keys in zip(views, seen):
                    pl.when(when(i))(functools.partial(attend, layer, i, j, keys))
                mix_copy(layer, i, j).start()

    def at(j, i, there, do):
        pl.when((j == there[0]) & (i == there[1]))(do)

    def project(layer, i):
        rows = rows_of(i)
        total = r.x_v[layer, rows, :].astype(F32)
        total = total + mm(r.mixed_v[layer, 0, rows, :], r.wo_v[layer, t])
        total = total + mm(r.mixed_v[layer, 1, rows, :], r.wo_v[layer, ax])
        for j in range(2):
            mix_copy(layer, i, j).wait()
        total = total + mm(r.mixr_v[0, rows, :], r.wo_v[layer, px])
        total = total + mm(r.mixr_v[1, rows, :], r.wo_v[layer, dx])
        r.x1_v[rows, :] = total
        normed, _ = normalize(total)
        r.b_v[rows, :] = (normed * r.gain_v[layer, 1:2, :]).astype(BF)

    def ar_copy(n, i):
        return remote(
            r.out_v.at[rows_of(i)], r.in_v.at[n % 2, rows_of(i)], "ar", (n % 2) * 2 + i, par
        )

    def summed(n, rows):
        return r.out_v[rows, :].astype(F32) + r.in_v[n % 2, rows, :].astype(F32)

    def hidden_of(layer, i, j):
        hidden = mm(r.b_v[rows_of(i), :], r.wf_v[layer, 0, j])
        cdf = 0.5 + 0.5 * lax.erf(hidden * 0.5**0.5)
        bell = jnp.exp(hidden * hidden * -0.5) * 0.3989422804014327
        return hidden * cdf, cdf + hidden * bell

    def units_of(j):
        return pl.ds(pl.multiple_of(j * width, width), width)

    def over_units(rows, ref, item, layer, product):
        return product(ref[rows, pl.ds(0, width)], r.wf_v[layer, item, 0]) + product(
            ref[rows, pl.ds(width, width)], r.wf_v[layer, item, 1]
        )

    def down(layer, rows):
        return over_units(rows, r.acted_v, 1, layer, mm).astype(BF)

    def up_back(layer, rows):
        return over_units(rows, r.slope_v, 0, layer, mm_nt).astype(BF)

    def dhidden_of(layer, i, j):
        return mm_nt(r.g_v[rows_of(i), :], r.wf_v[layer, 1, j])

    def activate(i, j):
        acted, slope = hidden_of(0, i, j)
        r.acted_v[rows_of(i), units_of(j)] = acted.astype(BF)
        r.slope_v[rows_of(i), units_of(j)] = slope.astype(BF)

    x_pass()
    owner_starts(0, (0,))
    sib_starts((1, 2))
    fill_bias(0)
    r.lse_v[...] = jnp.zeros_like(r.lse_v)
    x_wait()
    owner_starts(0, (1, 2))
    wo_start(0)
    need_own(0, 0)

    @pl.loop(0, 2)
    def _(i):
        make_a(0, rows_of(i))
        project_qkv(0, i, 0)

    step_y(0, 0)

    def between_0(j, i):
        @functools.partial(at, j, i, (0, 1))
        def _():
            step_z(0, 0)
            need_far(0, 0)
            project_qkv(0, 0, 1)
            project_qkv(0, 1, 1)

        @functools.partial(at, j, i, (1, 0))
        def _():
            step_y(0, 1)
            step_wo(0)

        @functools.partial(at, j, i, (1, 1))
        def _():
            step_z(0, 1)
            step_y(0, 2)

    attention(0, between_0)
    last_wo(0)
    step_z(0, 2)
    need_wo(0)
    need_own(0, 1)

    @pl.loop(0, 2)
    def _(i):
        project(0, i)
        activate(i, 0)

    for piece in (1, 2):
        need_far(0, piece)
    need_own(0, 2)
    owner_starts(1, (0,))

    @pl.loop(0, 2)
    def _(i):
        rows = rows_of(i)
        activate(i, 1)
        r.out_v[rows, :] = down(0, rows)
        ar_copy(0, i).start()

    kept = [
        (r.x1_v, r.h_x1),
        (r.b_v, r.h_b),
        (r.acted_v, r.h_acted),
        (r.slope_v, r.h_slope),
    ]
    for n, (here, there) in enumerate(kept):
        local(here, there, "lh", n).start()
    step_y(1, 0)
    c_start()
    owner_starts(1, (1, 2))
    fill_bias(1)
    step_z(1, 0)
    need_own(1, 0)
    need_far(1, 0)

    @pl.loop(0, 2)
    def _(i):
        rows = rows_of(i)
        ar_copy(0, i).wait()
        r.x_v[1, rows, :] = (r.x1_v[rows, :] + summed(0, rows)).astype(BF)
        make_a(1, rows)
        for j in range(2):
            project_qkv(1, i, j)

    c_pass()
    wo_start(1)

    def between_1(j, i):
        @functools.partial(at, j, i, (0, 0))
        def _():
            step_y(1, 1)

        @functools.partial(at, j, i, (0, 1))
        def _():
            step_z(1, 1)
            step_y(1, 2)
            step_wo(1)

        @functools.partial(at, j, i, (1, 0))
        def _():
            step_z(1, 2)

    attention(1, between_1)
    last_wo(1)
    need_wo(1)
    for piece in (1, 2):
        need_own(1, piece)
        need_far(1, piece)
    c_wait()
    for n, (here, there) in enumerate(kept):
        local(here, there, "lh", n).wait()

    @pl.loop(0, 2)
    def _(i):
        rows = rows_of(i)
        project(1, i)

        @pl.loop(0, 2)
        def _(j):
            acted, slope = hidden_of(1, i, j)
            r.acted_v[rows, units_of(j)] = acted.astype(BF)
            r.slope_v[rows, units_of(j)] = (dhidden_of(1, i, j) * slope).astype(BF)

        r.out_v[rows, :] = up_back(1, rows)
        ar_copy(1, i).start()

    own_rows, par_rows = rows_of(m), rows_of(1 - m)

    r.yout_v[...] = down(1, par_rows)
    y_copy = remote(r.yout_v, r.yin_v, "yy", 0, par)
    r.yown_v[...] = down(1, own_rows)

    def end_copies(src, section):
        stays = (c == section) & (p == section)

        def far():
            return remote(src, r.ends.at[p], "en", section * 2, (section, d, 2 * c + m), rn=p)

        return stays, far, lambda: local(src, r.ends.at[p], "le", section)

    def end_start(src, section):
        stays, far, near = end_copies(src, section)
        pl.when(stays)(lambda: near().start())
        pl.when(jnp.logical_not(stays))(lambda: far().start())

    def end_sent(src, section):
        stays, far, near = end_copies(src, section)
        pl.when(stays)(lambda: near().wait())
        pl.when(jnp.logical_not(stays))(lambda: far().wait_send())

    def end_arrived(src):
        for i in range(2):
            came = jnp.logical_not((c == p) & (i == c))

            @pl.when(came)
            def _():
                remote(src, r.ends.at[i], "en", i, par).wait_recv()

    def grad_f(layer, j):
        @pl.loop(0, width // TILE)
        def _(n):
            here = tile_of(n)
            cols = pl.ds(pl.multiple_of(n * TILE, TILE) + j * width, TILE)
            r.wf_v[layer, 0, j, :, here] = mm_tn(r.b_v[...], r.slope_v[:, cols]).astype(BF)
            r.wf_v[layer, 1, j, here, :] = mm_tn(r.acted_v[:, cols], r.g_v[...]).astype(BF)

    def held(which, layer, item):
        return r.wf_v.at[layer, item] if which == "f" else r.dwa_v.at[item]

    def crecv(which):
        return r.crecv_f if which == "f" else r.crecv_a

    def yrecv(which):
        return r.yrecv_f if which == "f" else r.yrecv_a

    def zsend(which):
        return r.zsend_f if which == "f" else r.zsend_a

    def zland(which):
        return r.zf_o if which == "f" else r.za_o

    def core_copy(which, layer, j):
        return remote(held(which, layer, 1 - c).at[j], crecv(which).at[j], "c" + which, j, sib)

    STEP = width // 4
    fourth = dp // 4
    place_z, offset = d // fourth, lax.rem(d, fourth)
    beside = (c, (place_z + 1 - 2 * lax.rem(place_z, 2)) * fourth + offset, t)

    def group_at(n):
        return (
            3 - place_z,
            lax.rem(place_z + 2, 4),
            place_z + 1 - 2 * lax.rem(place_z, 2),
            place_z,
        )[n]

    def y_copy_of(which, n):
        rows = tile_of(group_at(n), STEP)
        return remote(crecv(which).at[1, rows], yrecv(which).at[rows], "y" + which, n, acr)

    def credit(name, device):
        pl.semaphore_signal(getattr(r, name), inc=1, device_id=device, device_id_type=MESH)

    def spend(name):
        pl.semaphore_wait(getattr(r, name), 1)

    group = 1 if z.rows % 16 == 0 else 2

    def z_copy(layer, which, n, e):
        kind = 3 - n
        land = zland(which).at[c, kind * fourth + offset]
        return remote(
            zsend(which).at[e], land, "z" + which, e, (layer, e, t), rn=(c * 3 + kind) * fourth + offset
        )

    def swap(which):
        return r.zswap_f if which == "f" else r.zswap_a

    def swap_copy(which):
        shards = pl.ds(group_at(0) * fourth, fourth)
        return remote(zsend(which).at[shards], swap(which), "s" + which, 0, beside)

    def stage2(which, layer):
        core_copy(which, layer, 1).wait()
        if layer == 0:
            spend("free_y" + which)
        got = crecv(which)
        for n in range(4):
            rows = tile_of(group_at(n), STEP)
            got[1, rows, :] = (
                got[1, rows, :].astype(F32) + held(which, layer, c)[1, rows, :].astype(F32)
            ).astype(BF)
            y_copy_of(which, n).start()

    def z_each(n, do):
        @pl.loop(0, fourth)
        def _(f):
            do(group_at(n) * fourth + f)

    def z_wait_sends(layer, which):
        for n in range(1, 4):

            def sent(e):
                @pl.when((c != layer) | (e != d))
                def _():
                    z_copy(layer, which, n, e).wait_send()

            z_each(n, sent)

    def z_send(layer, which, n):
        def go(e):
            @pl.when((c != layer) | (e != d))
            def _():
                z_copy(layer, which, n, e).start()

            @pl.when((c == layer) & (e == d))
            def _():
                near = local(zsend(which).at[d], zland(which).at[c, offset], "lz", 0)
                near.start()
                near.wait()

        z_each(n, go)

    def z_arrived(which):
        for core in range(2):
            for kind in range(3):

                @pl.loop(0, fourth)
                def _(f):
                    @pl.when((core != c) | (kind != 0) | (f != offset))
                    def _():
                        remote(
                            zsend(which).at[0],
                            zland(which).at[core, kind * fourth + f],
                            "z" + which,
                            0,
                            par,
                            rn=(core * 3 + kind) * fourth + f,
                        ).wait_recv()

    def stage3(which, layer, n):
        if n == 0:
            core_copy(which, layer, 0).wait()
            if layer == 0:
                z_wait_sends(1, which)
        y_copy_of(which, n).wait()
        got, more, out, beside_too = crecv(which), yrecv(which), zsend(which), swap(which)
        if n == 1:
            swap_copy(which).wait()

        @pl.loop(0, fourth // group)
        def _(e):
            first = group_at(n) * fourth + e * group
            rows = pl.ds(pl.multiple_of(first * z.rows, group * z.rows), group * z.rows)
            total = (
                got[0, rows, :].astype(F32)
                + held(which, layer, c)[0, rows, :].astype(F32)
                + more[rows, :].astype(F32)
            ).reshape(group, z.rows, got.shape[-1])
            if n == 1:
                total = total + beside_too[pl.ds(e * group, group)].astype(F32)
            out[pl.ds(first, group)] = total.astype(BF)

        if layer == 1 and n == 3:
            credit("free_c" + which, sib)
            credit("free_y" + which, acr)
        if layer == 1 and n == 1:
            credit("free_s" + which, beside)
        if n == 0:
            if layer == 0:
                spend("free_s" + which)
            swap_copy(which).start()
        else:
            z_send(layer, which, n)

    r.gain_g[...] = jnp.zeros_like(r.gain_g)

    def gain_grad(layer, n, i, grad, normed):
        share = jnp.where(i == m, 1.0, 0.0)
        r.gain_g[layer, n : n + 1, :] += share * jnp.sum(grad * normed, axis=0, keepdims=True)

    def after_ffn(layer, n):
        @pl.loop(0, 2)
        def _(i):
            rows = rows_of(i)
            ar_copy(n, i).wait()
            grad = summed(n, rows)
            normed, inverse = normalize(r.x1_v[rows, :])
            gain_grad(layer, 1, i, grad, normed)
            back = normalize_back(grad, normed, inverse, r.gain_v[layer, 1:2, :])
            dx1 = r.g_v[rows, :].astype(F32) + back
            dc = dx1.astype(BF)
            r.x1_v[rows, :] = dx1
            r.dmix_v[0, rows, :] = mm_nt(dc, r.wo_v[layer, t]).astype(BF)
            r.dmix_v[1, rows, :] = mm_nt(dc, r.wo_v[layer, ax]).astype(BF)

    def pt_copy(n):
        return remote(r.dkv_v.at[n, :, away], r.other_v.at[n], "pt", n, sib)

    def attend_back(layer, j, keys):
        some = pl.ds(0, keys)
        zero = jnp.zeros((), BF)
        q, dmix = r.q_v[layer, j], r.dmix_v[j]
        q_t, dmix_t = q.T, dmix.T
        k, v = r.k_v[layer, j, some, :], r.v_v[layer, j, some, :]
        product = dmix.astype(F32) * r.mixed_v[layer, j].astype(F32)
        total = jnp.zeros((count, z.part), F32)
        for h in range(3):
            lanes = head_lanes(count, h)
            heads = pl.ds(h * HD, HD)
            scores = mm_nt(jnp.where(lanes, q, zero), k) + r.bias_v[:, some]
            dprobs = mm_nt(jnp.where(lanes, dmix, zero), v)
            probs = jnp.exp(scores - column_of(r.lse_v[layer], j * 3 + h))
            inner = jnp.sum(jnp.where(lanes, product, 0.0), axis=-1, keepdims=True)
            r.dkv_t[1, j, heads, some] = mm(dmix_t[h * HD : h * HD + HD], probs.astype(BF))
            dscores = (probs * (dprobs - inner)).astype(BF)
            total = total + jnp.where(lanes, mm(dscores, k), 0.0)
            r.dkv_t[0, j, heads, some] = mm(q_t[h * HD : h * HD + HD], dscores)
        r.q_v[layer, j] = (total * HD**-0.5).astype(BF)

    def attention_back(layer, between):
        @pl.loop(0, 2)
        def _(j):
            between(j)
            pl.when(c == 0)(functools.partial(attend_back, layer, j, near_keys))
            pl.when(c == 1)(functools.partial(attend_back, layer, j, z.tokens))

        for n in range(2):
            for j in range(2):
                r.dkv_v[n, j] = r.dkv_t[n, j].T.astype(BF)
        if layer == 0:
            spend("free_pt")
        for n in range(2):
            pt_copy(n).start()
        between(2)
        for n in range(2):
            pt_copy(n).wait()
            r.dkv_v[n, :, mine, :] = (
                r.dkv_v[n, :, mine, :].astype(F32) + r.other_v[n].astype(F32)
            ).astype(BF)
        if layer == 1:
            credit("free_pt", sib)

    def in_all(rows):
        return pl.ds(pl.multiple_of(c * count + rows.start, 16), quarter)

    def da_chunk(layer, rows):
        total = jnp.zeros((quarter, width), F32)
        for j in range(2):
            total = total + mm(r.q_v[layer, j, rows, :], r.wa_v[layer, 0, j])
            for e in range(2):
                total = total + mm(r.dkv_v[e, j, in_all(rows), :], r.wa_v[layer, 1 + e, j])
        r.out_v[rows, :] = total.astype(BF)

    def grad_a(layer):
        @pl.loop(0, 2)
        def _(n):
            j = 1 - n
            pair = jnp.concatenate([r.q_v[layer, j], r.dkv_v[0, j, mine, :]], axis=1)
            r.dwa_v[0, j] = mm_tn(r.a_v[...], pair).astype(BF)
            of_v = mm_tn(r.a_v[...], r.dkv_v[1, j, mine, :])
            of_out = mm_tn(r.x1_v[...].astype(BF), r.mixed_v[layer, j])
            r.dwa_v[1, j] = jnp.concatenate([of_v, of_out], axis=1).astype(BF)
            core_copy("a", layer, j).start()

    finish_weights(1)
    for j in (1, 0):
        grad_f(1, j)
        core_copy("f", 1, j).start()
    stage2("f", 1)
    r.yown_v[...] = (r.x1_v[own_rows, :] + r.yown_v[...].astype(F32)).astype(BF)
    r.dkv_t[...] = jnp.zeros_like(r.dkv_t)
    after_ffn(1, 1)
    y_copy.start()
    for n, (here, there) in enumerate(kept[1:]):
        local(there, here, "lh", n).start()

    def between_back_1(j):
        if isinstance(j, int):
            stage3("f", 1, 1)
            y_copy.wait()
            r.yown_v[...] = (r.yown_v[...].astype(F32) + r.yin_v[...].astype(F32)).astype(BF)
            end_start(r.yown_v, 1)
        else:
            pl.when(j == 1)(functools.partial(stage3, "f", 1, 0))

    attention_back(1, between_back_1)

    @pl.loop(0, 2)
    def _(i):
        da_chunk(1, rows_of(i))
        ar_copy(2, i).start()

    stage3("f", 1, 2)
    grad_a(1)
    stage3("f", 1, 3)
    stage2("a", 1)
    for n, (here, there) in enumerate(kept[1:]):
        local(there, here, "lh", n).wait()

    @pl.loop(0, 2)
    def _(i):
        rows = rows_of(i)
        ar_copy(2, i).wait()

        @pl.when(i == 1)
        def _():
            ar_copy(3, 0).start()

        grad = summed(2, rows)
        normed, inverse = normalize(r.x_v[1, rows, :].astype(F32))
        gain_grad(1, 0, i, grad, normed)
        back = normalize_back(grad, normed, inverse, r.gain_v[1, 0:1, :])
        r.g_v[rows, :] = (r.x1_v[rows, :] + back).astype(BF)

        @pl.loop(0, 2)
        def _(j):
            cols = units_of(j)
            du = dhidden_of(0, i, j)
            r.slope_v[rows, cols] = (du * r.slope_v[rows, cols].astype(F32)).astype(BF)

        r.out_v[rows, :] = up_back(0, rows)

        @pl.when(i == 1)
        def _():
            ar_copy(3, 1).start()

    local(r.h_x1, r.x1_v, "lh", 3).start()
    finish_weights(0)
    spend("free_cf")
    for j in (1, 0):
        grad_f(0, j)
        core_copy("f", 0, j).start()
    stage2("f", 0)
    for n in range(4):
        stage3("a", 1, n)
    fill_bias(0)
    r.dkv_t[...] = jnp.zeros_like(r.dkv_t)
    for i in range(2):
        make_a(0, rows_of(i))
    local(r.h_x1, r.x1_v, "lh", 3).wait()
    after_ffn(0, 3)

    def between_back_0(j):
        if isinstance(j, int):
            stage3("f", 0, 1)
        else:
            pl.when(j == 1)(functools.partial(stage3, "f", 0, 0))

    attention_back(0, between_back_0)
    da_chunk(0, par_rows)
    dx_copy = remote(r.out_v.at[par_rows], r.in_v.at[0, par_rows], "ar", 0, par)
    dx_copy.start()
    spend("free_ca")
    grad_a(0)
    da_chunk(0, own_rows)
    stage2("a", 0)
    stage3("f", 0, 2)
    stage3("f", 0, 3)
    stage3("a", 0, 0)
    dx_copy.wait()
    grad = summed(0, own_rows)
    normed, inverse = normalize(r.x_v[0, own_rows, :].astype(F32))
    gain_grad(0, 0, m, grad, normed)
    back = normalize_back(grad, normed, inverse, r.gain_v[0, 0:1, :])
    r.yin_v[...] = (r.x1_v[own_rows, :] + back).astype(BF)
    end_start(r.yin_v, 0)

    me = c * 4 + t

    def gain_group(e, f):
        return remote(r.gain_g, r.gain_i.at[me], "ga", e * 4 + f, (e, d, f), rn=me)

    def gain_over_z(e):
        return remote(r.gain_g, r.gain_z.at[d], "gz", e, (c, e, t), rn=d)

    def others(then):
        for e in range(2):
            for f in range(4):

                @pl.when((e != c) | (f != t))
                def _():
                    then(e, f)

    others(lambda e, f: gain_group(e, f).start())
    stage3("a", 0, 1)

    r.gain_i[me] = r.gain_g[...]
    others(lambda e, f: gain_group(e, f).wait_send())
    others(lambda e, f: remote(r.gain_g, r.gain_i.at[0], "ga", 0, par, rn=e * 4 + f).wait_recv())
    r.gain_g[...] = jnp.sum(r.gain_i[...], axis=0)

    def other_z(then):
        @pl.loop(0, dp)
        def _(e):
            @pl.when(e != d)
            def _():
                then(e)

    other_z(lambda e: gain_over_z(e).start())
    for n in range(2, 4):
        stage3("a", 0, n)
    r.gain_z[d] = r.gain_g[...]
    other_z(lambda e: gain_over_z(e).wait_send())
    other_z(lambda e: remote(r.gain_g, r.gain_z.at[0], "gz", 0, par, rn=e).wait_recv())
    r.dgain[...] = jnp.sum(r.gain_z[...], axis=0)
    z_wait_sends(0, "f")
    z_wait_sends(0, "a")
    z_arrived("f")
    z_arrived("a")
    end_sent(r.yown_v, 1)
    end_sent(r.yin_v, 0)
    end_arrived(r.yin_v)


def whole(z, *args):
    dma, regular = pltpu.SemaphoreType.DMA, pltpu.SemaphoreType.REGULAR
    shape = jax.ShapeDtypeStruct
    scratch = [VMEM(of(z), kind) for _, of, kind in BUFFERS]
    for _, of in PAIRS:
        scratch += [dma((of(z),)), dma((of(z),))]
    scratch += [dma((n,)) for _, n in LOCALS]
    scratch += [regular for _ in CREDITS]
    any_spec, vmem_spec = pl.BlockSpec(memory_space=ANY), pl.BlockSpec(memory_space=VMEM)
    return pl.pallas_call(
        functools.partial(kernel, z),
        out_shape=(
            shape((2, z.quarter, z.width), BF),
            shape((2, 3 * z.dp // 4, z.rows, z.width), BF),
            shape((2, 3 * z.dp // 4, z.rows, 2 * z.part), BF),
            shape((2, 2, z.width), F32),
            shape((z.count, z.width), F32),
            shape((z.count, z.width), BF),
            shape((z.count, 2 * z.width), BF),
            shape((z.count, 2 * z.width), BF),
        ),
        in_specs=[any_spec] * 6 + [vmem_spec] + [pl.BlockSpec(memory_space=pltpu.SMEM)] * 3,
        out_specs=[any_spec] * 3 + [vmem_spec] + [any_spec] * 4,
        scratch_shapes=scratch,
        compiler_params=pltpu.CompilerParams(
            collective_id=0, has_side_effects=True, vmem_limit_bytes=64 * 2**20
        ),
        cost_estimate=pl.CostEstimate(flops=10**11, bytes_accessed=10**8, transcendentals=0),
        name="two_layers",
    )(*args)


def on_device(inputs, cotangent, w_qkv, w_out, w_up, w_down, gains, image_sizes, lengths, shifts):
    core = lax.axis_index("section")
    t = lax.axis_index("tensor")
    z = Sizes()
    z.dp = lax.axis_size("dp")
    z.quarter, z.width = inputs.shape[1], inputs.shape[2]
    z.count, z.tokens = 2 * z.quarter, 4 * z.quarter
    z.part = w_qkv.shape[-1]
    z.rows = z.width // z.dp

    ends, zf, za, dgain = whole(
        z, inputs, cotangent, jnp.swapaxes(w_qkv[0], 1, 2), w_out[0], w_up[0], w_down[0], gains[0], image_sizes, lengths, shifts
    )[:4]
    f_sum = jnp.sum(zf.astype(F32), axis=1)
    a_sum = jnp.sum(za.astype(F32), axis=1)
    mine = lax.dynamic_index_in_dim(dgain, core, 0, keepdims=True)
    share = z.width // (z.dp * 4)
    slot = lax.axis_index("dp") * 4 + t
    gain_share = lax.dynamic_slice_in_dim(mine, slot * share, share, 2)
    return (
        ends[None],
        jnp.stack([a_sum[0, :, : z.part], a_sum[0, :, z.part :], a_sum[1, :, : z.part]])[None],
        a_sum[1, :, z.part :].T[None],
        f_sum[None, 0],
        f_sum[None, 1],
        gain_share,
    )


def solution(mesh):
    placed = (
        P("dp", "tensor", None),
        P("dp", "tensor", None),
        P("section", None, None, "tensor"),
        P("section", "tensor", None),
        P("section", None, "tensor"),
        P("section", "tensor", None),
        P("section", None, None),
        P("dp", None),
        P("dp"),
        P(),
    )
    return jax.shard_map(
        on_device,
        mesh=mesh,
        in_specs=placed,
        out_specs=(
            P("section", "dp", "tensor", None),
            P("section", None, "dp", "tensor"),
            P("section", "tensor", "dp"),
            P("section", "dp", "tensor"),
            P("section", ("tensor", "dp"), None),
            P("section", None, ("dp", "tensor")),
        ),
        check_vma=False,
    )
```
